32 devices in a mesh: acq: 2 (over y), tile: 16 (over z, x, core).
Axes of the slice: x: 2, y: 2, z: 4, core: 2. Of those that a mesh axis runs over, the one named last changes fastest.
Arguments:
- unprocessed_echo_data: float32 [2, 2, 768, 12288], P(None, 'acq', 'tile'), may hold values from -6 to 6
- slant_kernel_frequencies: float32 [2, 2, 12288], P(None, 'acq'), may hold values from -6 to 6
- along_track_kernel_angle: float32 [2, 768, 12288], P('acq', None, 'tile'), may hold values from -3.140625 to 3.140625
- pairs: int32 [2, 2], replicated, may hold values from 0 to 1, as said below
Outputs:
- interferogram: float32 [2, 2, 2, 128, 1536], P(None, None, 'acq', 'tile')
The draws below stay inside these ranges and needn't reach their ends.
Inputs may be any that keep to these rules, and one draw needn't show every extreme that they name: `pairs`: in each of the 2 rounds the partners of the 2 acquisitions are a permutation of them; an acquisition may be its own partner.
All inputs are finite; a program needn't handle non-finite values.
Results may differ from the reference program's by a relative error of at most 0.000098.
Values sent between devices are 32-bit elements; how exact they have to be, the bound alone decides.
No kernel may reach another device: no remote copies, remote signals or barrier semaphores. Data moves between devices by JAX's collectives and lax.ppermute only.
A program may use at most 192 MiB of HBM per device.

```python
import jax
import jax.numpy as jnp
from jax import lax

NA = 768
NR = 12288
ROUNDS = 2
LOOK_AZ = 2
LOOK_RG = 8
AOI = 256
ACQ = 2
AOI_START = 256


def draw_pairs(key, part):
    round_rows = []
    for round_id in range(ROUNDS):
        partner_row = jax.random.permutation(jax.random.fold_in(key, 11 + round_id), ACQ).astype(jnp.int32)
        round_rows.append(partner_row)
    return jnp.stack(round_rows)


def steps_of(own_key, extent, shards, smallest, largest):
    gain, own = 1.0, jax.random.fold_in(own_key, 6)
    for dim, parts in shards:
        draws = jnp.exp(jax.random.uniform(jax.random.fold_in(own, dim), (parts,), jnp.float32, smallest / len(shards), largest / len(shards)))
        gain = gain * jnp.repeat(draws, extent[dim] // parts).reshape([-1 if axis == dim else 1 for axis in range(len(extent))])
    return gain


def gaussian(rng, shape, deviation, reach, shards=(), kind=jnp.bfloat16):
    level = steps_of(rng, shape, shards, -0.22, 0.18) if shards else 1.0
    drawn = jax.random.normal(rng, shape, jnp.float32) * deviation * level
    return jnp.minimum(jnp.maximum(drawn, -reach), reach).astype(kind)


def setup_inputs(seed: int = 0) -> dict:
    streams_of = jax.random.split(jax.random.key(seed), 5)
    return {
        "unprocessed_echo_data": gaussian(streams_of[0], (2, ACQ, NA, NR), 1.0, 6.0, ((1, 2), (2, 16)), jnp.float32),
        "slant_kernel_frequencies": gaussian(streams_of[1], (2, ACQ, NR), 0.7071, 6.0, ((1, 2),), jnp.float32),
        "along_track_kernel_angle": jnp.clip(jax.random.uniform(streams_of[2], (ACQ, NA, NR), jnp.float32, -3.140625, 3.140625), -3.140625, 3.140625),
        "pairs": draw_pairs(jax.random.fold_in(streams_of[4], 71), 0),
    }


def sharpen_one_scene(scene_collection):
    echo_inphase, echo_quadrature, kernel_inphase, kernel_quadrature, angle_term = scene_collection
    signal = lax.complex(echo_inphase, echo_quadrature)
    spectrum = jnp.fft.fft(signal, axis=1) * lax.complex(kernel_inphase, kernel_quadrature)[None, :]
    range_lines = jnp.fft.ifft(spectrum, axis=1)
    doppler = jnp.fft.fft(range_lines, axis=0) * lax.complex(jnp.cos(angle_term), jnp.sin(angle_term))
    sharpened_scene = jnp.fft.ifft(doppler, axis=0)[AOI_START:AOI_START + AOI]
    return jnp.stack([jnp.real(sharpened_scene), jnp.imag(sharpened_scene)])


def multilook(field):
    shaped = field.reshape(ROUNDS, ACQ, AOI // LOOK_AZ, LOOK_AZ, NR // LOOK_RG, LOOK_RG)
    return jnp.sum(shaped, axis=(3, 5)) / (LOOK_AZ * LOOK_RG)


def reference(unprocessed_echo_data, slant_kernel_frequencies, along_track_kernel_angle, pairs):
    sharpened_scene = lax.map(sharpen_one_scene, (unprocessed_echo_data[0], unprocessed_echo_data[1], slant_kernel_frequencies[0], slant_kernel_frequencies[1], along_track_kernel_angle))
    others = sharpened_scene[pairs]
    mine = sharpened_scene[None]
    cross_real = mine[:, :, 0] * others[:, :, 0] + mine[:, :, 1] * others[:, :, 1]
    cross_imag = mine[:, :, 1] * others[:, :, 0] - mine[:, :, 0] * others[:, :, 1]
    return jnp.stack([multilook(cross_real), multilook(cross_imag)])
```

```python
import functools
import math

import jax
import jax.numpy as jnp
import ml_dtypes
import numpy as np
from jax import lax
from jax.experimental import pallas as pl
from jax.experimental.pallas import tpu as pltpu
from jax.sharding import PartitionSpec as P

LOOK_AZ = 2
LOOK_RG = 8
AOI = 256
LANES = 128
SUB = 8
FAR = 4
BATCH = 4
VMEM_LIMIT = 56 * 1024 * 1024


def high_low(table):
    high = table.astype(ml_dtypes.bfloat16)
    low = (table - high.astype(np.float64)).astype(ml_dtypes.bfloat16)
    return np.stack([high, low])


def trig(product, period):
    angle = (product % period) * (2.0 * math.pi / period)
    return np.cos(angle), np.sin(angle)


def split(value):
    high = value.astype(jnp.bfloat16)
    return high, (value - high.astype(jnp.float32)).astype(jnp.bfloat16)


def dot(left, right):
    return jnp.dot(left, right, preferred_element_type=jnp.float32)


def dot_stacked(table, value):
    high, low = split(value)
    both = dot(table, jnp.concatenate([high, low], axis=0))
    rows = table.shape[0] // 2
    return both[:rows] + both[rows:]


def thirds(a, b, c, sign):
    scale = sign * math.sqrt(3.0) / 2.0
    tr, ti = b[0] + c[0], b[1] + c[1]
    vr, vi = (b[0] - c[0]) * scale, (b[1] - c[1]) * scale
    ur, ui = a[0] - 0.5 * tr, a[1] - 0.5 * ti
    return (a[0] + tr, a[1] + ti), (ur - vi, ui + vr), (ur + vi, ui - vr)


def dot_table_right(value, table):
    high, low = split(value)
    return dot(jnp.concatenate([high, low, high], axis=1), table)


def stacked(table):
    high, low = high_low(table)
    return np.block([[high, high], [low, np.zeros_like(low)]])


def range_tables(length, order, halves):
    inner = LANES
    outer = length // inner
    part = outer // 3
    k1 = np.arange(outer)
    q = np.arange(inner)
    inside = np.arange(part)
    per_tile = outer // len(order)
    blocks = per_tile // halves
    a1, a4 = [], []
    for p0 in range(3):
        c, s = trig(np.outer(inside, 3 * inside + p0), outer)
        a1.append(stacked(np.block([[c, s], [-s, c]])))
        c, s = trig(np.outer(3 * inside + p0, inside), outer)
        rows = [
            cc * part + (t * per_tile + half * blocks) // 3 + b
            for half in range(halves)
            for t in order
            for cc in range(2)
            for b in range(blocks // 3)
        ]
        a4.append(stacked(np.block([[c, -s], [s, c]])[np.array(rows)] / length))
    c2, s2 = trig(np.outer(q, q), inner)
    b2 = np.block([[c2, -s2], [s2, c2]])
    b3 = np.block([[c2, s2], [-s2, c2]])
    ct, st = trig(np.outer(k1, q), length)
    twiddle = np.stack([ct, st]).astype(np.float32)
    b2, b3 = [np.concatenate(high_low(t)[[0, 0, 1]]) for t in (b2, b3)]
    return np.stack(a1), b2, b3, np.stack(a4), twiddle


def spot(tile, low):
    return lax.rem(tile, low) * FAR + lax.div(tile, low)


def range_kernel(outer, early, me_ref, x_ref, slant_ref, a1_ref, b2_ref, b3_ref, a4_ref, t_ref, *rest):
    outs, (rows_ref, h_ref), held = rest[: 1 + early], rest[1 + early : 3 + early], rest[3 + early :]
    part = outer // 3

    @pl.when(pl.program_id(0) == 0)
    def _():
        for c in range(2):
            for k2 in range(LANES):
                rows_ref[c, k2 : k2 + 1, :outer] = slant_ref[c, :, k2 * outer : (k2 + 1) * outer]
            h_ref[c] = rows_ref[c].T[:outer]

    rows = outs[0].shape[2]
    turned = held[0] if early else outs[0].reshape(outs[0].shape[0] * rows, LANES)
    ct, st = t_ref[0], t_ref[1]
    hr, hi = h_ref[0], h_ref[1]

    def batch(first):
        lines = range(first, first + BATCH)
        y = []
        for p0 in range(3):
            x = [
                jnp.concatenate(
                    [x_ref[c, 0, pl.ds(p0 * SUB + l, part, stride=3 * SUB), :] for c in range(2)], axis=0
                )
                for l in lines
            ]
            value = dot_stacked(a1_ref[p0], jnp.concatenate(x, axis=1))
            y.append((value[:part], value[part:]))
        yield
        y = thirds(*y, -1.0)
        z = []
        for b in range(BATCH):
            yr, yi = [
                jnp.concatenate([v[c][:, b * LANES : (b + 1) * LANES] for v in y], axis=0) for c in range(2)
            ]
            z.append(jnp.concatenate([yr * ct + yi * st, yi * ct - yr * st], axis=1))
        y = dot_table_right(jnp.concatenate(z, axis=0), b2_ref[...])
        yield
        z = []
        for b in range(BATCH):
            yr = y[b * outer : (b + 1) * outer, :LANES]
            yi = y[b * outer : (b + 1) * outer, LANES:]
            z.append(jnp.concatenate([yr * hr - yi * hi, yr * hi + yi * hr], axis=1))
        y = dot_table_right(jnp.concatenate(z, axis=0), b3_ref[...])
        yield
        z = []
        for b in range(BATCH):
            yr = y[b * outer : (b + 1) * outer, :LANES]
            yi = y[b * outer : (b + 1) * outer, LANES:]
            zr, zi = yr * ct - yi * st, yi * ct + yr * st
            z.append(thirds(*[(zr[k * part : (k + 1) * part], zi[k * part : (k + 1) * part]) for k in range(3)], 1.0))
        y = []
        for p0 in range(3):
            value = jnp.concatenate([jnp.concatenate(z[b][p0], axis=0) for b in range(BATCH)], axis=1)
            y.append(dot_stacked(a4_ref[p0], value))
        yield
        for p0 in range(3):
            for b, l in enumerate(lines):
                turned[pl.ds(p0 * SUB + l, 2 * part, stride=3 * SUB), :] = y[p0][
                    :, b * LANES : (b + 1) * LANES
                ]
        yield

    batches = [batch(first) for first in range(0, SUB, BATCH)]
    for _ in range(5):
        for work in batches:
            next(work)
    if not early:
        return
    near = outs[0].shape[0] // 2
    for k, out in enumerate(outs):
        for s in range(2 * near):
            tile = jnp.bitwise_xor(me_ref[1], s % near + k * near)
            dest = jnp.bitwise_xor(me_ref[0], s // near) * 2 * near + spot(tile, 2 * near // FAR)
            out[s, 0] = turned[pl.ds(pl.multiple_of(dest * rows, SUB), rows), :]


def range_call(echo, slant, me, first, steps, order, halves, early=False):
    length = echo.shape[3]
    outer = length // LANES
    view = echo.reshape(2, -1, SUB, outer, LANES).transpose(0, 1, 3, 2, 4).reshape(2, -1, outer * SUB, LANES)
    tables = [slant, *range_tables(length, order, halves)]
    dests = len(order) * halves
    rows = 2 * outer // dests * SUB
    whole = lambda shape: pl.BlockSpec(shape, lambda s, me: (0,) * len(shape))
    macs = steps * SUB * length * 2 * (2 * outer + 2 * LANES) * 2 * 3
    outs = 1 + early
    return pl.pallas_call(
        functools.partial(range_kernel, outer, early),
        grid_spec=pltpu.PrefetchScalarGridSpec(
            num_scalar_prefetch=1,
            grid=(steps,),
            in_specs=[pl.BlockSpec((2, 1, outer * SUB, LANES), lambda s, me: (0, first + s, 0, 0))]
            + [whole(t.shape) for t in tables],
            out_specs=[pl.BlockSpec((dests // outs, 1, rows, LANES), lambda s, me: (0, s, 0, 0))] * outs,
            scratch_shapes=[
                pltpu.VMEM((2, LANES, LANES), jnp.float32),
                pltpu.VMEM((2, outer, LANES), jnp.float32),
            ]
            + [pltpu.VMEM((dests * rows, LANES), jnp.float32)] * early,
        ),
        out_shape=[jax.ShapeDtypeStruct((dests // outs, steps, rows, LANES), jnp.float32)] * outs,
        compiler_params=pltpu.CompilerParams(vmem_limit_bytes=VMEM_LIMIT),
        cost_estimate=pl.CostEstimate(
            flops=2 * macs, bytes_accessed=16 * steps * SUB * length, transcendentals=0
        ),
        name=f"range_compress_{first}",
    )(me, view, *[jnp.asarray(t) for t in tables])


def pair_kernel(kept_ref, came_ref, *outs):
    for s, out in enumerate(outs):
        out[0] = kept_ref[s, 0]
        out[1] = came_ref[s, 0]


def pair_call(kept, came):
    count, _, rows, _ = kept.shape
    vmem = pl.BlockSpec(memory_space=pltpu.VMEM)
    return pl.pallas_call(
        pair_kernel,
        in_specs=[vmem] * 2,
        out_specs=[vmem] * count,
        out_shape=[jax.ShapeDtypeStruct((2, rows, LANES), jnp.float32)] * count,
        compiler_params=pltpu.CompilerParams(vmem_limit_bytes=VMEM_LIMIT),
        cost_estimate=pl.CostEstimate(flops=10**12, bytes_accessed=4 * kept.size, transcendentals=0),
        name="pair_halves",
    )(kept, came)


def azimuth_tables(length):
    part = length // 6
    f1 = np.arange(part)
    forward, backward = [], []
    first = (length - AOI) // 2
    u, s = np.arange(part // LOOK_AZ), np.arange(LOOK_AZ)
    lines = (first + u[None, :] * LOOK_AZ + s[:, None]).reshape(-1)
    for f0 in range(6):
        c, s = trig(np.outer(6 * f1 + f0, np.arange(part)), length)
        forward.append(np.block([[c, s], [-s, c]]))
        c, s = trig(np.outer(lines, 6 * f1 + f0), length)
        backward.append(np.block([[c, -s], [s, c]]) / length)
    return [np.concatenate(high_low(np.stack(t)), axis=1) for t in (forward, backward)]


def cos_sin(angle):
    y = 0.5 * angle
    z = y * y
    sine = [1.0, -1 / 6, 1 / 120, -1 / 5040, 1 / 362880, -1 / 39916800]
    cosine = [1.0, -1 / 2, 1 / 24, -1 / 720, 1 / 40320, -1 / 3628800, 1 / 479001600]
    s, c = sine[-1], cosine[-1]
    for k in sine[-2::-1]:
        s = s * z + k
    for k in cosine[-2::-1]:
        c = c * z + k
    s = s * y
    return 1.0 - 2.0 * (s * s), 2.0 * (s * c)


def three_pass(table, value):
    high, low = split(value)
    both = dot(table, high)
    rows = table.shape[0] // 2
    return (both[:rows] + both[rows:]) + dot(table[:rows], low)


def focus(xr, xi, cos_sin_of, tables):
    fw, bw = tables
    part, width = xr.shape[0] // 6, xr.shape[1]
    x = [(xr[k * part : (k + 1) * part], xi[k * part : (k + 1) * part]) for k in range(6)]
    classes = [None] * 6
    sums = thirds(*[(x[k][0] + x[k + 3][0], x[k][1] + x[k + 3][1]) for k in range(3)], -1.0)
    signs = [(x[k][0] - x[k + 3][0], x[k][1] - x[k + 3][1]) for k in range(3)]
    signs[1] = (x[4][0] - x[1][0], x[4][1] - x[1][1])
    diffs = thirds(*signs, -1.0)
    for e in range(3):
        classes[2 * e] = sums[e]
        classes[(2 * e + 3) % 6] = diffs[e]
    z, forward = [], []
    for f0 in range(7):
        if f0 < 6:
            forward.append(three_pass(fw[f0], jnp.concatenate(classes[f0], axis=0)))
        if f0 > 0:
            y, k = forward[f0 - 1], f0 - 1
            dr, di = y[:part], y[part:]
            pc, ps = cos_sin_of(k)
            e = jnp.concatenate([dr * pc - di * ps, dr * ps + di * pc], axis=0)
            z.append(three_pass(bw[k], e))
    half = math.sqrt(3.0) / 2.0
    first = (z[0] + z[3]) + (z[1] + z[4]) + (z[2] + z[5])
    a, b, c = z[0] - z[3], z[1] - z[4], z[2] - z[5]
    real = a + 0.5 * (b - c)
    turned = (b + c) * half
    fr = jnp.concatenate([first[:part], real[:part] - turned[part:]], axis=0)
    fi = jnp.concatenate([first[part:], real[part:] + turned[:part]], axis=0)
    return fr, fi


def lines_of(refs, first, order, part):
    tiles = len(order)
    at = [x[pl.ds(first, tiles), :, part, 0] for x in refs]
    value = at[0] if len(at) == 1 else jnp.concatenate(at, axis=1)
    if order != list(range(tiles)):
        value = jnp.stack([value[order.index(t)] for t in range(tiles)])
    return value.reshape(-1, LANES)


def looked_at(field, look):
    half = AOI // 2
    quarter = half // LOOK_AZ
    added = [field[h * half : h * half + quarter] + field[h * half + quarter : (h + 1) * half] for h in range(2)]
    high, low = split(jnp.concatenate(added, axis=0))
    return dot(high, look) + dot(low, look)


def trig_kernel(_, own_ref, other_ref, out):
    part = own_ref.shape[0] // 6
    for k in range(6):
        angle = jnp.concatenate([a[pl.ds(k, part, stride=6), :] for a in (own_ref, other_ref)], axis=1)
        out[0, 0, k], out[0, 1, k] = cos_sin(angle)


def trig_call(acq, angle, other_angle):
    lines, width = other_angle.shape
    blocks = width // LANES
    shape = (2, 6, lines // 6, 2 * LANES)
    return pl.pallas_call(
        trig_kernel,
        grid_spec=pltpu.PrefetchScalarGridSpec(
            num_scalar_prefetch=1,
            grid=(blocks,),
            in_specs=[
                pl.BlockSpec((lines, LANES), lambda b, acq: (0, acq[0] * blocks + b)),
                pl.BlockSpec((lines, LANES), lambda b, acq: (0, b)),
            ],
            out_specs=pl.BlockSpec((1,) + shape, lambda b, acq: (b, 0, 0, 0, 0)),
        ),
        out_shape=jax.ShapeDtypeStruct((blocks,) + shape, jnp.float32),
        compiler_params=pltpu.CompilerParams(vmem_limit_bytes=VMEM_LIMIT),
        cost_estimate=pl.CostEstimate(
            flops=64 * lines * width, bytes_accessed=24 * lines * width, transcendentals=0
        ),
        name="angle_phases",
    )(acq, angle, other_angle)


def joint_kernel(order, rounds, me_ref, same_ref, x_ref, early_ref, trig_ref, fw, bw, look_ref, out, stage):
    acq = me_ref[0]
    tiles = len(order)
    near = tiles // 2
    firsts = [acq * tiles, (1 - acq) * tiles]
    for part in range(2):
        for k, first in enumerate(firsts):
            lanes = slice(k * LANES, (k + 1) * LANES)
            for place, t in enumerate(order):
                stage[part, t, 1:, :, lanes] = x_ref[first + place, :, part, 0]
            for s in range(near):
                for side in range(2):
                    tile = jnp.bitwise_xor(me_ref[1], s + side * near)
                    stage[part, tile, 0, :, lanes] = early_ref[k * near + s, side, part, 0]
    xr, xi = [stage[part].reshape(-1, 2 * LANES) for part in range(2)]
    fr, fi = focus(xr, xi, lambda k: (trig_ref[0, 0, k], trig_ref[0, 1, k]), [fw, bw])
    mr, mi, pr, pi = fr[:, :LANES], fi[:, :LANES], fr[:, LANES:], fi[:, LANES:]
    look = look_ref[0]
    cross_real = looked_at(mr * pr + mi * pi, look[0])
    cross_imag = looked_at(mi * pr - mr * pi, look[1])
    own_real = looked_at(mr * mr + mi * mi, look[0])
    own_imag = looked_at(mi * mr - mr * mi, look[1])
    other_real = looked_at(pr * pr + pi * pi, look[0])
    other_imag = looked_at(pi * pr - pr * pi, look[1])
    per = AOI // LOOK_AZ // tiles

    @pl.when(pl.program_id(0) == 0)
    def _():
        out[...] = jnp.zeros_like(out)

    for r in range(rounds):
        same = same_ref[r] != 0
        own = jnp.where(same, own_real + own_imag, cross_real + cross_imag)
        other = jnp.where(same, other_real + other_imag, cross_real - cross_imag)
        for first, value in zip(firsts, (own, other)):
            for place, t in enumerate(order):
                out[first + place, r * per : (r + 1) * per, :] += value[t * per : (t + 1) * per]


def joint_call(me, same, array, early, trig, tables, order):
    dests, steps, _, blocks = array.shape[:4]
    tiles = len(order)
    lines = 6 * trig.shape[3]
    rounds = same.shape[0]
    rows = rounds * (AOI // LOOK_AZ // tiles)
    wide = blocks * LANES // LOOK_RG
    look = np.stack(
        [
            np.stack([look_table(LANES, c * wide + b * LANES // LOOK_RG) for c in range(2)])
            for b in range(blocks)
        ]
    )
    block = lambda a: pl.BlockSpec(a.shape[:3] + (1, SUB, LANES), lambda b, me, same: (0, 0, 0, b, 0, 0))
    return pl.pallas_call(
        functools.partial(joint_kernel, order, rounds),
        grid_spec=pltpu.PrefetchScalarGridSpec(
            num_scalar_prefetch=2,
            grid=(blocks,),
            in_specs=[
                block(array),
                block(early),
                pl.BlockSpec((1,) + trig.shape[1:], lambda b, me, same: (b, 0, 0, 0, 0)),
                *[pl.BlockSpec(t.shape, lambda b, me, same: (0, 0, 0)) for t in tables],
                pl.BlockSpec((1,) + look.shape[1:], lambda b, me, same: (b, 0, 0, 0)),
            ],
            out_specs=pl.BlockSpec((dests, rows, LANES), lambda b, me, same: (0, 0, 0)),
            scratch_shapes=[pltpu.VMEM((2, tiles, steps + 1, SUB, 2 * LANES), jnp.float32)],
        ),
        out_shape=jax.ShapeDtypeStruct((dests, rows, LANES), jnp.float32),
        compiler_params=pltpu.CompilerParams(vmem_limit_bytes=VMEM_LIMIT),
        cost_estimate=pl.CostEstimate(
            flops=2 * 2 * 3 * 6 * 256 * 256 * 2 * LANES * blocks,
            bytes_accessed=20 * lines * 2 * LANES * blocks,
            transcendentals=0,
        ),
        name="azimuth_interferogram",
    )(me, same, array, early, trig, *[jnp.asarray(t) for t in tables], jnp.asarray(look))


def single_kernel(tiles, x_ref, angle_ref, fw, bw, out):
    xr, xi = [lines_of([x_ref], 0, list(range(tiles)), part) for part in range(2)]
    fr, fi = focus(xr, xi, lambda k: cos_sin(angle_ref[pl.ds(k, AOI // 2, stride=6), :]), [fw, bw])
    out[:AOI] = fr
    out[AOI:] = fi


def single_call(array, angle, tables):
    tiles = array.shape[0]
    lines, columns = angle.shape
    return pl.pallas_call(
        functools.partial(single_kernel, tiles),
        grid=(columns // LANES,),
        in_specs=[
            pl.BlockSpec((tiles, array.shape[1], 2, 1, SUB, LANES), lambda b: (0, 0, 0, b, 0, 0)),
            pl.BlockSpec((lines, LANES), lambda b: (0, b)),
        ]
        + [pl.BlockSpec(t.shape, lambda b: (0, 0, 0)) for t in tables],
        out_specs=pl.BlockSpec((2 * AOI, LANES), lambda b: (0, b)),
        out_shape=jax.ShapeDtypeStruct((2 * AOI, columns), jnp.float32),
        compiler_params=pltpu.CompilerParams(vmem_limit_bytes=VMEM_LIMIT),
        name="azimuth_focus",
    )(array, angle, *[jnp.asarray(t) for t in tables])


def look_table(width, offset):
    table = np.zeros((width, LANES), np.float64)
    table[np.arange(width), offset + np.arange(width) // LOOK_RG] = 1.0 / (LOOK_AZ * LOOK_RG)
    return table.astype(ml_dtypes.bfloat16)


def cross_kernel(rounds, tiles, mine_ref, *refs):
    partner_refs, look_ref, out = refs[:rounds], refs[-2], refs[-1]
    mr, mi = mine_ref[:AOI], mine_ref[AOI:]
    per = AOI // LOOK_AZ // tiles
    for r in range(rounds):
        pr, pi = partner_refs[r][:AOI], partner_refs[r][AOI:]
        for c, field in enumerate((mr * pr + mi * pi, mi * pr - mr * pi)):
            looked = looked_at(field, look_ref[...])
            at = (c * rounds + r) * per
            for t in range(tiles):
                out[t, at : at + per, :] = looked[t * per : (t + 1) * per]


def cross_call(mine, partners, tiles):
    rounds = len(partners)
    width = mine.shape[1]
    look = jnp.asarray(look_table(width, 0))
    shape = (tiles, 2 * rounds * (AOI // LOOK_AZ // tiles), LANES)
    vmem = lambda: pl.BlockSpec(memory_space=pltpu.VMEM)
    return pl.pallas_call(
        functools.partial(cross_kernel, rounds, tiles),
        in_specs=[vmem() for _ in range(rounds + 2)],
        out_specs=vmem(),
        out_shape=jax.ShapeDtypeStruct(shape, jnp.float32),
        compiler_params=pltpu.CompilerParams(vmem_limit_bytes=VMEM_LIMIT),
        name="interferogram",
    )(mine, *partners, look)


def place_kernel(sources, valid, parts, in_ref, out):
    rows = in_ref.shape[1]
    lane = lax.broadcasted_iota(jnp.int32, (rows, LANES), 1)
    for c in range(parts):
        for o in range(len(sources) * valid // LANES):
            acc = None
            for place, source in enumerate(sources):
                shift = place * valid - o * LANES
                if shift + valid <= 0 or shift >= LANES:
                    continue
                value = in_ref[source]
                turn_by = (shift - c * valid) % LANES
                if turn_by:
                    value = pltpu.roll(value, turn_by, 1)
                acc = value if acc is None else jnp.where(lane >= shift, value, acc)
            out[c * rows : (c + 1) * rows, o * LANES : (o + 1) * LANES] = acc


def place_call(received, sources, valid, parts):
    _, rows, _ = received.shape
    return pl.pallas_call(
        functools.partial(place_kernel, sources, valid, parts),
        in_specs=[pl.BlockSpec(memory_space=pltpu.VMEM)],
        out_specs=pl.BlockSpec(memory_space=pltpu.VMEM),
        out_shape=jax.ShapeDtypeStruct((parts * rows, len(sources) * valid), jnp.float32),
        compiler_params=pltpu.CompilerParams(vmem_limit_bytes=VMEM_LIMIT),
        name="place_samples",
    )(received)


def turn(array, axes):
    return lax.all_to_all(array, axes, split_axis=0, concat_axis=0, tiled=True)


def by_block(array):
    dests, steps, rows, _ = array.shape
    return array.reshape(dests, steps, 2, rows // (2 * SUB), SUB, LANES)


def joint(tiles, echo, slant, angle, pairs):
    steps = echo.shape[2] // SUB
    columns = angle.shape[1]
    rounds = pairs.shape[0]
    acq = lax.axis_index("acq")
    side = acq.astype(jnp.int32).reshape(1)
    same = (lax.dynamic_index_in_dim(pairs, acq, 1, keepdims=False) == acq).astype(jnp.int32)
    theirs = lax.dynamic_slice_in_dim(angle, (1 - acq) * (columns // 2), columns // 2, 1)
    other_angle = lax.ppermute(theirs, "acq", [(0, 1), (1, 0)])
    low = lax.axis_size("low")
    order = [h * low + k for k in range(low) for h in range(tiles // low)]
    axes = ("acq", "low", "high")
    tile = lax.axis_index("high") * low + lax.axis_index("low")
    me = jnp.stack([acq, tile]).astype(jnp.int32)
    kept, given = range_call(echo, slant, me, 0, 1, order, 2, early=True)
    came = lax.ppermute(given, "high", [(h, h ^ (FAR // 2)) for h in range(FAR)])
    (sent,) = range_call(echo, slant, me, 1, steps - 1, order, 2)
    array = by_block(turn(sent, axes))
    early = list(pair_call(kept, came))
    near = tiles // 2
    for s in range(1, tiles):
        flip = s // near * tiles + s % near
        early[s] = lax.ppermute(early[s], ("acq", "high", "low"), [(i, i ^ flip) for i in range(2 * tiles)])
    early = by_block(jnp.stack(early))
    trig = trig_call(side, angle, other_angle)
    looked = joint_call(me, same, array, early, trig, azimuth_tables(angle.shape[0]), order)
    sources = [half * tiles + order.index(t) for t in range(tiles) for half in range(2)]
    result = place_call(turn(looked, axes), sources, columns // 2 // LOOK_RG, 2)
    return result.reshape(2, rounds, 1, -1, result.shape[1])


def separate(tiles, echo, slant, angle, pairs):
    columns = angle.shape[1]
    rounds = pairs.shape[0]
    (sent,) = range_call(echo, slant, jnp.zeros((2,), jnp.int32), 0, echo.shape[2] // SUB, list(range(tiles)), 1)
    mine = single_call(by_block(turn(sent, ("high", "low"))), angle, azimuth_tables(angle.shape[0]))
    every = lax.all_gather(mine, "acq", axis=0)
    partner = lax.dynamic_index_in_dim(pairs, lax.axis_index("acq"), 1, keepdims=False)
    partners = [lax.dynamic_index_in_dim(every, partner[r], 0, keepdims=False) for r in range(rounds)]
    looked = turn(cross_call(mine, partners, tiles), ("high", "low"))
    result = place_call(looked, list(range(tiles)), columns // LOOK_RG, 1)
    return result.reshape(2, rounds, 1, -1, result.shape[1])


def shards(tiles, acqs, echo, slant, angle, pairs):
    fits = echo.shape[2] > SUB and tiles == FAR * FAR and angle.shape[2] % (6 * LANES) == 0 and AOI // LOOK_AZ % (tiles * SUB) == 0
    program = joint if acqs == 2 and fits else separate
    return program(tiles, echo, slant, angle[0], pairs)


def solution(mesh):
    acqs, tiles = mesh.shape["acq"], mesh.shape["tile"]
    low = 1 << (tiles.bit_length() // 2)
    low = low if tiles % low == 0 else 1
    split_mesh = jax.sharding.Mesh(mesh.devices.reshape(acqs, tiles // low, low), ("acq", "high", "low"))
    tile = ("high", "low")
    in_specs = (P(None, "acq", tile, None), P(None, "acq", None), P("acq", None, tile), P())
    out_specs = P(None, None, "acq", tile, None)
    body = functools.partial(shards, tiles, acqs)
    return jax.shard_map(body, mesh=split_mesh, in_specs=in_specs, out_specs=out_specs, check_vma=False)
```

```python
import functools
import math

import jax
import jax.numpy as jnp
import ml_dtypes
import numpy as np
from jax import lax
from jax.experimental import pallas as pl
from jax.experimental.pallas import tpu as pltpu
from jax.sharding import PartitionSpec as P

LOOK_AZ = 2
LOOK_RG = 8
AOI = 256
LANES = 128
SUB = 8
FAR = 4
BATCH = 4
VMEM_LIMIT = 56 * 1024 * 1024


def high_low(table):
    high = table.astype(ml_dtypes.bfloat16)
    low = (table - high.astype(np.float64)).astype(ml_dtypes.bfloat16)
    return np.stack([high, low])


def trig(product, period):
    angle = (product % period) * (2.0 * math.pi / period)
    return np.cos(angle), np.sin(angle)


def split(value):
    high = value.astype(jnp.bfloat16)
    return high, (value - high.astype(jnp.float32)).astype(jnp.bfloat16)


def dot(left, right):
    return jnp.dot(left, right, preferred_element_type=jnp.float32)


def dot_stacked(table, value):
    high, low = split(value)
    both = dot(table, jnp.concatenate([high, low], axis=0))
    rows = table.shape[0] // 2
    return both[:rows] + both[rows:]


def thirds(a, b, c, sign):
    scale = sign * math.sqrt(3.0) / 2.0
    tr, ti = b[0] + c[0], b[1] + c[1]
    vr, vi = (b[0] - c[0]) * scale, (b[1] - c[1]) * scale
    ur, ui = a[0] - 0.5 * tr, a[1] - 0.5 * ti
    return (a[0] + tr, a[1] + ti), (ur - vi, ui + vr), (ur + vi, ui - vr)


def dot_table_right(value, table):
    high, low = split(value)
    return dot(jnp.concatenate([high, low, high], axis=1), table)


def stacked(table):
    high, low = high_low(table)
    return np.block([[high, high], [low, np.zeros_like(low)]])


def range_tables(length, order, halves):
    inner = LANES
    outer = length // inner
    part = outer // 3
    k1 = np.arange(outer)
    q = np.arange(inner)
    inside = np.arange(part)
    per_tile = outer // len(order)
    blocks = per_tile // halves
    a1, a4 = [], []
    for p0 in range(3):
        c, s = trig(np.outer(inside, 3 * inside + p0), outer)
        a1.append(stacked(np.block([[c, s], [-s, c]])))
        c, s = trig(np.outer(3 * inside + p0, inside), outer)
        rows = [
            cc * part + (t * per_tile + half * blocks) // 3 + b
            for half in range(halves)
            for t in order
            for cc in range(2)
            for b in range(blocks // 3)
        ]
        a4.append(stacked(np.block([[c, -s], [s, c]])[np.array(rows)] / length))
    c2, s2 = trig(np.outer(q, q), inner)
    b2 = np.block([[c2, -s2], [s2, c2]])
    b3 = np.block([[c2, s2], [-s2, c2]])
    ct, st = trig(np.outer(k1, q), length)
    twiddle = np.stack([ct, st]).astype(np.float32)
    b2, b3 = [np.concatenate(high_low(t)[[0, 0, 1]]) for t in (b2, b3)]
    return np.stack(a1), b2, b3, np.stack(a4), twiddle


def spot(tile, low):
    return lax.rem(tile, low) * FAR + lax.div(tile, low)


def range_kernel(outer, early, x_ref, slant_ref, a1_ref, b2_ref, b3_ref, a4_ref, t_ref, *rest):
    outs, (rows_ref, h_ref), held = rest[: 1 + early], rest[1 + early : 3 + early], rest[3 + early :]
    part = outer // 3

    @pl.when(pl.program_id(0) == 0)
    def _():
        for c in range(2):
            for k2 in range(LANES):
                rows_ref[c, k2 : k2 + 1, :outer] = slant_ref[c, :, k2 * outer : (k2 + 1) * outer]
            h_ref[c] = rows_ref[c].T[:outer]

    rows = outs[0].shape[2]
    turned = held[0] if early else outs[0].reshape(outs[0].shape[0] * rows, LANES)
    ct, st = t_ref[0], t_ref[1]
    hr, hi = h_ref[0], h_ref[1]

    def batch(first):
        lines = range(first, first + BATCH)
        y = []
        for p0 in range(3):
            x = [
                jnp.concatenate(
                    [x_ref[c, 0, pl.ds(p0 * SUB + l, part, stride=3 * SUB), :] for c in range(2)], axis=0
                )
                for l in lines
            ]
            value = dot_stacked(a1_ref[p0], jnp.concatenate(x, axis=1))
            y.append((value[:part], value[part:]))
        yield
        y = thirds(*y, -1.0)
        z = []
        for b in range(BATCH):
            yr, yi = [
                jnp.concatenate([v[c][:, b * LANES : (b + 1) * LANES] for v in y], axis=0) for c in range(2)
            ]
            z.append(jnp.concatenate([yr * ct + yi * st, yi * ct - yr * st], axis=1))
        y = dot_table_right(jnp.concatenate(z, axis=0), b2_ref[...])
        yield
        z = []
        for b in range(BATCH):
            yr = y[b * outer : (b + 1) * outer, :LANES]
            yi = y[b * outer : (b + 1) * outer, LANES:]
            z.append(jnp.concatenate([yr * hr - yi * hi, yr * hi + yi * hr], axis=1))
        y = dot_table_right(jnp.concatenate(z, axis=0), b3_ref[...])
        yield
        z = []
        for b in range(BATCH):
            yr = y[b * outer : (b + 1) * outer, :LANES]
            yi = y[b * outer : (b + 1) * outer, LANES:]
            zr, zi = yr * ct - yi * st, yi * ct + yr * st
            z.append(thirds(*[(zr[k * part : (k + 1) * part], zi[k * part : (k + 1) * part]) for k in range(3)], 1.0))
        y = []
        for p0 in range(3):
            value = jnp.concatenate([jnp.concatenate(z[b][p0], axis=0) for b in range(BATCH)], axis=1)
            y.append(dot_stacked(a4_ref[p0], value))
        yield
        for p0 in range(3):
            for b, l in enumerate(lines):
                turned[pl.ds(p0 * SUB + l, 2 * part, stride=3 * SUB), :] = y[p0][
                    :, b * LANES : (b + 1) * LANES
                ]
        yield

    batches = [batch(first) for first in range(0, SUB, BATCH)]
    for _ in range(5):
        for work in batches:
            next(work)
    if not early:
        return
    near = outs[0].shape[0] // 2
    acq = lax.axis_index("acq")
    place = lax.axis_index("high") * (2 * near // FAR) + lax.axis_index("low")
    for k, out in enumerate(outs):
        for s in range(2 * near):
            tile = jnp.bitwise_xor(place, s % near + k * near)
            dest = jnp.bitwise_xor(acq, s // near) * 2 * near + spot(tile, 2 * near // FAR)
            out[s, 0] = turned[pl.ds(pl.multiple_of(dest * rows, SUB), rows), :]


def range_call(echo, slant, first, steps, order, halves, early=False):
    length = echo.shape[3]
    outer = length // LANES
    view = echo.reshape(2, -1, SUB, outer, LANES).transpose(0, 1, 3, 2, 4).reshape(2, -1, outer * SUB, LANES)
    tables = [slant, *range_tables(length, order, halves)]
    dests = len(order) * halves
    rows = 2 * outer // dests * SUB
    whole = lambda shape: pl.BlockSpec(shape, lambda s: (0,) * len(shape))
    macs = steps * SUB * length * 2 * (2 * outer + 2 * LANES) * 2 * 3
    outs = 1 + early
    return pl.pallas_call(
        functools.partial(range_kernel, outer, early),
        grid=(steps,),
        in_specs=[pl.BlockSpec((2, 1, outer * SUB, LANES), lambda s: (0, first + s, 0, 0))]
        + [whole(t.shape) for t in tables],
        out_specs=[pl.BlockSpec((dests // outs, 1, rows, LANES), lambda s: (0, s, 0, 0))] * outs,
        scratch_shapes=[
            pltpu.VMEM((2, LANES, LANES), jnp.float32),
            pltpu.VMEM((2, outer, LANES), jnp.float32),
        ]
        + [pltpu.VMEM((dests * rows, LANES), jnp.float32)] * early,
        out_shape=[jax.ShapeDtypeStruct((dests // outs, steps, rows, LANES), jnp.float32)] * outs,
        compiler_params=pltpu.CompilerParams(vmem_limit_bytes=VMEM_LIMIT),
        cost_estimate=pl.CostEstimate(
            flops=2 * macs, bytes_accessed=16 * steps * SUB * length, transcendentals=0
        ),
        name=f"range_compress_{first}",
    )(view, *[jnp.asarray(t) for t in tables])


def pair_kernel(kept_ref, came_ref, *outs):
    for s, out in enumerate(outs):
        out[0] = kept_ref[s, 0]
        out[1] = came_ref[s, 0]


def pair_call(kept, came):
    count, _, rows, _ = kept.shape
    vmem = pl.BlockSpec(memory_space=pltpu.VMEM)
    return pl.pallas_call(
        pair_kernel,
        in_specs=[vmem] * 2,
        out_specs=[vmem] * count,
        out_shape=[jax.ShapeDtypeStruct((2, rows, LANES), jnp.float32)] * count,
        compiler_params=pltpu.CompilerParams(vmem_limit_bytes=VMEM_LIMIT),
        cost_estimate=pl.CostEstimate(flops=10**12, bytes_accessed=4 * kept.size, transcendentals=0),
        name="pair_halves",
    )(kept, came)


def azimuth_tables(length):
    part = length // 6
    f1 = np.arange(part)
    forward, backward = [], []
    first = (length - AOI) // 2
    u, s = np.arange(part // LOOK_AZ), np.arange(LOOK_AZ)
    lines = (first + u[None, :] * LOOK_AZ + s[:, None]).reshape(-1)
    for f0 in range(6):
        c, s = trig(np.outer(6 * f1 + f0, np.arange(part)), length)
        forward.append(np.block([[c, s], [-s, c]]))
        c, s = trig(np.outer(lines, 6 * f1 + f0), length)
        backward.append(np.block([[c, -s], [s, c]]) / length)
    return [np.concatenate(high_low(np.stack(t)), axis=1) for t in (forward, backward)]


def cos_sin(angle):
    y = 0.5 * angle
    z = y * y
    sine = [1.0, -1 / 6, 1 / 120, -1 / 5040, 1 / 362880, -1 / 39916800]
    cosine = [1.0, -1 / 2, 1 / 24, -1 / 720, 1 / 40320, -1 / 3628800, 1 / 479001600]
    s, c = sine[-1], cosine[-1]
    for k in sine[-2::-1]:
        s = s * z + k
    for k in cosine[-2::-1]:
        c = c * z + k
    s = s * y
    return 1.0 - 2.0 * (s * s), 2.0 * (s * c)


def three_pass(table, value):
    high, low = split(value)
    both = dot(table, high)
    rows = table.shape[0] // 2
    return (both[:rows] + both[rows:]) + dot(table[:rows], low)


def focus(xr, xi, cos_sin_of, tables):
    fw, bw = tables
    part, width = xr.shape[0] // 6, xr.shape[1]
    x = [(xr[k * part : (k + 1) * part], xi[k * part : (k + 1) * part]) for k in range(6)]
    classes = [None] * 6
    sums = thirds(*[(x[k][0] + x[k + 3][0], x[k][1] + x[k + 3][1]) for k in range(3)], -1.0)
    signs = [(x[k][0] - x[k + 3][0], x[k][1] - x[k + 3][1]) for k in range(3)]
    signs[1] = (x[4][0] - x[1][0], x[4][1] - x[1][1])
    diffs = thirds(*signs, -1.0)
    for e in range(3):
        classes[2 * e] = sums[e]
        classes[(2 * e + 3) % 6] = diffs[e]
    z, forward = [], []
    for f0 in range(7):
        if f0 < 6:
            forward.append(three_pass(fw[f0], jnp.concatenate(classes[f0], axis=0)))
        if f0 > 0:
            y, k = forward[f0 - 1], f0 - 1
            dr, di = y[:part], y[part:]
            pc, ps = cos_sin_of(k)
            e = jnp.concatenate([dr * pc - di * ps, dr * ps + di * pc], axis=0)
            z.append(three_pass(bw[k], e))
    half = math.sqrt(3.0) / 2.0
    first = (z[0] + z[3]) + (z[1] + z[4]) + (z[2] + z[5])
    a, b, c = z[0] - z[3], z[1] - z[4], z[2] - z[5]
    real = a + 0.5 * (b - c)
    turned = (b + c) * half
    fr = jnp.concatenate([first[:part], real[:part] - turned[part:]], axis=0)
    fi = jnp.concatenate([first[part:], real[part:] + turned[:part]], axis=0)
    return fr, fi


def lines_of(refs, first, order, part):
    tiles = len(order)
    at = [x[pl.ds(first, tiles), :, part, 0] for x in refs]
    value = at[0] if len(at) == 1 else jnp.concatenate(at, axis=1)
    if order != list(range(tiles)):
        value = jnp.stack([value[order.index(t)] for t in range(tiles)])
    return value.reshape(-1, LANES)


def looked_at(field, look):
    half = AOI // 2
    quarter = half // LOOK_AZ
    added = [field[h * half : h * half + quarter] + field[h * half + quarter : (h + 1) * half] for h in range(2)]
    high, low = split(jnp.concatenate(added, axis=0))
    return dot(high, look) + dot(low, look)


def joint_kernel(order, rounds, me_ref, same_ref, x_ref, early_ref, own_angle, other_angle, fw, bw, look_ref, out, stage):
    acq = me_ref[0]
    tiles = len(order)
    near = tiles // 2
    firsts = [acq * tiles, (1 - acq) * tiles]
    for part in range(2):
        for k, first in enumerate(firsts):
            lanes = slice(k * LANES, (k + 1) * LANES)
            for place, t in enumerate(order):
                stage[part, t, 1:, :, lanes] = x_ref[first + place, :, part, 0]
            for s in range(near):
                for side in range(2):
                    tile = jnp.bitwise_xor(me_ref[1], s + side * near)
                    stage[part, tile, 0, :, lanes] = early_ref[k * near + s, side, part, 0]
    xr, xi = [stage[part].reshape(-1, 2 * LANES) for part in range(2)]
    class_of = lambda k: pl.ds(k, AOI // 2, stride=6)
    phases = lambda k: cos_sin(jnp.concatenate([a[class_of(k), :] for a in (own_angle, other_angle)], axis=1))
    fr, fi = focus(xr, xi, phases, [fw, bw])
    mr, mi, pr, pi = fr[:, :LANES], fi[:, :LANES], fr[:, LANES:], fi[:, LANES:]
    look = look_ref[0]
    cross_real = looked_at(mr * pr + mi * pi, look[0])
    cross_imag = looked_at(mi * pr - mr * pi, look[1])
    own_real = looked_at(mr * mr + mi * mi, look[0])
    own_imag = looked_at(mi * mr - mr * mi, look[1])
    other_real = looked_at(pr * pr + pi * pi, look[0])
    other_imag = looked_at(pi * pr - pr * pi, look[1])
    per = AOI // LOOK_AZ // tiles

    @pl.when(pl.program_id(0) == 0)
    def _():
        out[...] = jnp.zeros_like(out)

    for r in range(rounds):
        same = same_ref[r] != 0
        own = jnp.where(same, own_real + own_imag, cross_real + cross_imag)
        other = jnp.where(same, other_real + other_imag, cross_real - cross_imag)
        for first, value in zip(firsts, (own, other)):
            for place, t in enumerate(order):
                out[first + place, r * per : (r + 1) * per, :] += value[t * per : (t + 1) * per]


def joint_call(me, same, array, early, angle, other_angle, tables, order):
    dests, steps, _, blocks = array.shape[:4]
    tiles = len(order)
    lines = angle.shape[0]
    rounds = same.shape[0]
    rows = rounds * (AOI // LOOK_AZ // tiles)
    wide = blocks * LANES // LOOK_RG
    look = np.stack(
        [
            np.stack([look_table(LANES, c * wide + b * LANES // LOOK_RG) for c in range(2)])
            for b in range(blocks)
        ]
    )
    block = lambda a: pl.BlockSpec(a.shape[:3] + (1, SUB, LANES), lambda b, me, same: (0, 0, 0, b, 0, 0))
    return pl.pallas_call(
        functools.partial(joint_kernel, order, rounds),
        grid_spec=pltpu.PrefetchScalarGridSpec(
            num_scalar_prefetch=2,
            grid=(blocks,),
            in_specs=[
                block(array),
                block(early),
                pl.BlockSpec((lines, LANES), lambda b, me, same: (0, me[0] * blocks + b)),
                pl.BlockSpec((lines, LANES), lambda b, me, same: (0, b)),
                *[pl.BlockSpec(t.shape, lambda b, me, same: (0, 0, 0)) for t in tables],
                pl.BlockSpec((1,) + look.shape[1:], lambda b, me, same: (b, 0, 0, 0)),
            ],
            out_specs=pl.BlockSpec((dests, rows, LANES), lambda b, me, same: (0, 0, 0)),
            scratch_shapes=[pltpu.VMEM((2, tiles, steps + 1, SUB, 2 * LANES), jnp.float32)],
        ),
        out_shape=jax.ShapeDtypeStruct((dests, rows, LANES), jnp.float32),
        compiler_params=pltpu.CompilerParams(vmem_limit_bytes=VMEM_LIMIT),
        cost_estimate=pl.CostEstimate(
            flops=2 * 2 * 3 * 6 * 256 * 256 * 2 * LANES * blocks,
            bytes_accessed=20 * lines * 2 * LANES * blocks,
            transcendentals=0,
        ),
        name="azimuth_interferogram",
    )(me, same, array, early, angle, other_angle, *[jnp.asarray(t) for t in tables], jnp.asarray(look))


def single_kernel(tiles, x_ref, angle_ref, fw, bw, out):
    xr, xi = [lines_of([x_ref], 0, list(range(tiles)), part) for part in range(2)]
    fr, fi = focus(xr, xi, lambda k: cos_sin(angle_ref[pl.ds(k, AOI // 2, stride=6), :]), [fw, bw])
    out[:AOI] = fr
    out[AOI:] = fi


def single_call(array, angle, tables):
    tiles = array.shape[0]
    lines, columns = angle.shape
    return pl.pallas_call(
        functools.partial(single_kernel, tiles),
        grid=(columns // LANES,),
        in_specs=[
            pl.BlockSpec((tiles, array.shape[1], 2, 1, SUB, LANES), lambda b: (0, 0, 0, b, 0, 0)),
            pl.BlockSpec((lines, LANES), lambda b: (0, b)),
        ]
        + [pl.BlockSpec(t.shape, lambda b: (0, 0, 0)) for t in tables],
        out_specs=pl.BlockSpec((2 * AOI, LANES), lambda b: (0, b)),
        out_shape=jax.ShapeDtypeStruct((2 * AOI, columns), jnp.float32),
        compiler_params=pltpu.CompilerParams(vmem_limit_bytes=VMEM_LIMIT),
        name="azimuth_focus",
    )(array, angle, *[jnp.asarray(t) for t in tables])


def look_table(width, offset):
    table = np.zeros((width, LANES), np.float64)
    table[np.arange(width), offset + np.arange(width) // LOOK_RG] = 1.0 / (LOOK_AZ * LOOK_RG)
    return table.astype(ml_dtypes.bfloat16)


def cross_kernel(rounds, tiles, mine_ref, *refs):
    partner_refs, look_ref, out = refs[:rounds], refs[-2], refs[-1]
    mr, mi = mine_ref[:AOI], mine_ref[AOI:]
    per = AOI // LOOK_AZ // tiles
    for r in range(rounds):
        pr, pi = partner_refs[r][:AOI], partner_refs[r][AOI:]
        for c, field in enumerate((mr * pr + mi * pi, mi * pr - mr * pi)):
            looked = looked_at(field, look_ref[...])
            at = (c * rounds + r) * per
            for t in range(tiles):
                out[t, at : at + per, :] = looked[t * per : (t + 1) * per]


def cross_call(mine, partners, tiles):
    rounds = len(partners)
    width = mine.shape[1]
    look = jnp.asarray(look_table(width, 0))
    shape = (tiles, 2 * rounds * (AOI // LOOK_AZ // tiles), LANES)
    vmem = lambda: pl.BlockSpec(memory_space=pltpu.VMEM)
    return pl.pallas_call(
        functools.partial(cross_kernel, rounds, tiles),
        in_specs=[vmem() for _ in range(rounds + 2)],
        out_specs=vmem(),
        out_shape=jax.ShapeDtypeStruct(shape, jnp.float32),
        compiler_params=pltpu.CompilerParams(vmem_limit_bytes=VMEM_LIMIT),
        name="interferogram",
    )(mine, *partners, look)


def place_kernel(sources, valid, parts, in_ref, out):
    rows = in_ref.shape[1]
    lane = lax.broadcasted_iota(jnp.int32, (rows, LANES), 1)
    for c in range(parts):
        for o in range(len(sources) * valid // LANES):
            acc = None
            for place, source in enumerate(sources):
                shift = place * valid - o * LANES
                if shift + valid <= 0 or shift >= LANES:
                    continue
                value = in_ref[source]
                turn_by = (shift - c * valid) % LANES
                if turn_by:
                    value = pltpu.roll(value, turn_by, 1)
                acc = value if acc is None else jnp.where(lane >= shift, value, acc)
            out[c * rows : (c + 1) * rows, o * LANES : (o + 1) * LANES] = acc


def place_call(received, sources, valid, parts):
    _, rows, _ = received.shape
    return pl.pallas_call(
        functools.partial(place_kernel, sources, valid, parts),
        in_specs=[pl.BlockSpec(memory_space=pltpu.VMEM)],
        out_specs=pl.BlockSpec(memory_space=pltpu.VMEM),
        out_shape=jax.ShapeDtypeStruct((parts * rows, len(sources) * valid), jnp.float32),
        compiler_params=pltpu.CompilerParams(vmem_limit_bytes=VMEM_LIMIT),
        name="place_samples",
    )(received)


def turn(array, axes):
    return lax.all_to_all(array, axes, split_axis=0, concat_axis=0, tiled=True)


def by_block(array):
    dests, steps, rows, _ = array.shape
    return array.reshape(dests, steps, 2, rows // (2 * SUB), SUB, LANES)


def joint(tiles, echo, slant, angle, pairs):
    steps = echo.shape[2] // SUB
    columns = angle.shape[1]
    rounds = pairs.shape[0]
    acq = lax.axis_index("acq")
    same = (lax.dynamic_index_in_dim(pairs, acq, 1, keepdims=False) == acq).astype(jnp.int32)
    theirs = lax.dynamic_slice_in_dim(angle, (1 - acq) * (columns // 2), columns // 2, 1)
    other_angle = lax.ppermute(theirs, "acq", [(0, 1), (1, 0)])
    low = lax.axis_size("low")
    order = [h * low + k for k in range(low) for h in range(tiles // low)]
    axes = ("acq", "low", "high")
    tile = lax.axis_index("high") * low + lax.axis_index("low")
    me = jnp.stack([acq, tile]).astype(jnp.int32)
    kept, given = range_call(echo, slant, 0, 1, order, 2, early=True)
    came = lax.ppermute(given, "high", [(h, h ^ (FAR // 2)) for h in range(FAR)])
    (sent,) = range_call(echo, slant, 1, steps - 1, order, 2)
    array = by_block(turn(sent, axes))
    early = list(pair_call(kept, came))
    near = tiles // 2
    for s in range(1, tiles):
        flip = s // near * tiles + s % near
        early[s] = lax.ppermute(early[s], ("acq", "high", "low"), [(i, i ^ flip) for i in range(2 * tiles)])
    early = by_block(jnp.stack(early))
    looked = joint_call(me, same, array, early, angle, other_angle, azimuth_tables(angle.shape[0]), order)
    sources = [half * tiles + order.index(t) for t in range(tiles) for half in range(2)]
    result = place_call(turn(looked, axes), sources, columns // 2 // LOOK_RG, 2)
    return result.reshape(2, rounds, 1, -1, result.shape[1])


def separate(tiles, echo, slant, angle, pairs):
    columns = angle.shape[1]
    rounds = pairs.shape[0]
    (sent,) = range_call(echo, slant, 0, echo.shape[2] // SUB, list(range(tiles)), 1)
    mine = single_call(by_block(turn(sent, ("high", "low"))), angle, azimuth_tables(angle.shape[0]))
    every = lax.all_gather(mine, "acq", axis=0)
    partner = lax.dynamic_index_in_dim(pairs, lax.axis_index("acq"), 1, keepdims=False)
    partners = [lax.dynamic_index_in_dim(every, partner[r], 0, keepdims=False) for r in range(rounds)]
    looked = turn(cross_call(mine, partners, tiles), ("high", "low"))
    result = place_call(looked, list(range(tiles)), columns // LOOK_RG, 1)
    return result.reshape(2, rounds, 1, -1, result.shape[1])


def shards(tiles, acqs, echo, slant, angle, pairs):
    fits = echo.shape[2] > SUB and tiles == FAR * FAR and angle.shape[2] % (6 * LANES) == 0 and AOI // LOOK_AZ % (tiles * SUB) == 0
    program = joint if acqs == 2 and fits else separate
    return program(tiles, echo, slant, angle[0], pairs)


def solution(mesh):
    acqs, tiles = mesh.shape["acq"], mesh.shape["tile"]
    low = 1 << (tiles.bit_length() // 2)
    low = low if tiles % low == 0 else 1
    split_mesh = jax.sharding.Mesh(mesh.devices.reshape(acqs, tiles // low, low), ("acq", "high", "low"))
    tile = ("high", "low")
    in_specs = (P(None, "acq", tile, None), P(None, "acq", None), P("acq", None, tile), P())
    out_specs = P(None, None, "acq", tile, None)
    body = functools.partial(shards, tiles, acqs)
    return jax.shard_map(body, mesh=split_mesh, in_specs=in_specs, out_specs=out_specs, check_vma=False)
```

```python
import functools
import math

import jax
import jax.numpy as jnp
import ml_dtypes
import numpy as np
from jax import lax
from jax.experimental import pallas as pl
from jax.experimental.pallas import tpu as pltpu
from jax.sharding import PartitionSpec as P

LOOK_AZ = 2
LOOK_RG = 8
AOI = 256
LANES = 128
SUB = 8
FAR = 4
CLASSES = 12
BATCH = 4
VMEM_LIMIT = 56 * 1024 * 1024


def high_low(table):
    high = table.astype(ml_dtypes.bfloat16)
    low = (table - high.astype(np.float64)).astype(ml_dtypes.bfloat16)
    return np.stack([high, low])


def trig(product, period):
    angle = (product % period) * (2.0 * math.pi / period)
    return np.cos(angle), np.sin(angle)


def split(value):
    high = value.astype(jnp.bfloat16)
    return high, (value - high.astype(jnp.float32)).astype(jnp.bfloat16)


def dot(left, right):
    return jnp.dot(left, right, preferred_element_type=jnp.float32)


def dot_stacked(table, value):
    high, low = split(value)
    both = dot(table, jnp.concatenate([high, low], axis=0))
    rows = table.shape[0] // 2
    return both[:rows] + both[rows:]


def thirds(a, b, c, sign):
    scale = sign * math.sqrt(3.0) / 2.0
    tr, ti = b[0] + c[0], b[1] + c[1]
    vr, vi = (b[0] - c[0]) * scale, (b[1] - c[1]) * scale
    ur, ui = a[0] - 0.5 * tr, a[1] - 0.5 * ti
    return (a[0] + tr, a[1] + ti), (ur - vi, ui + vr), (ur + vi, ui - vr)


def dot_table_right(value, table):
    high, low = split(value)
    return dot(jnp.concatenate([high, low, high], axis=1), table)


def stacked(table):
    high, low = high_low(table)
    return np.block([[high, high], [low, np.zeros_like(low)]])


def range_tables(length, order, halves):
    inner = LANES
    outer = length // inner
    part = outer // 3
    k1 = np.arange(outer)
    q = np.arange(inner)
    inside = np.arange(part)
    per_tile = outer // len(order)
    blocks = per_tile // halves
    a1, a4 = [], []
    for p0 in range(3):
        c, s = trig(np.outer(inside, 3 * inside + p0), outer)
        a1.append(stacked(np.block([[c, s], [-s, c]])))
        c, s = trig(np.outer(3 * inside + p0, inside), outer)
        rows = [
            cc * part + (t * per_tile + half * blocks) // 3 + b
            for cc in range(2)
            for half in range(halves)
            for t in order
            for b in range(blocks // 3)
        ]
        a4.append(stacked(np.block([[c, -s], [s, c]])[np.array(rows)] / length))
    c2, s2 = trig(np.outer(q, q), inner)
    b2 = np.block([[c2, -s2], [s2, c2]])
    b3 = np.block([[c2, s2], [-s2, c2]])
    ct, st = trig(np.outer(k1, q), length)
    twiddle = np.stack([ct, st]).astype(np.float32)
    b2, b3 = [np.concatenate(high_low(t)[[0, 0, 1]]) for t in (b2, b3)]
    return np.stack(a1), b2, b3, np.stack(a4), twiddle


def spot(tile, low):
    return lax.rem(tile, low) * FAR + lax.div(tile, low)


def range_kernel(outer, early, x_ref, slant_ref, a1_ref, b2_ref, b3_ref, a4_ref, t_ref, *rest):
    outs, (rows_ref, h_ref), held = rest[: 1 + early], rest[1 + early : 3 + early], rest[3 + early :]
    part = outer // 3

    @pl.when(pl.program_id(0) == 0)
    def _():
        for c in range(2):
            for k2 in range(LANES):
                rows_ref[c, k2 : k2 + 1, :outer] = slant_ref[c, :, k2 * outer : (k2 + 1) * outer]
            h_ref[c] = rows_ref[c].T[:outer]

    rows = outs[0].shape[1] * outs[0].shape[3]
    turned = held[0] if early else outs[0].reshape(outs[0].shape[0] * rows, LANES)
    ct, st = t_ref[0], t_ref[1]
    hr, hi = h_ref[0], h_ref[1]

    def batch(first):
        lines = range(first, first + BATCH)
        y = []
        for p0 in range(3):
            x = [
                jnp.concatenate(
                    [x_ref[c, 0, pl.ds(p0 * SUB + l, part, stride=3 * SUB), :] for c in range(2)], axis=0
                )
                for l in lines
            ]
            value = dot_stacked(a1_ref[p0], jnp.concatenate(x, axis=1))
            y.append((value[:part], value[part:]))
        yield
        y = thirds(*y, -1.0)
        z = []
        for b in range(BATCH):
            yr, yi = [
                jnp.concatenate([v[c][:, b * LANES : (b + 1) * LANES] for v in y], axis=0) for c in range(2)
            ]
            z.append(jnp.concatenate([yr * ct + yi * st, yi * ct - yr * st], axis=1))
        y = dot_table_right(jnp.concatenate(z, axis=0), b2_ref[...])
        yield
        z = []
        for b in range(BATCH):
            yr = y[b * outer : (b + 1) * outer, :LANES]
            yi = y[b * outer : (b + 1) * outer, LANES:]
            z.append(jnp.concatenate([yr * hr - yi * hi, yr * hi + yi * hr], axis=1))
        y = dot_table_right(jnp.concatenate(z, axis=0), b3_ref[...])
        yield
        z = []
        for b in range(BATCH):
            yr = y[b * outer : (b + 1) * outer, :LANES]
            yi = y[b * outer : (b + 1) * outer, LANES:]
            zr, zi = yr * ct - yi * st, yi * ct + yr * st
            z.append(thirds(*[(zr[k * part : (k + 1) * part], zi[k * part : (k + 1) * part]) for k in range(3)], 1.0))
        y = []
        for p0 in range(3):
            value = jnp.concatenate([jnp.concatenate(z[b][p0], axis=0) for b in range(BATCH)], axis=1)
            y.append(dot_stacked(a4_ref[p0], value))
        yield
        for p0 in range(3):
            for b, l in enumerate(lines):
                for c in range(2):
                    turned[pl.ds((2 * p0 + c) * SUB + l, part, stride=6 * SUB), :] = y[p0][
                        c * part : (c + 1) * part, b * LANES : (b + 1) * LANES
                    ]
        yield

    batches = [batch(first) for first in range(0, SUB, BATCH)]
    for _ in range(5):
        for work in batches:
            next(work)
    if not early:
        return
    near = outs[0].shape[0] // 2
    acq = lax.axis_index("acq")
    place = lax.axis_index("high") * (2 * near // FAR) + lax.axis_index("low")
    for k, out in enumerate(outs):
        for s in range(2 * near):
            tile = jnp.bitwise_xor(place, s % near + k * near)
            dest = jnp.bitwise_xor(acq, s // near) * 2 * near + spot(tile, 2 * near // FAR)
            value = turned[pl.ds(pl.multiple_of(dest * rows, SUB), rows), :]
            out[s, :, 0] = value.reshape(out.shape[1], out.shape[3], LANES)


def range_call(echo, slant, first, steps, order, halves, early=False):
    length = echo.shape[3]
    outer = length // LANES
    view = echo.reshape(2, -1, SUB, outer, LANES).transpose(0, 1, 3, 2, 4).reshape(2, -1, outer * SUB, LANES)
    tables = [slant, *range_tables(length, order, halves)]
    dests = len(order) * halves
    blocks = outer // dests
    rows = 2 * blocks * SUB
    whole = lambda shape: pl.BlockSpec(shape, lambda s: (0,) * len(shape))
    macs = steps * SUB * length * 2 * (2 * outer + 2 * LANES) * 2 * 3
    outs = 1 + early
    return pl.pallas_call(
        functools.partial(range_kernel, outer, early),
        grid=(steps,),
        in_specs=[pl.BlockSpec((2, 1, outer * SUB, LANES), lambda s: (0, first + s, 0, 0))]
        + [whole(t.shape) for t in tables],
        out_specs=[pl.BlockSpec((dests // outs, blocks, 1, 2 * SUB, LANES), lambda s: (0, 0, s, 0, 0))] * outs,
        scratch_shapes=[
            pltpu.VMEM((2, LANES, LANES), jnp.float32),
            pltpu.VMEM((2, outer, LANES), jnp.float32),
        ]
        + [pltpu.VMEM((dests * rows, LANES), jnp.float32)] * early,
        out_shape=[jax.ShapeDtypeStruct((dests // outs, blocks, steps, 2 * SUB, LANES), jnp.float32)] * outs,
        compiler_params=pltpu.CompilerParams(vmem_limit_bytes=VMEM_LIMIT),
        cost_estimate=pl.CostEstimate(
            flops=2 * macs, bytes_accessed=16 * steps * SUB * length, transcendentals=0
        ),
        name=f"range_compress_{first}",
    )(view, *[jnp.asarray(t) for t in tables])


def pair_kernel(kept_ref, came_ref, *outs):
    for s, out in enumerate(outs):
        out[0] = kept_ref[s, :, 0]
        out[1] = came_ref[s, :, 0]


def pair_call(kept, came):
    count, blocks, _, rows, _ = kept.shape
    vmem = pl.BlockSpec(memory_space=pltpu.VMEM)
    return pl.pallas_call(
        pair_kernel,
        in_specs=[vmem] * 2,
        out_specs=[vmem] * count,
        out_shape=[jax.ShapeDtypeStruct((2, blocks, rows, LANES), jnp.float32)] * count,
        compiler_params=pltpu.CompilerParams(vmem_limit_bytes=VMEM_LIMIT),
        cost_estimate=pl.CostEstimate(flops=10**12, bytes_accessed=4 * kept.size, transcendentals=0),
        name="pair_halves",
    )(kept, came)


def azimuth_tables(length):
    part = length // CLASSES
    f1 = np.arange(part)
    ahead, back = [], []
    first = (length - AOI) // 2
    u, s = np.arange(part // LOOK_AZ), np.arange(LOOK_AZ)
    lines = (first + u[None, :] * LOOK_AZ + s[:, None]).reshape(-1)
    for f0 in range(CLASSES):
        c, s = trig(np.outer(CLASSES * f1 + f0, np.arange(part)), length)
        ahead.append(stacked(np.block([[c, s], [-s, c]])))
        c, s = trig(np.outer(lines, CLASSES * f1 + f0), length)
        back.append(stacked(np.block([[c, -s], [s, c]]) / length))
    return [np.stack(ahead), np.stack(back)]


def cos_sin(angle):
    y = 0.5 * angle
    z = y * y
    sine = [1.0, -1 / 6, 1 / 120, -1 / 5040, 1 / 362880, -1 / 39916800]
    cosine = [1.0, -1 / 2, 1 / 24, -1 / 720, 1 / 40320, -1 / 3628800, 1 / 479001600]
    s, c = sine[-1], cosine[-1]
    for k in sine[-2::-1]:
        s = s * z + k
    for k in cosine[-2::-1]:
        c = c * z + k
    s = s * y
    return 1.0 - 2.0 * (s * s), 2.0 * (s * c)


def fours(a, b, c, d):
    (ar, ai), (br, bi), (cr, ci), (dr, di) = a, b, c, d
    pr, pi, mr, mi = ar + cr, ai + ci, ar - cr, ai - ci
    qr, qi, nr, ni = br + dr, bi + di, br - dr, bi - di
    return (pr + qr, pi + qi), (mr + ni, mi - nr), (pr - qr, pi - qi), (mr - ni, mi + nr)


def class_of(e, g):
    return (4 * e + 9 * g) % CLASSES


def focus(xr, xi, phases, tables):
    fw, bw = tables
    part = xr.shape[0] // CLASSES
    x = [(xr[k * part : (k + 1) * part], xi[k * part : (k + 1) * part]) for k in range(CLASSES)]
    columns = [thirds(*[x[(4 * i + 3 * j) % CLASSES] for i in range(3)], -1.0) for j in range(4)]
    classes = [None] * CLASSES
    for e in range(3):
        for g, pair in enumerate(fours(*[columns[j][e] for j in range(4)])):
            classes[class_of(e, g)] = pair
    z, forward = [], []
    for f0 in range(CLASSES + 1):
        if f0 < CLASSES:
            forward.append(dot_stacked(fw[f0], jnp.concatenate(classes[f0], axis=0)))
        if f0 > 0:
            y, k = forward[f0 - 1], f0 - 1
            dr, di = y[:part], y[part:]
            pc, ps = phases(k)
            e = jnp.concatenate([dr * pc - di * ps, dr * ps + di * pc], axis=0)
            y = dot_stacked(bw[k], e)
            z.append((y[:part], y[part:]))
    sums = [fours(*[z[class_of(e, g)] for g in range(4)]) for e in range(3)]
    outs = []
    for h in range(AOI // part):
        terms = [sums[e][h] for e in range(3)]
        outs.append(thirds(*terms, 1.0)[h % 3])
    return [jnp.concatenate([pair[c] for pair in outs], axis=0) for c in range(2)]


def looked_at(field, look):
    lines = AOI // 4 // LOOK_AZ
    groups = [field[k * lines : (k + 1) * lines] for k in range(AOI // lines)]
    added = [groups[k] + groups[k + 1] for k in range(0, len(groups), LOOK_AZ)]
    high, low = split(jnp.concatenate(added, axis=0))
    return dot(high, look) + dot(low, look)


def joint_kernel(order, rounds, me_ref, same_ref, x_ref, early_ref, own_angle, other_angle, fw, bw, look_ref, out, stage):
    acq = me_ref[0]
    tiles = len(order)
    near = tiles // 2
    firsts = [acq * tiles, (1 - acq) * tiles]
    for part in range(2):
        for k, first in enumerate(firsts):
            lanes = slice(k * LANES, (k + 1) * LANES)
            for place, t in enumerate(order):
                stage[part, t, 1:, :, lanes] = x_ref[first + place, 0, :, part * SUB : (part + 1) * SUB, :]
            for s in range(near):
                for side in range(2):
                    tile = jnp.bitwise_xor(me_ref[1], s + side * near)
                    stage[part, tile, 0, :, lanes] = early_ref[k * near + s, side, 0, part * SUB : (part + 1) * SUB, :]
    xr, xi = [stage[part].reshape(-1, 2 * LANES) for part in range(2)]
    rows_of = lambda k: pl.ds(k, own_angle.shape[0] // CLASSES, stride=CLASSES)
    phases = lambda k: cos_sin(jnp.concatenate([a[rows_of(k), :] for a in (own_angle, other_angle)], axis=1))
    fr, fi = focus(xr, xi, phases, [fw, bw])
    mr, mi, pr, pi = fr[:, :LANES], fi[:, :LANES], fr[:, LANES:], fi[:, LANES:]
    look = look_ref[0]
    cross_real = looked_at(mr * pr + mi * pi, look[0])
    cross_imag = looked_at(mi * pr - mr * pi, look[1])
    own_real = looked_at(mr * mr + mi * mi, look[0])
    own_imag = looked_at(mi * mr - mr * mi, look[1])
    other_real = looked_at(pr * pr + pi * pi, look[0])
    other_imag = looked_at(pi * pr - pr * pi, look[1])
    per = AOI // LOOK_AZ // tiles

    @pl.when(pl.program_id(0) == 0)
    def _():
        out[...] = jnp.zeros_like(out)

    for r in range(rounds):
        same = same_ref[r] != 0
        own = jnp.where(same, own_real + own_imag, cross_real + cross_imag)
        other = jnp.where(same, other_real + other_imag, cross_real - cross_imag)
        for first, value in zip(firsts, (own, other)):
            for place, t in enumerate(order):
                out[first + place, r * per : (r + 1) * per, :] += value[t * per : (t + 1) * per]


def joint_call(me, same, array, early, angle, other_angle, tables, order):
    dests, blocks, steps = array.shape[:3]
    tiles = len(order)
    lines = angle.shape[0]
    rounds = same.shape[0]
    rows = rounds * (AOI // LOOK_AZ // tiles)
    wide = blocks * LANES // LOOK_RG
    look = np.stack(
        [
            np.stack([look_table(LANES, c * wide + b * LANES // LOOK_RG) for c in range(2)])
            for b in range(blocks)
        ]
    )
    return pl.pallas_call(
        functools.partial(joint_kernel, order, rounds),
        grid_spec=pltpu.PrefetchScalarGridSpec(
            num_scalar_prefetch=2,
            grid=(blocks,),
            in_specs=[
                pl.BlockSpec((dests, 1) + array.shape[2:], lambda b, me, same: (0, b, 0, 0, 0)),
                pl.BlockSpec(early.shape[:2] + (1,) + early.shape[3:], lambda b, me, same: (0, 0, b, 0, 0)),
                pl.BlockSpec((lines, LANES), lambda b, me, same: (0, me[0] * blocks + b)),
                pl.BlockSpec((lines, LANES), lambda b, me, same: (0, b)),
                *[pl.BlockSpec(t.shape, lambda b, me, same: (0, 0, 0)) for t in tables],
                pl.BlockSpec((1,) + look.shape[1:], lambda b, me, same: (b, 0, 0, 0)),
            ],
            out_specs=pl.BlockSpec((dests, rows, LANES), lambda b, me, same: (0, 0, 0)),
            scratch_shapes=[pltpu.VMEM((2, tiles, steps + 1, SUB, 2 * LANES), jnp.float32)],
        ),
        out_shape=jax.ShapeDtypeStruct((dests, rows, LANES), jnp.float32),
        compiler_params=pltpu.CompilerParams(vmem_limit_bytes=VMEM_LIMIT),
        cost_estimate=pl.CostEstimate(
            flops=2 * 2 * 3 * 6 * 256 * 256 * 2 * LANES * blocks,
            bytes_accessed=20 * lines * 2 * LANES * blocks,
            transcendentals=0,
        ),
        name="azimuth_interferogram",
    )(me, same, array, early, angle, other_angle, *[jnp.asarray(t) for t in tables], jnp.asarray(look))


def single_kernel(tiles, x_ref, angle_ref, fw, bw, out):
    xr, xi = [x_ref[:, 0, :, part * SUB : (part + 1) * SUB, :].reshape(-1, LANES) for part in range(2)]
    fr, fi = focus(xr, xi, lambda k: cos_sin(angle_ref[pl.ds(k, angle_ref.shape[0] // CLASSES, stride=CLASSES), :]), [fw, bw])
    out[:AOI] = fr
    out[AOI:] = fi


def single_call(array, angle, tables):
    tiles = array.shape[0]
    lines, columns = angle.shape
    return pl.pallas_call(
        functools.partial(single_kernel, tiles),
        grid=(columns // LANES,),
        in_specs=[
            pl.BlockSpec((tiles, 1) + array.shape[2:], lambda b: (0, b, 0, 0, 0)),
            pl.BlockSpec((lines, LANES), lambda b: (0, b)),
        ]
        + [pl.BlockSpec(t.shape, lambda b: (0, 0, 0)) for t in tables],
        out_specs=pl.BlockSpec((2 * AOI, LANES), lambda b: (0, b)),
        out_shape=jax.ShapeDtypeStruct((2 * AOI, columns), jnp.float32),
        compiler_params=pltpu.CompilerParams(vmem_limit_bytes=VMEM_LIMIT),
        name="azimuth_focus",
    )(array, angle, *[jnp.asarray(t) for t in tables])


def look_table(width, offset):
    table = np.zeros((width, LANES), np.float64)
    table[np.arange(width), offset + np.arange(width) // LOOK_RG] = 1.0 / (LOOK_AZ * LOOK_RG)
    return table.astype(ml_dtypes.bfloat16)


def cross_kernel(rounds, tiles, mine_ref, *refs):
    partner_refs, look_ref, out = refs[:rounds], refs[-2], refs[-1]
    mr, mi = mine_ref[:AOI], mine_ref[AOI:]
    per = AOI // LOOK_AZ // tiles
    for r in range(rounds):
        pr, pi = partner_refs[r][:AOI], partner_refs[r][AOI:]
        for c, field in enumerate((mr * pr + mi * pi, mi * pr - mr * pi)):
            looked = looked_at(field, look_ref[...])
            at = (c * rounds + r) * per
            for t in range(tiles):
                out[t, at : at + per, :] = looked[t * per : (t + 1) * per]


def cross_call(mine, partners, tiles):
    rounds = len(partners)
    width = mine.shape[1]
    look = jnp.asarray(look_table(width, 0))
    shape = (tiles, 2 * rounds * (AOI // LOOK_AZ // tiles), LANES)
    vmem = lambda: pl.BlockSpec(memory_space=pltpu.VMEM)
    return pl.pallas_call(
        functools.partial(cross_kernel, rounds, tiles),
        in_specs=[vmem() for _ in range(rounds + 2)],
        out_specs=vmem(),
        out_shape=jax.ShapeDtypeStruct(shape, jnp.float32),
        compiler_params=pltpu.CompilerParams(vmem_limit_bytes=VMEM_LIMIT),
        name="interferogram",
    )(mine, *partners, look)


def place_kernel(sources, valid, parts, in_ref, out):
    rows = in_ref.shape[1]
    lane = lax.broadcasted_iota(jnp.int32, (rows, LANES), 1)
    for c in range(parts):
        for o in range(len(sources) * valid // LANES):
            acc = None
            for place, source in enumerate(sources):
                shift = place * valid - o * LANES
                if shift + valid <= 0 or shift >= LANES:
                    continue
                value = in_ref[source]
                turn_by = (shift - c * valid) % LANES
                if turn_by:
                    value = pltpu.roll(value, turn_by, 1)
                acc = value if acc is None else jnp.where(lane >= shift, value, acc)
            out[c * rows : (c + 1) * rows, o * LANES : (o + 1) * LANES] = acc


def place_call(received, sources, valid, parts):
    _, rows, _ = received.shape
    return pl.pallas_call(
        functools.partial(place_kernel, sources, valid, parts),
        in_specs=[pl.BlockSpec(memory_space=pltpu.VMEM)],
        out_specs=pl.BlockSpec(memory_space=pltpu.VMEM),
        out_shape=jax.ShapeDtypeStruct((parts * rows, len(sources) * valid), jnp.float32),
        compiler_params=pltpu.CompilerParams(vmem_limit_bytes=VMEM_LIMIT),
        name="place_samples",
    )(received)


def turn(array, axes):
    return lax.all_to_all(array, axes, split_axis=0, concat_axis=0, tiled=True)


def joint(tiles, echo, slant, angle, pairs):
    steps = echo.shape[2] // SUB
    columns = angle.shape[1]
    rounds = pairs.shape[0]
    acq = lax.axis_index("acq")
    same = (lax.dynamic_index_in_dim(pairs, acq, 1, keepdims=False) == acq).astype(jnp.int32)
    theirs = lax.dynamic_slice_in_dim(angle, (1 - acq) * (columns // 2), columns // 2, 1)
    other_angle = lax.ppermute(theirs, "acq", [(0, 1), (1, 0)])
    low = lax.axis_size("low")
    order = [h * low + k for k in range(low) for h in range(tiles // low)]
    axes = ("acq", "low", "high")
    tile = lax.axis_index("high") * low + lax.axis_index("low")
    me = jnp.stack([acq, tile]).astype(jnp.int32)
    kept, given = range_call(echo, slant, 0, 1, order, 2, early=True)
    came = lax.ppermute(given, "high", [(h, h ^ (FAR // 2)) for h in range(FAR)])
    (sent,) = range_call(echo, slant, 1, steps - 1, order, 2)
    array = turn(sent, axes)
    early = list(pair_call(kept, came))
    near = tiles // 2
    for s in range(1, tiles):
        flip = s // near * tiles + s % near
        early[s] = lax.ppermute(early[s], ("acq", "high", "low"), [(i, i ^ flip) for i in range(2 * tiles)])
    early = jnp.stack(early)
    looked = joint_call(me, same, array, early, angle, other_angle, azimuth_tables(angle.shape[0]), order)
    sources = [half * tiles + order.index(t) for t in range(tiles) for half in range(2)]
    result = place_call(turn(looked, axes), sources, columns // 2 // LOOK_RG, 2)
    return result.reshape(2, rounds, 1, -1, result.shape[1])


def separate(tiles, echo, slant, angle, pairs):
    columns = angle.shape[1]
    rounds = pairs.shape[0]
    (sent,) = range_call(echo, slant, 0, echo.shape[2] // SUB, list(range(tiles)), 1)
    mine = single_call(turn(sent, ("high", "low")), angle, azimuth_tables(angle.shape[0]))
    every = lax.all_gather(mine, "acq", axis=0)
    partner = lax.dynamic_index_in_dim(pairs, lax.axis_index("acq"), 1, keepdims=False)
    partners = [lax.dynamic_index_in_dim(every, partner[r], 0, keepdims=False) for r in range(rounds)]
    looked = turn(cross_call(mine, partners, tiles), ("high", "low"))
    result = place_call(looked, list(range(tiles)), columns // LOOK_RG, 1)
    return result.reshape(2, rounds, 1, -1, result.shape[1])


def shards(tiles, acqs, echo, slant, angle, pairs):
    fits = echo.shape[2] > SUB and tiles == FAR * FAR and angle.shape[2] % (6 * LANES) == 0 and AOI // LOOK_AZ % (tiles * SUB) == 0
    program = joint if acqs == 2 and fits else separate
    return program(tiles, echo, slant, angle[0], pairs)


def solution(mesh):
    acqs, tiles = mesh.shape["acq"], mesh.shape["tile"]
    low = 1 << (tiles.bit_length() // 2)
    low = low if tiles % low == 0 else 1
    split_mesh = jax.sharding.Mesh(mesh.devices.reshape(acqs, tiles // low, low), ("acq", "high", "low"))
    tile = ("high", "low")
    in_specs = (P(None, "acq", tile, None), P(None, "acq", None), P("acq", None, tile), P())
    out_specs = P(None, None, "acq", tile, None)
    body = functools.partial(shards, tiles, acqs)
    return jax.shard_map(body, mesh=split_mesh, in_specs=in_specs, out_specs=out_specs, check_vma=False)
```

```python
import functools
import math

import jax
import jax.numpy as jnp
import ml_dtypes
import numpy as np
from jax import lax
from jax.experimental import pallas as pl
from jax.experimental.pallas import tpu as pltpu
from jax.sharding import PartitionSpec as P

LOOK_AZ = 2
LOOK_RG = 8
AOI = 256
LANES = 128
SUB = 8
FAR = 4
SPARE = 32
USED = LANES - SPARE
CLASSES = 12
BATCH = 4
VMEM_LIMIT = 56 * 1024 * 1024


def high_low(table):
    high = table.astype(ml_dtypes.bfloat16)
    low = (table - high.astype(np.float64)).astype(ml_dtypes.bfloat16)
    return np.stack([high, low])


def trig(product, period):
    angle = (product % period) * (2.0 * math.pi / period)
    return np.cos(angle), np.sin(angle)


def split(value):
    high = value.astype(jnp.bfloat16)
    return high, (value - high.astype(jnp.float32)).astype(jnp.bfloat16)


def dot(left, right):
    return jnp.dot(left, right, preferred_element_type=jnp.float32)


def dot_stacked(table, value):
    high, low = split(value)
    both = dot(table, jnp.concatenate([high, low], axis=0))
    rows = table.shape[0] // 2
    return both[:rows] + both[rows:]


def dot_parts(table, value):
    rows = table.shape[0] // 2
    high, low = table[:rows], table[rows:]
    left = [jnp.concatenate(pair, axis=1) for pair in ((high, high), (low, jnp.zeros_like(low)))]
    return dot_stacked(jnp.concatenate(left, axis=0), value)


def thirds(a, b, c, sign):
    scale = sign * math.sqrt(3.0) / 2.0
    tr, ti = b[0] + c[0], b[1] + c[1]
    vr, vi = (b[0] - c[0]) * scale, (b[1] - c[1]) * scale
    ur, ui = a[0] - 0.5 * tr, a[1] - 0.5 * ti
    return (a[0] + tr, a[1] + ti), (ur - vi, ui + vr), (ur + vi, ui - vr)


def dot_table_right(value, table):
    rows = table.shape[0] // 2
    high_table, low_table = table[:rows], table[rows:]
    high, low = split(value)
    return dot(
        jnp.concatenate([high, low, high], axis=1),
        jnp.concatenate([high_table, high_table, low_table], axis=0),
    )


def stacked(table):
    high, low = high_low(table)
    return np.block([[high, high], [low, np.zeros_like(low)]])


def range_tables(length, order, halves):
    inner = LANES
    outer = length // inner
    part = outer // 3
    k1 = np.arange(outer)
    q = np.arange(inner)
    inside = np.arange(part)
    per_tile = outer // len(order)
    blocks = per_tile // halves
    a1, a4 = [], []
    for p0 in range(3):
        c, s = trig(np.outer(inside, 3 * inside + p0), outer)
        a1.append(stacked(np.block([[c, s], [-s, c]])))
        c, s = trig(np.outer(3 * inside + p0, inside), outer)
        rows = [
            cc * part + (t * per_tile + half * blocks) // 3 + b
            for cc in range(2)
            for half in range(halves)
            for t in order
            for b in range(blocks // 3)
        ]
        a4.append(stacked(np.block([[c, -s], [s, c]])[np.array(rows)] / length))
    c2, s2 = trig(np.outer(q, q), inner)
    b2 = np.block([[c2, -s2], [s2, c2]])
    ct, st = trig(np.outer(k1, q), length)
    twiddle = np.stack([ct, st]).astype(np.float32)
    b2 = np.concatenate(high_low(b2))
    return np.stack(a1), b2, np.stack(a4), twiddle


def spot(tile, low):
    return lax.rem(tile, low) * FAR + lax.div(tile, low)


def range_kernel(outer, early, x_ref, slant_ref, a1_ref, b2_ref, a4_ref, t_ref, *rest):
    outs, (rows_ref, h_ref), held = rest[: 1 + early], rest[1 + early : 3 + early], rest[3 + early :]
    part = outer // 3

    @pl.when(pl.program_id(0) == 0)
    def _():
        for c in range(2):
            for k2 in range(LANES):
                rows_ref[c, k2 : k2 + 1, :outer] = slant_ref[c, :, k2 * outer : (k2 + 1) * outer]
            h_ref[c] = rows_ref[c].T[:outer]

    rows = outs[0].shape[1] * outs[0].shape[3]
    turned = held[0] if early else outs[0].reshape(outs[0].shape[0] * rows, LANES)
    ct, st = t_ref[0], t_ref[1]
    hr, hi = h_ref[0], h_ref[1]

    def batch(first):
        lines = range(first, first + BATCH)
        y = []
        for p0 in range(3):
            x = [
                jnp.concatenate(
                    [x_ref[c, 0, pl.ds(p0 * SUB + l, part, stride=3 * SUB), :] for c in range(2)], axis=0
                )
                for l in lines
            ]
            value = dot_stacked(a1_ref[p0], jnp.concatenate(x, axis=1))
            y.append((value[:part], value[part:]))
        yield
        y = thirds(*y, -1.0)
        z = []
        for b in range(BATCH):
            yr, yi = [
                jnp.concatenate([v[c][:, b * LANES : (b + 1) * LANES] for v in y], axis=0) for c in range(2)
            ]
            z.append(jnp.concatenate([yr * ct + yi * st, yi * ct - yr * st], axis=1))
        y = dot_table_right(jnp.concatenate(z, axis=0), b2_ref[...])
        yield
        z = []
        for b in range(BATCH):
            yr = y[b * outer : (b + 1) * outer, :LANES]
            yi = y[b * outer : (b + 1) * outer, LANES:]
            z.append(jnp.concatenate([yr * hr - yi * hi, -yr * hi - yi * hr], axis=1))
        y = dot_table_right(jnp.concatenate(z, axis=0), b2_ref[...])
        yield
        z = []
        for b in range(BATCH):
            yr = y[b * outer : (b + 1) * outer, :LANES]
            yi = y[b * outer : (b + 1) * outer, LANES:]
            zr, zi = yr * ct + yi * st, yr * st - yi * ct
            z.append(thirds(*[(zr[k * part : (k + 1) * part], zi[k * part : (k + 1) * part]) for k in range(3)], 1.0))
        y = []
        for p0 in range(3):
            value = jnp.concatenate([jnp.concatenate(z[b][p0], axis=0) for b in range(BATCH)], axis=1)
            y.append(dot_stacked(a4_ref[p0], value))
        yield
        for p0 in range(3):
            for b, l in enumerate(lines):
                for c in range(2):
                    turned[pl.ds((2 * p0 + c) * SUB + l, part, stride=6 * SUB), :] = y[p0][
                        c * part : (c + 1) * part, b * LANES : (b + 1) * LANES
                    ]
        yield

    batches = [batch(first) for first in range(0, SUB, BATCH)]
    for _ in range(5):
        for work in batches:
            next(work)
    if not early:
        return
    near = outs[0].shape[0] // 2
    acq = lax.axis_index("acq")
    place = lax.axis_index("high") * (2 * near // FAR) + lax.axis_index("low")
    for k, out in enumerate(outs):
        for s in range(2 * near):
            tile = jnp.bitwise_xor(place, s % near + k * near)
            dest = jnp.bitwise_xor(acq, s // near) * 2 * near + spot(tile, 2 * near // FAR)
            value = turned[pl.ds(pl.multiple_of(dest * rows, SUB), rows), :]
            out[s, :, 0] = value.reshape(out.shape[1], out.shape[3], LANES)


def range_call(echo, slant, first, steps, order, halves, early=False):
    length = echo.shape[3]
    outer = length // LANES
    view = echo.reshape(2, -1, SUB, outer, LANES).transpose(0, 1, 3, 2, 4).reshape(2, -1, outer * SUB, LANES)
    tables = [slant, *range_tables(length, order, halves)]
    dests = len(order) * halves
    blocks = outer // dests
    rows = 2 * blocks * SUB
    whole = lambda shape: pl.BlockSpec(shape, lambda s: (0,) * len(shape))
    macs = steps * SUB * length * 2 * (2 * outer + 2 * LANES) * 2 * 3
    outs = 1 + early
    return pl.pallas_call(
        functools.partial(range_kernel, outer, early),
        grid=(steps,),
        in_specs=[pl.BlockSpec((2, 1, outer * SUB, LANES), lambda s: (0, first + s, 0, 0))]
        + [whole(t.shape) for t in tables],
        out_specs=[pl.BlockSpec((dests // outs, blocks, 1, 2 * SUB, LANES), lambda s: (0, 0, s, 0, 0))] * outs,
        scratch_shapes=[
            pltpu.VMEM((2, LANES, LANES), jnp.float32),
            pltpu.VMEM((2, outer, LANES), jnp.float32),
        ]
        + [pltpu.VMEM((dests * rows, LANES), jnp.float32)] * early,
        out_shape=[jax.ShapeDtypeStruct((dests // outs, blocks, steps, 2 * SUB, LANES), jnp.float32)] * outs,
        compiler_params=pltpu.CompilerParams(vmem_limit_bytes=VMEM_LIMIT),
        cost_estimate=pl.CostEstimate(
            flops=2 * macs, bytes_accessed=16 * steps * SUB * length, transcendentals=0
        ),
        name=f"range_compress_{first}",
    )(view, *[jnp.asarray(t) for t in tables])


def pair_kernel(kept_ref, came_ref, *outs):
    for s, out in enumerate(outs):
        out[0] = kept_ref[s, :, 0]
        out[1] = came_ref[s, :, 0]


def pair_call(kept, came):
    count, blocks, _, rows, _ = kept.shape
    vmem = pl.BlockSpec(memory_space=pltpu.VMEM)
    return pl.pallas_call(
        pair_kernel,
        in_specs=[vmem] * 2,
        out_specs=[vmem] * count,
        out_shape=[jax.ShapeDtypeStruct((2, blocks, rows, LANES), jnp.float32)] * count,
        compiler_params=pltpu.CompilerParams(vmem_limit_bytes=VMEM_LIMIT),
        cost_estimate=pl.CostEstimate(flops=10**12, bytes_accessed=4 * kept.size, transcendentals=0),
        name="pair_halves",
    )(kept, came)


def azimuth_tables(length):
    part = length // CLASSES
    f1 = np.arange(part)
    ahead, back = [], []
    first = (length - AOI) // 2
    u, s = np.arange(part // LOOK_AZ), np.arange(LOOK_AZ)
    lines = (first + u[None, :] * LOOK_AZ + s[:, None]).reshape(-1)
    for f0 in range(CLASSES):
        c, s = trig(np.outer(CLASSES * f1 + f0, np.arange(part)), length)
        ahead.append(np.concatenate(high_low(np.block([[c, s], [-s, c]]))))
        c, s = trig(np.outer(lines, CLASSES * f1 + f0), length)
        back.append(np.concatenate(high_low(np.block([[c, -s], [s, c]]) / length)))
    return [np.stack(ahead), np.stack(back)]


def cos_sin(angle):
    y = 0.5 * angle
    z = y * y
    sine = [1.0, -1 / 6, 1 / 120, -1 / 5040, 1 / 362880, -1 / 39916800]
    cosine = [1.0, -1 / 2, 1 / 24, -1 / 720, 1 / 40320, -1 / 3628800, 1 / 479001600]
    s, c = sine[-1], cosine[-1]
    for k in sine[-2::-1]:
        s = s * z + k
    for k in cosine[-2::-1]:
        c = c * z + k
    s = s * y
    return 1.0 - 2.0 * (s * s), 2.0 * (s * c)


def fours(a, b, c, d):
    (ar, ai), (br, bi), (cr, ci), (dr, di) = a, b, c, d
    pr, pi, mr, mi = ar + cr, ai + ci, ar - cr, ai - ci
    qr, qi, nr, ni = br + dr, bi + di, br - dr, bi - di
    return (pr + qr, pi + qi), (mr + ni, mi - nr), (pr - qr, pi - qi), (mr - ni, mi + nr)


def class_of(e, g):
    return (4 * e + 9 * g) % CLASSES


def focus(xr, xi, phases, tables):
    fw, bw = tables
    part = xr.shape[0] // CLASSES
    x = [(xr[k * part : (k + 1) * part], xi[k * part : (k + 1) * part]) for k in range(CLASSES)]
    columns = [thirds(*[x[(4 * i + 3 * j) % CLASSES] for i in range(3)], -1.0) for j in range(4)]
    classes = [None] * CLASSES
    for e in range(3):
        for g, pair in enumerate(fours(*[columns[j][e] for j in range(4)])):
            classes[class_of(e, g)] = pair
    z, forward = [], []
    for f0 in range(CLASSES + 1):
        if f0 < CLASSES:
            forward.append(dot_parts(fw[f0], jnp.concatenate(classes[f0], axis=0)))
        if f0 > 0:
            y, k = forward[f0 - 1], f0 - 1
            dr, di = y[:part], y[part:]
            pc, ps = phases(k)
            e = jnp.concatenate([dr * pc - di * ps, dr * ps + di * pc], axis=0)
            y = dot_parts(bw[k], e)
            z.append((y[:part], y[part:]))
    sums = [fours(*[z[class_of(e, g)] for g in range(4)]) for e in range(3)]
    outs = []
    for h in range(AOI // part):
        terms = [sums[e][h] for e in range(3)]
        outs.append(thirds(*terms, 1.0)[h % 3])
    return [jnp.concatenate([pair[c] for pair in outs], axis=0) for c in range(2)]


def looked_at(field, look):
    lines = AOI // 4 // LOOK_AZ
    groups = [field[k * lines : (k + 1) * lines] for k in range(AOI // lines)]
    added = [groups[k] + groups[k + 1] for k in range(0, len(groups), LOOK_AZ)]
    high, low = split(jnp.concatenate(added, axis=0))
    return dot(high, look) + dot(low, look)


def joint_kernel(order, rounds, me_ref, same_ref, x_ref, early_ref, own_angle, other_angle, fw, bw, look_ref, out, stage, looked):
    acq = me_ref[0]
    tiles = len(order)
    near = tiles // 2
    firsts = [acq * tiles, (1 - acq) * tiles]
    for part in range(2):
        for k, first in enumerate(firsts):
            lanes = slice(k * LANES, (k + 1) * LANES)
            for place, t in enumerate(order):
                stage[part, t, 1:, :, lanes] = x_ref[first + place, 0, :, part * SUB : (part + 1) * SUB, :]
            for s in range(near):
                for side in range(2):
                    tile = jnp.bitwise_xor(me_ref[1], s + side * near)
                    stage[part, tile, 0, :, lanes] = early_ref[k * near + s, side, 0, part * SUB : (part + 1) * SUB, :]
    xr, xi = [stage[part].reshape(-1, 2 * LANES) for part in range(2)]
    rows_of = lambda k: pl.ds(k, own_angle.shape[0] // CLASSES, stride=CLASSES)
    phases = lambda k: cos_sin(jnp.concatenate([a[rows_of(k), :] for a in (own_angle, other_angle)], axis=1))
    fr, fi = focus(xr, xi, phases, [fw, bw])
    mr, mi, pr, pi = fr[:, :LANES], fi[:, :LANES], fr[:, LANES:], fi[:, LANES:]
    look = look_ref[0]
    cross_real = looked_at(mr * pr + mi * pi, look[0])
    cross_imag = looked_at(mi * pr - mr * pi, look[1])
    own_real = looked_at(mr * mr + mi * mi, look[0])
    own_imag = looked_at(mi * mr - mr * mi, look[1])
    other_real = looked_at(pr * pr + pi * pi, look[0])
    other_imag = looked_at(pi * pr - pr * pi, look[1])
    block = pl.program_id(0)

    @pl.when(block == 0)
    def _():
        looked[...] = jnp.zeros_like(looked)

    for r in range(rounds):
        same = same_ref[r] != 0
        looked[0, r] += jnp.where(same, own_real + own_imag, cross_real + cross_imag)
        looked[1, r] += jnp.where(same, other_real + other_imag, cross_real - cross_imag)

    @pl.when(block == pl.num_programs(0) - 1)
    def _():
        for k, first in enumerate(firsts):
            groups = pack(looked[k, 0], looked[k, 1])
            for place, t in enumerate(order):
                for j, (value, at) in enumerate(groups):
                    out[first + place, j] = value[t * SUB + at : t * SUB + at + SUB // 2]


def pack(even, odd):
    half = SUB // 2
    free = lax.broadcasted_iota(jnp.int32, even.shape, 1) >= USED
    rest = [pltpu.roll(odd, (USED - SPARE * j) % LANES, 1) for j in range(3)]
    up = lambda value: pltpu.roll(value, value.shape[0] - half, 0)
    return (
        (jnp.where(free, up(rest[0]), even), 0),
        (jnp.where(free, rest[1], even), half),
        (jnp.where(free, up(rest[2]), odd), 0),
    )


def unpack(parts):
    lane = lax.broadcasted_iota(jnp.int32, parts[0].shape, 1)
    rest = [pltpu.roll(part, (SPARE * j - USED) % LANES, 1) for j, part in enumerate(parts)]
    last = jnp.where(lane < SPARE, rest[0], jnp.where(lane < 2 * SPARE, rest[1], rest[2]))
    return jnp.concatenate([parts[0], parts[1], parts[2], last], axis=0)


def joint_call(me, same, array, early, angle, other_angle, tables, order):
    dests, blocks, steps = array.shape[:3]
    tiles = len(order)
    lines = angle.shape[0]
    rounds = same.shape[0]
    wide = blocks * LANES // LOOK_RG
    look = np.stack(
        [
            np.stack([look_table(LANES, c * wide + b * LANES // LOOK_RG) for c in range(2)])
            for b in range(blocks)
        ]
    )
    return pl.pallas_call(
        functools.partial(joint_kernel, order, rounds),
        grid_spec=pltpu.PrefetchScalarGridSpec(
            num_scalar_prefetch=2,
            grid=(blocks,),
            in_specs=[
                pl.BlockSpec((dests, 1) + array.shape[2:], lambda b, me, same: (0, b, 0, 0, 0)),
                pl.BlockSpec(early.shape[:2] + (1,) + early.shape[3:], lambda b, me, same: (0, 0, b, 0, 0)),
                pl.BlockSpec((lines, LANES), lambda b, me, same: (0, me[0] * blocks + b)),
                pl.BlockSpec((lines, LANES), lambda b, me, same: (0, b)),
                *[pl.BlockSpec(t.shape, lambda b, me, same: (0, 0, 0)) for t in tables],
                pl.BlockSpec((1,) + look.shape[1:], lambda b, me, same: (b, 0, 0, 0)),
            ],
            out_specs=pl.BlockSpec((dests, 3, SUB // 2, LANES), lambda b, me, same: (0, 0, 0, 0)),
            scratch_shapes=[
                pltpu.VMEM((2, tiles, steps + 1, SUB, 2 * LANES), jnp.float32),
                pltpu.VMEM((2, rounds, AOI // LOOK_AZ, LANES), jnp.float32),
            ],
        ),
        out_shape=jax.ShapeDtypeStruct((dests, 3, SUB // 2, LANES), jnp.float32),
        compiler_params=pltpu.CompilerParams(vmem_limit_bytes=VMEM_LIMIT),
        cost_estimate=pl.CostEstimate(
            flops=2 * 2 * 3 * 6 * 256 * 256 * 2 * LANES * blocks,
            bytes_accessed=20 * lines * 2 * LANES * blocks,
            transcendentals=0,
        ),
        name="azimuth_interferogram",
    )(me, same, array, early, angle, other_angle, *[jnp.asarray(t) for t in tables], jnp.asarray(look))


def single_kernel(tiles, x_ref, angle_ref, fw, bw, out):
    xr, xi = [x_ref[:, 0, :, part * SUB : (part + 1) * SUB, :].reshape(-1, LANES) for part in range(2)]
    fr, fi = focus(xr, xi, lambda k: cos_sin(angle_ref[pl.ds(k, angle_ref.shape[0] // CLASSES, stride=CLASSES), :]), [fw, bw])
    out[:AOI] = fr
    out[AOI:] = fi


def single_call(array, angle, tables):
    tiles = array.shape[0]
    lines, columns = angle.shape
    return pl.pallas_call(
        functools.partial(single_kernel, tiles),
        grid=(columns // LANES,),
        in_specs=[
            pl.BlockSpec((tiles, 1) + array.shape[2:], lambda b: (0, b, 0, 0, 0)),
            pl.BlockSpec((lines, LANES), lambda b: (0, b)),
        ]
        + [pl.BlockSpec(t.shape, lambda b: (0, 0, 0)) for t in tables],
        out_specs=pl.BlockSpec((2 * AOI, LANES), lambda b: (0, b)),
        out_shape=jax.ShapeDtypeStruct((2 * AOI, columns), jnp.float32),
        compiler_params=pltpu.CompilerParams(vmem_limit_bytes=VMEM_LIMIT),
        name="azimuth_focus",
    )(array, angle, *[jnp.asarray(t) for t in tables])


def look_table(width, offset):
    table = np.zeros((width, LANES), np.float64)
    table[np.arange(width), offset + np.arange(width) // LOOK_RG] = 1.0 / (LOOK_AZ * LOOK_RG)
    return table.astype(ml_dtypes.bfloat16)


def cross_kernel(rounds, tiles, mine_ref, *refs):
    partner_refs, look_ref, out = refs[:rounds], refs[-2], refs[-1]
    mr, mi = mine_ref[:AOI], mine_ref[AOI:]
    per = AOI // LOOK_AZ // tiles
    for r in range(rounds):
        pr, pi = partner_refs[r][:AOI], partner_refs[r][AOI:]
        for c, field in enumerate((mr * pr + mi * pi, mi * pr - mr * pi)):
            looked = looked_at(field, look_ref[...])
            at = (c * rounds + r) * per
            for t in range(tiles):
                out[t, at : at + per, :] = looked[t * per : (t + 1) * per]


def cross_call(mine, partners, tiles):
    rounds = len(partners)
    width = mine.shape[1]
    look = jnp.asarray(look_table(width, 0))
    shape = (tiles, 2 * rounds * (AOI // LOOK_AZ // tiles), LANES)
    vmem = lambda: pl.BlockSpec(memory_space=pltpu.VMEM)
    return pl.pallas_call(
        functools.partial(cross_kernel, rounds, tiles),
        in_specs=[vmem() for _ in range(rounds + 2)],
        out_specs=vmem(),
        out_shape=jax.ShapeDtypeStruct(shape, jnp.float32),
        compiler_params=pltpu.CompilerParams(vmem_limit_bytes=VMEM_LIMIT),
        name="interferogram",
    )(mine, *partners, look)


def place_kernel(sources, valid, parts, in_ref, out):
    if in_ref.shape[1:] == (3, SUB // 2, LANES):
        values = {k: unpack([in_ref[k, j] for j in range(3)]) for k in sources}
    else:
        values = {k: in_ref[k] for k in sources}
    rows = values[sources[0]].shape[0]
    lane = lax.broadcasted_iota(jnp.int32, (rows, LANES), 1)
    for c in range(parts):
        for o in range(len(sources) * valid // LANES):
            acc = None
            for place, source in enumerate(sources):
                shift = place * valid - o * LANES
                if shift + valid <= 0 or shift >= LANES:
                    continue
                value = values[source]
                turn_by = (shift - c * valid) % LANES
                if turn_by:
                    value = pltpu.roll(value, turn_by, 1)
                acc = value if acc is None else jnp.where(lane >= shift, value, acc)
            out[c * rows : (c + 1) * rows, o * LANES : (o + 1) * LANES] = acc


def place_call(received, rows, sources, valid, parts):
    return pl.pallas_call(
        functools.partial(place_kernel, sources, valid, parts),
        in_specs=[pl.BlockSpec(memory_space=pltpu.VMEM)],
        out_specs=pl.BlockSpec(memory_space=pltpu.VMEM),
        out_shape=jax.ShapeDtypeStruct((parts * rows, len(sources) * valid), jnp.float32),
        compiler_params=pltpu.CompilerParams(vmem_limit_bytes=VMEM_LIMIT),
        name="place_samples",
    )(received)


def turn(array, axes):
    return lax.all_to_all(array, axes, split_axis=0, concat_axis=0, tiled=True)


def joint(tiles, echo, slant, angle, pairs):
    steps = echo.shape[2] // SUB
    columns = angle.shape[1]
    rounds = pairs.shape[0]
    acq = lax.axis_index("acq")
    same = (lax.dynamic_index_in_dim(pairs, acq, 1, keepdims=False) == acq).astype(jnp.int32)
    theirs = lax.dynamic_slice_in_dim(angle, (1 - acq) * (columns // 2), columns // 2, 1)
    other_angle = lax.ppermute(theirs, "acq", [(0, 1), (1, 0)])
    low = lax.axis_size("low")
    order = [h * low + k for k in range(low) for h in range(tiles // low)]
    axes = ("acq", "low", "high")
    tile = lax.axis_index("high") * low + lax.axis_index("low")
    me = jnp.stack([acq, tile]).astype(jnp.int32)
    kept, given = range_call(echo, slant, 0, 1, order, 2, early=True)
    came = lax.ppermute(given, "high", [(h, h ^ (FAR // 2)) for h in range(FAR)])
    (sent,) = range_call(echo, slant, 1, steps - 1, order, 2)
    array = turn(sent, axes)
    early = list(pair_call(kept, came))
    near = tiles // 2
    for s in range(1, tiles):
        flip = s // near * tiles + s % near
        early[s] = lax.ppermute(early[s], ("acq", "high", "low"), [(i, i ^ flip) for i in range(2 * tiles)])
    early = jnp.stack(early)
    looked = joint_call(me, same, array, early, angle, other_angle, azimuth_tables(angle.shape[0]), order)
    sources = [half * tiles + order.index(t) for t in range(tiles) for half in range(2)]
    result = place_call(turn(looked, axes), rounds * SUB, sources, columns // 2 // LOOK_RG, 2)
    return result.reshape(2, rounds, 1, -1, result.shape[1])


def separate(tiles, echo, slant, angle, pairs):
    columns = angle.shape[1]
    rounds = pairs.shape[0]
    (sent,) = range_call(echo, slant, 0, echo.shape[2] // SUB, list(range(tiles)), 1)
    mine = single_call(turn(sent, ("high", "low")), angle, azimuth_tables(angle.shape[0]))
    every = lax.all_gather(mine, "acq", axis=0)
    partner = lax.dynamic_index_in_dim(pairs, lax.axis_index("acq"), 1, keepdims=False)
    partners = [lax.dynamic_index_in_dim(every, partner[r], 0, keepdims=False) for r in range(rounds)]
    looked = turn(cross_call(mine, partners, tiles), ("high", "low"))
    result = place_call(looked, looked.shape[1], list(range(tiles)), columns // LOOK_RG, 1)
    return result.reshape(2, rounds, 1, -1, result.shape[1])


def shards(tiles, acqs, echo, slant, angle, pairs):
    fits = echo.shape[2] > SUB and tiles == FAR * FAR and AOI // LOOK_AZ == tiles * SUB
    fits = fits and angle.shape[2] // LOOK_RG == USED and pairs.shape[0] == 2
    program = joint if acqs == 2 and fits else separate
    return program(tiles, echo, slant, angle[0], pairs)


def solution(mesh):
    acqs, tiles = mesh.shape["acq"], mesh.shape["tile"]
    low = 1 << (tiles.bit_length() // 2)
    low = low if tiles % low == 0 else 1
    split_mesh = jax.sharding.Mesh(mesh.devices.reshape(acqs, tiles // low, low), ("acq", "high", "low"))
    tile = ("high", "low")
    in_specs = (P(None, "acq", tile, None), P(None, "acq", None), P("acq", None, tile), P())
    out_specs = P(None, None, "acq", tile, None)
    body = functools.partial(shards, tiles, acqs)
    return jax.shard_map(body, mesh=split_mesh, in_specs=in_specs, out_specs=out_specs, check_vma=False)
```

```python
import functools
import math

import jax
import jax.numpy as jnp
import ml_dtypes
import numpy as np
from jax import lax
from jax.experimental import pallas as pl
from jax.experimental.pallas import tpu as pltpu
from jax.sharding import PartitionSpec as P

LOOK_AZ = 2
LOOK_RG = 8
AOI = 256
LANES = 128
SUB = 8
FAR = 4
SPARE = 32
USED = LANES - SPARE
CLASSES = 12
BATCH = 4
VMEM_LIMIT = 56 * 1024 * 1024


def high_low(table):
    high = table.astype(ml_dtypes.bfloat16)
    low = (table - high.astype(np.float64)).astype(ml_dtypes.bfloat16)
    return np.stack([high, low])


def trig(product, period):
    angle = (product % period) * (2.0 * math.pi / period)
    return np.cos(angle), np.sin(angle)


def split(value):
    high = value.astype(jnp.bfloat16)
    return high, (value - high.astype(jnp.float32)).astype(jnp.bfloat16)


def dot(left, right):
    return jnp.dot(left, right, preferred_element_type=jnp.float32)


def dot_stacked(table, value):
    high, low = split(value)
    both = dot(table, jnp.concatenate([high, low], axis=0))
    rows = table.shape[0] // 2
    return both[:rows] + both[rows:]


def dot_parts(table, value):
    rows = table.shape[0] // 2
    high, low = table[:rows], table[rows:]
    left = [jnp.concatenate(pair, axis=1) for pair in ((high, high), (low, jnp.zeros_like(low)))]
    return dot_stacked(jnp.concatenate(left, axis=0), value)


def thirds(a, b, c, sign):
    scale = sign * math.sqrt(3.0) / 2.0
    tr, ti = b[0] + c[0], b[1] + c[1]
    vr, vi = (b[0] - c[0]) * scale, (b[1] - c[1]) * scale
    ur, ui = a[0] - 0.5 * tr, a[1] - 0.5 * ti
    return (a[0] + tr, a[1] + ti), (ur - vi, ui + vr), (ur + vi, ui - vr)


def dot_table_right(value, table):
    rows = table.shape[0] // 2
    high_table, low_table = table[:rows], table[rows:]
    high, low = split(value)
    return dot(
        jnp.concatenate([high, low, high], axis=1),
        jnp.concatenate([high_table, high_table, low_table], axis=0),
    )


def stacked(table):
    high, low = high_low(table)
    return np.block([[high, high], [low, np.zeros_like(low)]])


def range_tables(length, order, halves):
    inner = LANES
    outer = length // inner
    part = outer // 3
    k1 = np.arange(outer)
    q = np.arange(inner)
    inside = np.arange(part)
    per_tile = outer // len(order)
    blocks = per_tile // halves
    a1, a4 = [], []
    for p0 in range(3):
        c, s = trig(np.outer(inside, 3 * inside + p0), outer)
        a1.append(stacked(np.block([[c, s], [-s, c]])))
        c, s = trig(np.outer(3 * inside + p0, inside), outer)
        rows = [
            cc * part + (t * per_tile + half * blocks) // 3 + b
            for cc in range(2)
            for half in range(halves)
            for t in order
            for b in range(blocks // 3)
        ]
        a4.append(stacked(np.block([[c, -s], [s, c]])[np.array(rows)] / length))
    c2, s2 = trig(np.outer(q, q), inner)
    b2 = np.block([[c2, -s2], [s2, c2]])
    ct, st = trig(np.outer(k1, q), length)
    twiddle = np.stack([ct, st]).astype(np.float32)
    b2 = np.concatenate(high_low(b2))
    return np.stack(a1), b2, np.stack(a4), twiddle


def spot(tile, low):
    return lax.rem(tile, low) * FAR + lax.div(tile, low)


def range_kernel(outer, early, x_ref, slant_ref, a1_ref, b2_ref, a4_ref, t_ref, *rest):
    outs, (rows_ref, h_ref), held = rest[: 1 + early], rest[1 + early : 3 + early], rest[3 + early :]
    part = outer // 3

    @pl.when(pl.program_id(0) == 0)
    def _():
        for c in range(2):
            for k2 in range(LANES):
                rows_ref[c, k2 : k2 + 1, :outer] = slant_ref[c, :, k2 * outer : (k2 + 1) * outer]
            h_ref[c] = rows_ref[c].T[:outer]

    rows = outs[0].shape[1] * outs[0].shape[3]
    turned = held[0] if early else outs[0].reshape(outs[0].shape[0] * rows, LANES)
    ct, st = t_ref[0], t_ref[1]
    hr, hi = h_ref[0], h_ref[1]

    def batch(first):
        lines = range(first, first + BATCH)
        y = []
        for p0 in range(3):
            x = [
                jnp.concatenate(
                    [x_ref[c, 0, pl.ds(p0 * SUB + l, part, stride=3 * SUB), :] for c in range(2)], axis=0
                )
                for l in lines
            ]
            value = dot_stacked(a1_ref[p0], jnp.concatenate(x, axis=1))
            y.append((value[:part], value[part:]))
        yield
        y = thirds(*y, -1.0)
        z = []
        for b in range(BATCH):
            yr, yi = [
                jnp.concatenate([v[c][:, b * LANES : (b + 1) * LANES] for v in y], axis=0) for c in range(2)
            ]
            z.append(jnp.concatenate([yr * ct + yi * st, yi * ct - yr * st], axis=1))
        y = dot_table_right(jnp.concatenate(z, axis=0), b2_ref[...])
        yield
        z = []
        for b in range(BATCH):
            yr = y[b * outer : (b + 1) * outer, :LANES]
            yi = y[b * outer : (b + 1) * outer, LANES:]
            z.append(jnp.concatenate([yr * hr - yi * hi, -yr * hi - yi * hr], axis=1))
        y = dot_table_right(jnp.concatenate(z, axis=0), b2_ref[...])
        yield
        z = []
        for b in range(BATCH):
            yr = y[b * outer : (b + 1) * outer, :LANES]
            yi = y[b * outer : (b + 1) * outer, LANES:]
            zr, zi = yr * ct + yi * st, yr * st - yi * ct
            z.append(thirds(*[(zr[k * part : (k + 1) * part], zi[k * part : (k + 1) * part]) for k in range(3)], 1.0))
        y = []
        for p0 in range(3):
            value = jnp.concatenate([jnp.concatenate(z[b][p0], axis=0) for b in range(BATCH)], axis=1)
            y.append(dot_stacked(a4_ref[p0], value))
        yield
        for p0 in range(3):
            for b, l in enumerate(lines):
                for c in range(2):
                    turned[pl.ds((2 * p0 + c) * SUB + l, part, stride=6 * SUB), :] = y[p0][
                        c * part : (c + 1) * part, b * LANES : (b + 1) * LANES
                    ]
        yield

    batches = [batch(first) for first in range(0, SUB, BATCH)]
    for _ in range(5):
        for work in batches:
            next(work)
    if not early:
        return
    near = outs[0].shape[0] // 2
    acq = lax.axis_index("acq")
    place = lax.axis_index("high") * (2 * near // FAR) + lax.axis_index("low")
    for k, out in enumerate(outs):
        for s in range(2 * near):
            tile = jnp.bitwise_xor(place, s % near + k * near)
            dest = jnp.bitwise_xor(acq, s // near) * 2 * near + spot(tile, 2 * near // FAR)
            value = turned[pl.ds(pl.multiple_of(dest * rows, SUB), rows), :]
            out[s, :, 0] = value.reshape(out.shape[1], out.shape[3], LANES)


def range_call(echo, slant, first, steps, order, halves, early=False):
    length = echo.shape[3]
    outer = length // LANES
    view = echo.reshape(2, -1, SUB, outer, LANES).transpose(0, 1, 3, 2, 4).reshape(2, -1, outer * SUB, LANES)
    tables = [slant, *range_tables(length, order, halves)]
    dests = len(order) * halves
    blocks = outer // dests
    rows = 2 * blocks * SUB
    whole = lambda shape: pl.BlockSpec(shape, lambda s: (0,) * len(shape))
    macs = steps * SUB * length * 2 * (2 * outer + 2 * LANES) * 2 * 3
    outs = 1 + early
    return pl.pallas_call(
        functools.partial(range_kernel, outer, early),
        grid=(steps,),
        in_specs=[pl.BlockSpec((2, 1, outer * SUB, LANES), lambda s: (0, first + s, 0, 0))]
        + [whole(t.shape) for t in tables],
        out_specs=[pl.BlockSpec((dests // outs, blocks, 1, 2 * SUB, LANES), lambda s: (0, 0, s, 0, 0))] * outs,
        scratch_shapes=[
            pltpu.VMEM((2, LANES, LANES), jnp.float32),
            pltpu.VMEM((2, outer, LANES), jnp.float32),
        ]
        + [pltpu.VMEM((dests * rows, LANES), jnp.float32)] * early,
        out_shape=[jax.ShapeDtypeStruct((dests // outs, blocks, steps, 2 * SUB, LANES), jnp.float32)] * outs,
        compiler_params=pltpu.CompilerParams(vmem_limit_bytes=VMEM_LIMIT),
        cost_estimate=pl.CostEstimate(
            flops=2 * macs, bytes_accessed=16 * steps * SUB * length, transcendentals=0
        ),
        name=f"range_compress_{first}",
    )(view, *[jnp.asarray(t) for t in tables])


def pair_kernel(kept_ref, came_ref, *outs):
    for s, out in enumerate(outs):
        out[0] = kept_ref[s, :, 0]
        out[1] = came_ref[s, :, 0]


def pair_call(kept, came):
    count, blocks, _, rows, _ = kept.shape
    vmem = pl.BlockSpec(memory_space=pltpu.VMEM)
    return pl.pallas_call(
        pair_kernel,
        in_specs=[vmem] * 2,
        out_specs=[vmem] * count,
        out_shape=[jax.ShapeDtypeStruct((2, blocks, rows, LANES), jnp.float32)] * count,
        compiler_params=pltpu.CompilerParams(vmem_limit_bytes=VMEM_LIMIT),
        cost_estimate=pl.CostEstimate(flops=10**12, bytes_accessed=4 * kept.size, transcendentals=0),
        name="pair_halves",
    )(kept, came)


def azimuth_tables(length):
    part = length // CLASSES
    f1 = np.arange(part)
    ahead, back = [], []
    first = (length - AOI) // 2
    u, s = np.arange(part // LOOK_AZ), np.arange(LOOK_AZ)
    lines = (first + u[None, :] * LOOK_AZ + s[:, None]).reshape(-1)
    for f0 in range(CLASSES):
        c, s = trig(np.outer(CLASSES * f1 + f0, np.arange(part)), length)
        ahead.append(np.concatenate(high_low(np.block([[c, s], [-s, c]]))))
        c, s = trig(np.outer(lines, CLASSES * f1 + f0), length)
        back.append(np.concatenate(high_low(np.block([[c, -s], [s, c]]) / length)))
    return [np.stack(ahead), np.stack(back)]


def cos_sin(angle):
    y = 0.5 * angle
    z = y * y
    sine = [1.0, -1 / 6, 1 / 120, -1 / 5040, 1 / 362880, -1 / 39916800]
    cosine = [1.0, -1 / 2, 1 / 24, -1 / 720, 1 / 40320, -1 / 3628800, 1 / 479001600]
    s, c = sine[-1], cosine[-1]
    for k in sine[-2::-1]:
        s = s * z + k
    for k in cosine[-2::-1]:
        c = c * z + k
    s = s * y
    return 1.0 - 2.0 * (s * s), 2.0 * (s * c)


def fours(a, b, c, d):
    (ar, ai), (br, bi), (cr, ci), (dr, di) = a, b, c, d
    pr, pi, mr, mi = ar + cr, ai + ci, ar - cr, ai - ci
    qr, qi, nr, ni = br + dr, bi + di, br - dr, bi - di
    return (pr + qr, pi + qi), (mr + ni, mi - nr), (pr - qr, pi - qi), (mr - ni, mi + nr)


def class_of(e, g):
    return (4 * e + 9 * g) % CLASSES


def focus(xr, xi, phases, tables):
    fw, bw = tables
    part = xr.shape[0] // CLASSES
    x = [(xr[k * part : (k + 1) * part], xi[k * part : (k + 1) * part]) for k in range(CLASSES)]
    columns = [thirds(*[x[(4 * i + 3 * j) % CLASSES] for i in range(3)], -1.0) for j in range(4)]
    classes = [None] * CLASSES
    for e in range(3):
        for g, pair in enumerate(fours(*[columns[j][e] for j in range(4)])):
            classes[class_of(e, g)] = pair
    z, forward = [], []
    for f0 in range(CLASSES + 1):
        if f0 < CLASSES:
            forward.append(dot_parts(fw[f0], jnp.concatenate(classes[f0], axis=0)))
        if f0 > 0:
            y, k = forward[f0 - 1], f0 - 1
            dr, di = y[:part], y[part:]
            pc, ps = phases(k)
            e = jnp.concatenate([dr * pc - di * ps, dr * ps + di * pc], axis=0)
            y = dot_parts(bw[k], e)
            z.append((y[:part], y[part:]))
    sums = [fours(*[z[class_of(e, g)] for g in range(4)]) for e in range(3)]
    outs = []
    for h in range(AOI // part):
        terms = [sums[e][h] for e in range(3)]
        outs.append(thirds(*terms, 1.0)[h % 3])
    return [jnp.concatenate([pair[c] for pair in outs], axis=0) for c in range(2)]


def looked_at(fields, look):
    lines = AOI // 4 // LOOK_AZ
    added = []
    for field in fields:
        groups = [field[k * lines : (k + 1) * lines] for k in range(AOI // lines)]
        added += [groups[k] + groups[k + 1] for k in range(0, len(groups), LOOK_AZ)]
    high, low = split(jnp.concatenate(added, axis=0))
    looked = dot(high, look) + dot(low, look)
    rows = AOI // LOOK_AZ
    return [looked[k * rows : (k + 1) * rows] for k in range(len(fields))]


def joint_kernel(order, rounds, me_ref, same_ref, x_ref, early_ref, own_angle, other_angle, fw, bw, look_ref, out, looked):
    acq = me_ref[0]
    tiles = len(order)
    near = tiles // 2
    firsts = [acq * tiles, (1 - acq) * tiles]
    steps = x_ref.shape[2] + 1
    places = [jnp.bitwise_xor(me_ref[1], t) for t in range(tiles)]

    def piece(k, t, step, part):
        rows = slice(part * SUB, (part + 1) * SUB)
        if step:
            return x_ref[firsts[k] + order.index(t), 0, step - 1, rows, :]
        return early_ref[k * near + lax.rem(places[t], near), lax.div(places[t], near), 0, rows, :]

    xr, xi = [
        jnp.concatenate(
            [
                jnp.concatenate([piece(k, t, step, part) for t in range(tiles) for step in range(steps)], axis=0)
                for k in range(2)
            ],
            axis=1,
        )
        for part in range(2)
    ]
    rows_of = lambda k: pl.ds(k, own_angle.shape[0] // CLASSES, stride=CLASSES)
    phases = lambda k: cos_sin(jnp.concatenate([a[rows_of(k), :] for a in (own_angle, other_angle)], axis=1))
    fr, fi = focus(xr, xi, phases, [fw, bw])
    mr, mi, pr, pi = fr[:, :LANES], fi[:, :LANES], fr[:, LANES:], fi[:, LANES:]
    look = look_ref[0]
    reals = [mr * pr + mi * pi, mr * mr + mi * mi, pr * pr + pi * pi]
    imags = [mi * pr - mr * pi, mi * mr - mr * mi, pi * pr - pr * pi]
    cross_real, own_real, other_real = looked_at(reals, look[0])
    cross_imag, own_imag, other_imag = looked_at(imags, look[1])
    block = pl.program_id(0)

    @pl.when(block == 0)
    def _():
        looked[...] = jnp.zeros_like(looked)

    for r in range(rounds):
        same = same_ref[r] != 0
        looked[0, r] += jnp.where(same, own_real + own_imag, cross_real + cross_imag)
        looked[1, r] += jnp.where(same, other_real + other_imag, cross_real - cross_imag)

    @pl.when(block == pl.num_programs(0) - 1)
    def _():
        for k, first in enumerate(firsts):
            groups = pack(looked[k, 0], looked[k, 1])
            for place, t in enumerate(order):
                for j, (value, at) in enumerate(groups):
                    out[first + place, j] = value[t * SUB + at : t * SUB + at + SUB // 2]


def pack(even, odd):
    half = SUB // 2
    free = lax.broadcasted_iota(jnp.int32, even.shape, 1) >= USED
    rest = [pltpu.roll(odd, (USED - SPARE * j) % LANES, 1) for j in range(3)]
    up = lambda value: pltpu.roll(value, value.shape[0] - half, 0)
    return (
        (jnp.where(free, up(rest[0]), even), 0),
        (jnp.where(free, rest[1], even), half),
        (jnp.where(free, up(rest[2]), odd), 0),
    )


def unpack(parts):
    lane = lax.broadcasted_iota(jnp.int32, parts[0].shape, 1)
    rest = [pltpu.roll(part, (SPARE * j - USED) % LANES, 1) for j, part in enumerate(parts)]
    last = jnp.where(lane < SPARE, rest[0], jnp.where(lane < 2 * SPARE, rest[1], rest[2]))
    return jnp.concatenate([parts[0], parts[1], parts[2], last], axis=0)


def joint_call(me, same, array, early, angle, other_angle, tables, order):
    dests, blocks, steps = array.shape[:3]
    tiles = len(order)
    lines = angle.shape[0]
    rounds = same.shape[0]
    wide = blocks * LANES // LOOK_RG
    look = np.stack(
        [
            np.stack([look_table(LANES, c * wide + b * LANES // LOOK_RG) for c in range(2)])
            for b in range(blocks)
        ]
    )
    return pl.pallas_call(
        functools.partial(joint_kernel, order, rounds),
        grid_spec=pltpu.PrefetchScalarGridSpec(
            num_scalar_prefetch=2,
            grid=(blocks,),
            in_specs=[
                pl.BlockSpec((dests, 1) + array.shape[2:], lambda b, me, same: (0, b, 0, 0, 0)),
                pl.BlockSpec(early.shape[:2] + (1,) + early.shape[3:], lambda b, me, same: (0, 0, b, 0, 0)),
                pl.BlockSpec((lines, LANES), lambda b, me, same: (0, me[0] * blocks + b)),
                pl.BlockSpec((lines, LANES), lambda b, me, same: (0, b)),
                *[pl.BlockSpec(t.shape, lambda b, me, same: (0, 0, 0)) for t in tables],
                pl.BlockSpec((1,) + look.shape[1:], lambda b, me, same: (b, 0, 0, 0)),
            ],
            out_specs=pl.BlockSpec((dests, 3, SUB // 2, LANES), lambda b, me, same: (0, 0, 0, 0)),
            scratch_shapes=[
                pltpu.VMEM((2, rounds, AOI // LOOK_AZ, LANES), jnp.float32),
            ],
        ),
        out_shape=jax.ShapeDtypeStruct((dests, 3, SUB // 2, LANES), jnp.float32),
        compiler_params=pltpu.CompilerParams(vmem_limit_bytes=VMEM_LIMIT),
        cost_estimate=pl.CostEstimate(
            flops=2 * 2 * 3 * 6 * 256 * 256 * 2 * LANES * blocks,
            bytes_accessed=20 * lines * 2 * LANES * blocks,
            transcendentals=0,
        ),
        name="azimuth_interferogram",
    )(me, same, array, early, angle, other_angle, *[jnp.asarray(t) for t in tables], jnp.asarray(look))


def single_kernel(tiles, x_ref, angle_ref, fw, bw, out):
    xr, xi = [x_ref[:, 0, :, part * SUB : (part + 1) * SUB, :].reshape(-1, LANES) for part in range(2)]
    fr, fi = focus(xr, xi, lambda k: cos_sin(angle_ref[pl.ds(k, angle_ref.shape[0] // CLASSES, stride=CLASSES), :]), [fw, bw])
    out[:AOI] = fr
    out[AOI:] = fi


def single_call(array, angle, tables):
    tiles = array.shape[0]
    lines, columns = angle.shape
    return pl.pallas_call(
        functools.partial(single_kernel, tiles),
        grid=(columns // LANES,),
        in_specs=[
            pl.BlockSpec((tiles, 1) + array.shape[2:], lambda b: (0, b, 0, 0, 0)),
            pl.BlockSpec((lines, LANES), lambda b: (0, b)),
        ]
        + [pl.BlockSpec(t.shape, lambda b: (0, 0, 0)) for t in tables],
        out_specs=pl.BlockSpec((2 * AOI, LANES), lambda b: (0, b)),
        out_shape=jax.ShapeDtypeStruct((2 * AOI, columns), jnp.float32),
        compiler_params=pltpu.CompilerParams(vmem_limit_bytes=VMEM_LIMIT),
        name="azimuth_focus",
    )(array, angle, *[jnp.asarray(t) for t in tables])


def look_table(width, offset):
    table = np.zeros((width, LANES), np.float64)
    table[np.arange(width), offset + np.arange(width) // LOOK_RG] = 1.0 / (LOOK_AZ * LOOK_RG)
    return table.astype(ml_dtypes.bfloat16)


def cross_kernel(rounds, tiles, mine_ref, *refs):
    partner_refs, look_ref, out = refs[:rounds], refs[-2], refs[-1]
    mr, mi = mine_ref[:AOI], mine_ref[AOI:]
    per = AOI // LOOK_AZ // tiles
    for r in range(rounds):
        pr, pi = partner_refs[r][:AOI], partner_refs[r][AOI:]
        for c, field in enumerate((mr * pr + mi * pi, mi * pr - mr * pi)):
            (looked,) = looked_at([field], look_ref[...])
            at = (c * rounds + r) * per
            for t in range(tiles):
                out[t, at : at + per, :] = looked[t * per : (t + 1) * per]


def cross_call(mine, partners, tiles):
    rounds = len(partners)
    width = mine.shape[1]
    look = jnp.asarray(look_table(width, 0))
    shape = (tiles, 2 * rounds * (AOI // LOOK_AZ // tiles), LANES)
    vmem = lambda: pl.BlockSpec(memory_space=pltpu.VMEM)
    return pl.pallas_call(
        functools.partial(cross_kernel, rounds, tiles),
        in_specs=[vmem() for _ in range(rounds + 2)],
        out_specs=vmem(),
        out_shape=jax.ShapeDtypeStruct(shape, jnp.float32),
        compiler_params=pltpu.CompilerParams(vmem_limit_bytes=VMEM_LIMIT),
        name="interferogram",
    )(mine, *partners, look)


def place_kernel(sources, valid, parts, in_ref, out):
    if in_ref.shape[1:] == (3, SUB // 2, LANES):
        values = {k: unpack([in_ref[k, j] for j in range(3)]) for k in sources}
    else:
        values = {k: in_ref[k] for k in sources}
    rows = values[sources[0]].shape[0]
    lane = lax.broadcasted_iota(jnp.int32, (rows, LANES), 1)
    for c in range(parts):
        for o in range(len(sources) * valid // LANES):
            acc = None
            for place, source in enumerate(sources):
                shift = place * valid - o * LANES
                if shift + valid <= 0 or shift >= LANES:
                    continue
                value = values[source]
                turn_by = (shift - c * valid) % LANES
                if turn_by:
                    value = pltpu.roll(value, turn_by, 1)
                acc = value if acc is None else jnp.where(lane >= shift, value, acc)
            out[c * rows : (c + 1) * rows, o * LANES : (o + 1) * LANES] = acc


def place_call(received, rows, sources, valid, parts):
    return pl.pallas_call(
        functools.partial(place_kernel, sources, valid, parts),
        in_specs=[pl.BlockSpec(memory_space=pltpu.VMEM)],
        out_specs=pl.BlockSpec(memory_space=pltpu.VMEM),
        out_shape=jax.ShapeDtypeStruct((parts * rows, len(sources) * valid), jnp.float32),
        compiler_params=pltpu.CompilerParams(vmem_limit_bytes=VMEM_LIMIT),
        name="place_samples",
    )(received)


def turn(array, axes):
    return lax.all_to_all(array, axes, split_axis=0, concat_axis=0, tiled=True)


def joint(tiles, echo, slant, angle, pairs):
    steps = echo.shape[2] // SUB
    columns = angle.shape[1]
    rounds = pairs.shape[0]
    acq = lax.axis_index("acq")
    same = (lax.dynamic_index_in_dim(pairs, acq, 1, keepdims=False) == acq).astype(jnp.int32)
    theirs = lax.dynamic_slice_in_dim(angle, (1 - acq) * (columns // 2), columns // 2, 1)
    other_angle = lax.ppermute(theirs, "acq", [(0, 1), (1, 0)])
    low = lax.axis_size("low")
    order = [h * low + k for k in range(low) for h in range(tiles // low)]
    axes = ("acq", "low", "high")
    tile = lax.axis_index("high") * low + lax.axis_index("low")
    me = jnp.stack([acq, tile]).astype(jnp.int32)
    kept, given = range_call(echo, slant, 0, 1, order, 2, early=True)
    came = lax.ppermute(given, "high", [(h, h ^ (FAR // 2)) for h in range(FAR)])
    (sent,) = range_call(echo, slant, 1, steps - 1, order, 2)
    array = turn(sent, axes)
    early = list(pair_call(kept, came))
    near = tiles // 2
    for s in range(1, tiles):
        flip = s // near * tiles + s % near
        early[s] = lax.ppermute(early[s], ("acq", "high", "low"), [(i, i ^ flip) for i in range(2 * tiles)])
    early = jnp.stack(early)
    looked = joint_call(me, same, array, early, angle, other_angle, azimuth_tables(angle.shape[0]), order)
    sources = [half * tiles + order.index(t) for t in range(tiles) for half in range(2)]
    result = place_call(turn(looked, axes), rounds * SUB, sources, columns // 2 // LOOK_RG, 2)
    return result.reshape(2, rounds, 1, -1, result.shape[1])


def separate(tiles, echo, slant, angle, pairs):
    columns = angle.shape[1]
    rounds = pairs.shape[0]
    (sent,) = range_call(echo, slant, 0, echo.shape[2] // SUB, list(range(tiles)), 1)
    mine = single_call(turn(sent, ("high", "low")), angle, azimuth_tables(angle.shape[0]))
    every = lax.all_gather(mine, "acq", axis=0)
    partner = lax.dynamic_index_in_dim(pairs, lax.axis_index("acq"), 1, keepdims=False)
    partners = [lax.dynamic_index_in_dim(every, partner[r], 0, keepdims=False) for r in range(rounds)]
    looked = turn(cross_call(mine, partners, tiles), ("high", "low"))
    result = place_call(looked, looked.shape[1], list(range(tiles)), columns // LOOK_RG, 1)
    return result.reshape(2, rounds, 1, -1, result.shape[1])


def shards(tiles, acqs, echo, slant, angle, pairs):
    fits = echo.shape[2] > SUB and tiles == FAR * FAR and AOI // LOOK_AZ == tiles * SUB
    fits = fits and angle.shape[2] // LOOK_RG == USED and pairs.shape[0] == 2
    program = joint if acqs == 2 and fits else separate
    return program(tiles, echo, slant, angle[0], pairs)


def solution(mesh):
    acqs, tiles = mesh.shape["acq"], mesh.shape["tile"]
    low = 1 << (tiles.bit_length() // 2)
    low = low if tiles % low == 0 else 1
    split_mesh = jax.sharding.Mesh(mesh.devices.reshape(acqs, tiles // low, low), ("acq", "high", "low"))
    tile = ("high", "low")
    in_specs = (P(None, "acq", tile, None), P(None, "acq", None), P("acq", None, tile), P())
    out_specs = P(None, None, "acq", tile, None)
    body = functools.partial(shards, tiles, acqs)
    return jax.shard_map(body, mesh=split_mesh, in_specs=in_specs, out_specs=out_specs, check_vma=False)
```

```python
import functools
import math

import jax
import jax.numpy as jnp
import ml_dtypes
import numpy as np
from jax import lax
from jax.experimental import pallas as pl
from jax.experimental.pallas import tpu as pltpu
from jax.sharding import PartitionSpec as P

LOOK_AZ = 2
LOOK_RG = 8
AOI = 256
LANES = 128
SUB = 8
FAR = 4
SPARE = 32
USED = LANES - SPARE
CLASSES = 12
BATCH = 4
VMEM_LIMIT = 56 * 1024 * 1024


def high_low(table):
    high = table.astype(ml_dtypes.bfloat16)
    low = (table - high.astype(np.float64)).astype(ml_dtypes.bfloat16)
    return np.stack([high, low])


def trig(product, period):
    angle = (product % period) * (2.0 * math.pi / period)
    return np.cos(angle), np.sin(angle)


def split(value):
    high = value.astype(jnp.bfloat16)
    return high, (value - high.astype(jnp.float32)).astype(jnp.bfloat16)


def dot(left, right):
    return jnp.dot(left, right, preferred_element_type=jnp.float32)


def dot_stacked(table, value):
    high, low = split(value)
    both = dot(table, jnp.concatenate([high, low], axis=0))
    rows = table.shape[0] // 2
    return both[:rows] + both[rows:]


def dot_parts(table, value):
    rows = table.shape[0] // 2
    high, low = table[:rows], table[rows:]
    left = [jnp.concatenate(pair, axis=1) for pair in ((high, high), (low, jnp.zeros_like(low)))]
    return dot_stacked(jnp.concatenate(left, axis=0), value)


def thirds(a, b, c, sign):
    scale = sign * math.sqrt(3.0) / 2.0
    tr, ti = b[0] + c[0], b[1] + c[1]
    vr, vi = (b[0] - c[0]) * scale, (b[1] - c[1]) * scale
    ur, ui = a[0] - 0.5 * tr, a[1] - 0.5 * ti
    return (a[0] + tr, a[1] + ti), (ur - vi, ui + vr), (ur + vi, ui - vr)


def dot_table_right(value, table):
    rows = table.shape[0] // 2
    high_table, low_table = table[:rows], table[rows:]
    high, low = split(value)
    return dot(
        jnp.concatenate([high, low, high], axis=1),
        jnp.concatenate([high_table, high_table, low_table], axis=0),
    )


def stacked(table):
    high, low = high_low(table)
    return np.block([[high, high], [low, np.zeros_like(low)]])


def range_tables(length, order, halves):
    inner = LANES
    outer = length // inner
    part = outer // 3
    k1 = np.arange(outer)
    q = np.arange(inner)
    inside = np.arange(part)
    per_tile = outer // len(order)
    blocks = per_tile // halves
    a1, a4 = [], []
    for p0 in range(3):
        c, s = trig(np.outer(inside, 3 * inside + p0), outer)
        a1.append(stacked(np.block([[c, s], [-s, c]])))
        c, s = trig(np.outer(3 * inside + p0, inside), outer)
        rows = [
            cc * part + (t * per_tile + half * blocks) // 3 + b
            for cc in range(2)
            for half in range(halves)
            for t in order
            for b in range(blocks // 3)
        ]
        a4.append(stacked(np.block([[c, -s], [s, c]])[np.array(rows)] / length))
    c2, s2 = trig(np.outer(q, q), inner)
    b2 = np.block([[c2, -s2], [s2, c2]])
    ct, st = trig(np.outer(k1, q), length)
    twiddle = np.stack([ct, st]).astype(np.float32)
    b2 = np.concatenate(high_low(b2))
    return np.stack(a1), b2, np.stack(a4), twiddle


def spot(tile, low):
    return lax.rem(tile, low) * FAR + lax.div(tile, low)


def range_kernel(outer, early, x_ref, slant_ref, a1_ref, b2_ref, a4_ref, t_ref, *rest):
    outs, (rows_ref, h_ref), held = rest[: 1 + early], rest[1 + early : 3 + early], rest[3 + early :]
    part = outer // 3

    @pl.when(pl.program_id(0) == 0)
    def _():
        for c in range(2):
            for k2 in range(LANES):
                rows_ref[c, k2 : k2 + 1, :outer] = slant_ref[c, :, k2 * outer : (k2 + 1) * outer]
            h_ref[c] = rows_ref[c].T[:outer]

    rows = outs[0].shape[1] * outs[0].shape[3]
    turned = held[0] if early else outs[0].reshape(outs[0].shape[0] * rows, LANES)
    ct, st = t_ref[0], t_ref[1]
    hr, hi = h_ref[0], h_ref[1]

    def batch(first):
        lines = range(first, first + BATCH)
        y = []
        for p0 in range(3):
            x = [
                jnp.concatenate(
                    [x_ref[c, 0, pl.ds(p0 * SUB + l, part, stride=3 * SUB), :] for c in range(2)], axis=0
                )
                for l in lines
            ]
            value = dot_stacked(a1_ref[p0], jnp.concatenate(x, axis=1))
            y.append((value[:part], value[part:]))
        yield
        y = thirds(*y, -1.0)
        z = []
        for b in range(BATCH):
            yr, yi = [
                jnp.concatenate([v[c][:, b * LANES : (b + 1) * LANES] for v in y], axis=0) for c in range(2)
            ]
            z.append(jnp.concatenate([yr * ct + yi * st, yi * ct - yr * st], axis=1))
        y = dot_table_right(jnp.concatenate(z, axis=0), b2_ref[...])
        yield
        z = []
        for b in range(BATCH):
            yr = y[b * outer : (b + 1) * outer, :LANES]
            yi = y[b * outer : (b + 1) * outer, LANES:]
            z.append(jnp.concatenate([yr * hr - yi * hi, -yr * hi - yi * hr], axis=1))
        y = dot_table_right(jnp.concatenate(z, axis=0), b2_ref[...])
        yield
        z = []
        for b in range(BATCH):
            yr = y[b * outer : (b + 1) * outer, :LANES]
            yi = y[b * outer : (b + 1) * outer, LANES:]
            zr, zi = yr * ct + yi * st, yr * st - yi * ct
            z.append(thirds(*[(zr[k * part : (k + 1) * part], zi[k * part : (k + 1) * part]) for k in range(3)], 1.0))
        y = []
        for p0 in range(3):
            value = jnp.concatenate([jnp.concatenate(z[b][p0], axis=0) for b in range(BATCH)], axis=1)
            y.append(dot_stacked(a4_ref[p0], value))
        yield
        for p0 in range(3):
            for b, l in enumerate(lines):
                for c in range(2):
                    turned[pl.ds((2 * p0 + c) * SUB + l, part, stride=6 * SUB), :] = y[p0][
                        c * part : (c + 1) * part, b * LANES : (b + 1) * LANES
                    ]
        yield

    batches = [batch(first) for first in range(0, SUB, BATCH)]
    for _ in range(5):
        for work in batches:
            next(work)
    if not early:
        return
    near = outs[0].shape[0] // 2
    acq = lax.axis_index("acq")
    place = lax.axis_index("high") * (2 * near // FAR) + lax.axis_index("low")
    for k, out in enumerate(outs):
        for s in range(2 * near):
            tile = jnp.bitwise_xor(place, s % near + k * near)
            dest = jnp.bitwise_xor(acq, s // near) * 2 * near + spot(tile, 2 * near // FAR)
            value = turned[pl.ds(pl.multiple_of(dest * rows, SUB), rows), :]
            out[s, :, 0] = value.reshape(out.shape[1], out.shape[3], LANES)


def range_call(echo, slant, first, steps, order, halves, early=False):
    length = echo.shape[3]
    outer = length // LANES
    view = echo.reshape(2, -1, SUB, outer, LANES).transpose(0, 1, 3, 2, 4).reshape(2, -1, outer * SUB, LANES)
    tables = [slant, *range_tables(length, order, halves)]
    dests = len(order) * halves
    blocks = outer // dests
    rows = 2 * blocks * SUB
    whole = lambda shape: pl.BlockSpec(shape, lambda s: (0,) * len(shape))
    macs = steps * SUB * length * 2 * (2 * outer + 2 * LANES) * 2 * 3
    outs = 1 + early
    return pl.pallas_call(
        functools.partial(range_kernel, outer, early),
        grid=(steps,),
        in_specs=[pl.BlockSpec((2, 1, outer * SUB, LANES), lambda s: (0, first + s, 0, 0))]
        + [whole(t.shape) for t in tables],
        out_specs=[pl.BlockSpec((dests // outs, blocks, 1, 2 * SUB, LANES), lambda s: (0, 0, s, 0, 0))] * outs,
        scratch_shapes=[
            pltpu.VMEM((2, LANES, LANES), jnp.float32),
            pltpu.VMEM((2, outer, LANES), jnp.float32),
        ]
        + [pltpu.VMEM((dests * rows, LANES), jnp.float32)] * early,
        out_shape=[jax.ShapeDtypeStruct((dests // outs, blocks, steps, 2 * SUB, LANES), jnp.float32)] * outs,
        compiler_params=pltpu.CompilerParams(vmem_limit_bytes=VMEM_LIMIT),
        cost_estimate=pl.CostEstimate(
            flops=2 * macs, bytes_accessed=16 * steps * SUB * length, transcendentals=0
        ),
        name=f"range_compress_{first}",
    )(view, *[jnp.asarray(t) for t in tables])


def pair_kernel(kept_ref, came_ref, *outs):
    for s, out in enumerate(outs):
        out[0] = kept_ref[s, :, 0]
        out[1] = came_ref[s, :, 0]


def pair_call(kept, came):
    count, blocks, _, rows, _ = kept.shape
    vmem = pl.BlockSpec(memory_space=pltpu.VMEM)
    return pl.pallas_call(
        pair_kernel,
        in_specs=[vmem] * 2,
        out_specs=[vmem] * count,
        out_shape=[jax.ShapeDtypeStruct((2, blocks, rows, LANES), jnp.float32)] * count,
        compiler_params=pltpu.CompilerParams(vmem_limit_bytes=VMEM_LIMIT),
        cost_estimate=pl.CostEstimate(flops=10**12, bytes_accessed=4 * kept.size, transcendentals=0),
        name="pair_halves",
    )(kept, came)


def azimuth_tables(length):
    part = length // CLASSES
    f1 = np.arange(part)
    ahead, back = [], []
    first = (length - AOI) // 2
    u, s = np.arange(part // LOOK_AZ), np.arange(LOOK_AZ)
    lines = (first + u[None, :] * LOOK_AZ + s[:, None]).reshape(-1)
    for f0 in range(CLASSES):
        c, s = trig(np.outer(CLASSES * f1 + f0, np.arange(part)), length)
        ahead.append(np.concatenate(high_low(np.block([[c, s], [-s, c]]))))
        c, s = trig(np.outer(lines, CLASSES * f1 + f0), length)
        back.append(np.concatenate(high_low(np.block([[c, -s], [s, c]]) / length)))
    return [np.stack(ahead), np.stack(back)]


def cos_sin(angle):
    y = 0.5 * angle
    z = y * y
    sine = [1.0, -1 / 6, 1 / 120, -1 / 5040, 1 / 362880, -1 / 39916800]
    cosine = [1.0, -1 / 2, 1 / 24, -1 / 720, 1 / 40320, -1 / 3628800, 1 / 479001600]
    s, c = sine[-1], cosine[-1]
    for k in sine[-2::-1]:
        s = s * z + k
    for k in cosine[-2::-1]:
        c = c * z + k
    s = s * y
    return 1.0 - 2.0 * (s * s), 2.0 * (s * c)


def fours(a, b, c, d):
    (ar, ai), (br, bi), (cr, ci), (dr, di) = a, b, c, d
    pr, pi, mr, mi = ar + cr, ai + ci, ar - cr, ai - ci
    qr, qi, nr, ni = br + dr, bi + di, br - dr, bi - di
    return (pr + qr, pi + qi), (mr + ni, mi - nr), (pr - qr, pi - qi), (mr - ni, mi + nr)


def class_of(e, g):
    return (4 * e + 9 * g) % CLASSES


def focus(xr, xi, phases, tables):
    fw, bw = tables
    part = xr.shape[0] // CLASSES
    x = [(xr[k * part : (k + 1) * part], xi[k * part : (k + 1) * part]) for k in range(CLASSES)]
    columns = [thirds(*[x[(4 * i + 3 * j) % CLASSES] for i in range(3)], -1.0) for j in range(4)]
    made, ahead, done, sums = [], [], [], []
    make = lambda e: made.append(fours(*[columns[j][e] for j in range(4)]))
    make(0)
    for i in range(CLASSES + 1):
        e, g = divmod(i, 4)
        if g == 2 and e < 2:
            make(e + 1)
        if i < CLASSES:
            ahead.append(dot_parts(fw[class_of(e, g)], jnp.concatenate(made[e][g], axis=0)))
        if i > 0:
            y, k = ahead[i - 1], class_of(*divmod(i - 1, 4))
            dr, di = y[:part], y[part:]
            pc, ps = phases(k)
            value = jnp.concatenate([dr * pc - di * ps, dr * ps + di * pc], axis=0)
            y = dot_parts(bw[k], value)
            done.append((y[:part], y[part:]))
            if i > 4 and g == 1:
                sums.append(fours(*done[i - 5 : i - 1]))
    sums.append(fours(*done[8:]))
    outs = []
    for h in range(AOI // part):
        terms = [sums[e][h] for e in range(3)]
        outs.append(thirds(*terms, 1.0)[h % 3])
    return [jnp.concatenate([pair[c] for pair in outs], axis=0) for c in range(2)]


def looked_at(field, look):
    lines = AOI // 4 // LOOK_AZ
    groups = [field[k * lines : (k + 1) * lines] for k in range(AOI // lines)]
    added = [groups[k] + groups[k + 1] for k in range(0, len(groups), LOOK_AZ)]
    high, low = split(jnp.concatenate(added, axis=0))
    return dot(high, look) + dot(low, look)


def joint_kernel(order, rounds, me_ref, same_ref, x_ref, early_ref, own_angle, other_angle, fw, bw, look_ref, out, stage, looked):
    acq = me_ref[0]
    tiles = len(order)
    near = tiles // 2
    firsts = [acq * tiles, (1 - acq) * tiles]
    for part in range(2):
        for k, first in enumerate(firsts):
            lanes = slice(k * LANES, (k + 1) * LANES)
            for place, t in enumerate(order):
                stage[part, t, 1:, :, lanes] = x_ref[first + place, 0, :, part * SUB : (part + 1) * SUB, :]
            for s in range(near):
                for side in range(2):
                    tile = jnp.bitwise_xor(me_ref[1], s + side * near)
                    stage[part, tile, 0, :, lanes] = early_ref[k * near + s, side, 0, part * SUB : (part + 1) * SUB, :]
    xr, xi = [stage[part].reshape(-1, 2 * LANES) for part in range(2)]
    rows_of = lambda k: pl.ds(k, own_angle.shape[0] // CLASSES, stride=CLASSES)
    phases = lambda k: cos_sin(jnp.concatenate([a[rows_of(k), :] for a in (own_angle, other_angle)], axis=1))
    fr, fi = focus(xr, xi, phases, [fw, bw])
    mr, mi, pr, pi = fr[:, :LANES], fi[:, :LANES], fr[:, LANES:], fi[:, LANES:]
    look = look_ref[0]
    cross_real = looked_at(mr * pr + mi * pi, look[0])
    cross_imag = looked_at(mi * pr - mr * pi, look[1])
    own_real = looked_at(mr * mr + mi * mi, look[0])
    own_imag = looked_at(mi * mr - mr * mi, look[1])
    other_real = looked_at(pr * pr + pi * pi, look[0])
    other_imag = looked_at(pi * pr - pr * pi, look[1])
    block = pl.program_id(0)

    @pl.when(block == 0)
    def _():
        looked[...] = jnp.zeros_like(looked)

    for r in range(rounds):
        same = same_ref[r] != 0
        looked[0, r] += jnp.where(same, own_real + own_imag, cross_real + cross_imag)
        looked[1, r] += jnp.where(same, other_real + other_imag, cross_real - cross_imag)

    @pl.when(block == pl.num_programs(0) - 1)
    def _():
        for k, first in enumerate(firsts):
            groups = pack(looked[k, 0], looked[k, 1])
            for place, t in enumerate(order):
                for j, (value, at) in enumerate(groups):
                    out[first + place, j] = value[t * SUB + at : t * SUB + at + SUB // 2]


def pack(even, odd):
    half = SUB // 2
    free = lax.broadcasted_iota(jnp.int32, even.shape, 1) >= USED
    rest = [pltpu.roll(odd, (USED - SPARE * j) % LANES, 1) for j in range(3)]
    up = lambda value: pltpu.roll(value, value.shape[0] - half, 0)
    return (
        (jnp.where(free, up(rest[0]), even), 0),
        (jnp.where(free, rest[1], even), half),
        (jnp.where(free, up(rest[2]), odd), 0),
    )


def unpack(parts):
    lane = lax.broadcasted_iota(jnp.int32, parts[0].shape, 1)
    rest = [pltpu.roll(part, (SPARE * j - USED) % LANES, 1) for j, part in enumerate(parts)]
    last = jnp.where(lane < SPARE, rest[0], jnp.where(lane < 2 * SPARE, rest[1], rest[2]))
    return jnp.concatenate([parts[0], parts[1], parts[2], last], axis=0)


def joint_call(me, same, array, early, angle, other_angle, tables, order):
    dests, blocks, steps = array.shape[:3]
    tiles = len(order)
    lines = angle.shape[0]
    rounds = same.shape[0]
    wide = blocks * LANES // LOOK_RG
    look = np.stack(
        [
            np.stack([look_table(LANES, c * wide + b * LANES // LOOK_RG) for c in range(2)])
            for b in range(blocks)
        ]
    )
    return pl.pallas_call(
        functools.partial(joint_kernel, order, rounds),
        grid_spec=pltpu.PrefetchScalarGridSpec(
            num_scalar_prefetch=2,
            grid=(blocks,),
            in_specs=[
                pl.BlockSpec((dests, 1) + array.shape[2:], lambda b, me, same: (0, b, 0, 0, 0)),
                pl.BlockSpec(early.shape[:2] + (1,) + early.shape[3:], lambda b, me, same: (0, 0, b, 0, 0)),
                pl.BlockSpec((lines, LANES), lambda b, me, same: (0, me[0] * blocks + b)),
                pl.BlockSpec((lines, LANES), lambda b, me, same: (0, b)),
                *[pl.BlockSpec(t.shape, lambda b, me, same: (0, 0, 0)) for t in tables],
                pl.BlockSpec((1,) + look.shape[1:], lambda b, me, same: (b, 0, 0, 0)),
            ],
            out_specs=pl.BlockSpec((dests, 3, SUB // 2, LANES), lambda b, me, same: (0, 0, 0, 0)),
            scratch_shapes=[
                pltpu.VMEM((2, tiles, steps + 1, SUB, 2 * LANES), jnp.float32),
                pltpu.VMEM((2, rounds, AOI // LOOK_AZ, LANES), jnp.float32),
            ],
        ),
        out_shape=jax.ShapeDtypeStruct((dests, 3, SUB // 2, LANES), jnp.float32),
        compiler_params=pltpu.CompilerParams(vmem_limit_bytes=VMEM_LIMIT),
        cost_estimate=pl.CostEstimate(
            flops=2 * 2 * 3 * 6 * 256 * 256 * 2 * LANES * blocks,
            bytes_accessed=20 * lines * 2 * LANES * blocks,
            transcendentals=0,
        ),
        name="azimuth_interferogram",
    )(me, same, array, early, angle, other_angle, *[jnp.asarray(t) for t in tables], jnp.asarray(look))


def single_kernel(tiles, x_ref, angle_ref, fw, bw, out):
    xr, xi = [x_ref[:, 0, :, part * SUB : (part + 1) * SUB, :].reshape(-1, LANES) for part in range(2)]
    fr, fi = focus(xr, xi, lambda k: cos_sin(angle_ref[pl.ds(k, angle_ref.shape[0] // CLASSES, stride=CLASSES), :]), [fw, bw])
    out[:AOI] = fr
    out[AOI:] = fi


def single_call(array, angle, tables):
    tiles = array.shape[0]
    lines, columns = angle.shape
    return pl.pallas_call(
        functools.partial(single_kernel, tiles),
        grid=(columns // LANES,),
        in_specs=[
            pl.BlockSpec((tiles, 1) + array.shape[2:], lambda b: (0, b, 0, 0, 0)),
            pl.BlockSpec((lines, LANES), lambda b: (0, b)),
        ]
        + [pl.BlockSpec(t.shape, lambda b: (0, 0, 0)) for t in tables],
        out_specs=pl.BlockSpec((2 * AOI, LANES), lambda b: (0, b)),
        out_shape=jax.ShapeDtypeStruct((2 * AOI, columns), jnp.float32),
        compiler_params=pltpu.CompilerParams(vmem_limit_bytes=VMEM_LIMIT),
        name="azimuth_focus",
    )(array, angle, *[jnp.asarray(t) for t in tables])


def look_table(width, offset):
    table = np.zeros((width, LANES), np.float64)
    table[np.arange(width), offset + np.arange(width) // LOOK_RG] = 1.0 / (LOOK_AZ * LOOK_RG)
    return table.astype(ml_dtypes.bfloat16)


def cross_kernel(rounds, tiles, mine_ref, *refs):
    partner_refs, look_ref, out = refs[:rounds], refs[-2], refs[-1]
    mr, mi = mine_ref[:AOI], mine_ref[AOI:]
    per = AOI // LOOK_AZ // tiles
    for r in range(rounds):
        pr, pi = partner_refs[r][:AOI], partner_refs[r][AOI:]
        for c, field in enumerate((mr * pr + mi * pi, mi * pr - mr * pi)):
            looked = looked_at(field, look_ref[...])
            at = (c * rounds + r) * per
            for t in range(tiles):
                out[t, at : at + per, :] = looked[t * per : (t + 1) * per]


def cross_call(mine, partners, tiles):
    rounds = len(partners)
    width = mine.shape[1]
    look = jnp.asarray(look_table(width, 0))
    shape = (tiles, 2 * rounds * (AOI // LOOK_AZ // tiles), LANES)
    vmem = lambda: pl.BlockSpec(memory_space=pltpu.VMEM)
    return pl.pallas_call(
        functools.partial(cross_kernel, rounds, tiles),
        in_specs=[vmem() for _ in range(rounds + 2)],
        out_specs=vmem(),
        out_shape=jax.ShapeDtypeStruct(shape, jnp.float32),
        compiler_params=pltpu.CompilerParams(vmem_limit_bytes=VMEM_LIMIT),
        name="interferogram",
    )(mine, *partners, look)


def place_kernel(sources, valid, parts, in_ref, out):
    if in_ref.shape[1:] == (3, SUB // 2, LANES):
        values = {k: unpack([in_ref[k, j] for j in range(3)]) for k in sources}
    else:
        values = {k: in_ref[k] for k in sources}
    rows = values[sources[0]].shape[0]
    lane = lax.broadcasted_iota(jnp.int32, (rows, LANES), 1)
    for c in range(parts):
        for o in range(len(sources) * valid // LANES):
            acc = None
            for place, source in enumerate(sources):
                shift = place * valid - o * LANES
                if shift + valid <= 0 or shift >= LANES:
                    continue
                value = values[source]
                turn_by = (shift - c * valid) % LANES
                if turn_by:
                    value = pltpu.roll(value, turn_by, 1)
                acc = value if acc is None else jnp.where(lane >= shift, value, acc)
            out[c * rows : (c + 1) * rows, o * LANES : (o + 1) * LANES] = acc


def place_call(received, rows, sources, valid, parts):
    return pl.pallas_call(
        functools.partial(place_kernel, sources, valid, parts),
        in_specs=[pl.BlockSpec(memory_space=pltpu.VMEM)],
        out_specs=pl.BlockSpec(memory_space=pltpu.VMEM),
        out_shape=jax.ShapeDtypeStruct((parts * rows, len(sources) * valid), jnp.float32),
        compiler_params=pltpu.CompilerParams(vmem_limit_bytes=VMEM_LIMIT),
        name="place_samples",
    )(received)


def turn(array, axes):
    return lax.all_to_all(array, axes, split_axis=0, concat_axis=0, tiled=True)


def joint(tiles, echo, slant, angle, pairs):
    steps = echo.shape[2] // SUB
    columns = angle.shape[1]
    rounds = pairs.shape[0]
    acq = lax.axis_index("acq")
    same = (lax.dynamic_index_in_dim(pairs, acq, 1, keepdims=False) == acq).astype(jnp.int32)
    theirs = lax.dynamic_slice_in_dim(angle, (1 - acq) * (columns // 2), columns // 2, 1)
    other_angle = lax.ppermute(theirs, "acq", [(0, 1), (1, 0)])
    low = lax.axis_size("low")
    order = [h * low + k for k in range(low) for h in range(tiles // low)]
    axes = ("acq", "low", "high")
    tile = lax.axis_index("high") * low + lax.axis_index("low")
    me = jnp.stack([acq, tile]).astype(jnp.int32)
    kept, given = range_call(echo, slant, 0, 1, order, 2, early=True)
    came = lax.ppermute(given, "high", [(h, h ^ (FAR // 2)) for h in range(FAR)])
    (sent,) = range_call(echo, slant, 1, steps - 1, order, 2)
    array = turn(sent, axes)
    early = list(pair_call(kept, came))
    near = tiles // 2
    for s in range(1, tiles):
        flip = s // near * tiles + s % near
        early[s] = lax.ppermute(early[s], ("acq", "high", "low"), [(i, i ^ flip) for i in range(2 * tiles)])
    early = jnp.stack(early)
    looked = joint_call(me, same, array, early, angle, other_angle, azimuth_tables(angle.shape[0]), order)
    sources = [half * tiles + order.index(t) for t in range(tiles) for half in range(2)]
    result = place_call(turn(looked, axes), rounds * SUB, sources, columns // 2 // LOOK_RG, 2)
    return result.reshape(2, rounds, 1, -1, result.shape[1])


def separate(tiles, echo, slant, angle, pairs):
    columns = angle.shape[1]
    rounds = pairs.shape[0]
    (sent,) = range_call(echo, slant, 0, echo.shape[2] // SUB, list(range(tiles)), 1)
    mine = single_call(turn(sent, ("high", "low")), angle, azimuth_tables(angle.shape[0]))
    every = lax.all_gather(mine, "acq", axis=0)
    partner = lax.dynamic_index_in_dim(pairs, lax.axis_index("acq"), 1, keepdims=False)
    partners = [lax.dynamic_index_in_dim(every, partner[r], 0, keepdims=False) for r in range(rounds)]
    looked = turn(cross_call(mine, partners, tiles), ("high", "low"))
    result = place_call(looked, looked.shape[1], list(range(tiles)), columns // LOOK_RG, 1)
    return result.reshape(2, rounds, 1, -1, result.shape[1])


def shards(tiles, acqs, echo, slant, angle, pairs):
    fits = echo.shape[2] > SUB and tiles == FAR * FAR and AOI // LOOK_AZ == tiles * SUB
    fits = fits and angle.shape[2] // LOOK_RG == USED and pairs.shape[0] == 2
    program = joint if acqs == 2 and fits else separate
    return program(tiles, echo, slant, angle[0], pairs)


def solution(mesh):
    acqs, tiles = mesh.shape["acq"], mesh.shape["tile"]
    low = 1 << (tiles.bit_length() // 2)
    low = low if tiles % low == 0 else 1
    split_mesh = jax.sharding.Mesh(mesh.devices.reshape(acqs, tiles // low, low), ("acq", "high", "low"))
    tile = ("high", "low")
    in_specs = (P(None, "acq", tile, None), P(None, "acq", None), P("acq", None, tile), P())
    out_specs = P(None, None, "acq", tile, None)
    body = functools.partial(shards, tiles, acqs)
    return jax.shard_map(body, mesh=split_mesh, in_specs=in_specs, out_specs=out_specs, check_vma=False)
```

```python
import functools
import math

import jax
import jax.numpy as jnp
import ml_dtypes
import numpy as np
from jax import lax
from jax.experimental import pallas as pl
from jax.experimental.pallas import tpu as pltpu
from jax.sharding import PartitionSpec as P

LOOK_AZ = 2
LOOK_RG = 8
AOI = 256
LANES = 128
SUB = 8
FAR = 4
SPARE = 32
USED = LANES - SPARE
CLASSES = 12
BATCH = 4
VMEM_LIMIT = 56 * 1024 * 1024


def high_low(table):
    high = table.astype(ml_dtypes.bfloat16)
    low = (table - high.astype(np.float64)).astype(ml_dtypes.bfloat16)
    return np.stack([high, low])


def trig(product, period):
    angle = (product % period) * (2.0 * math.pi / period)
    return np.cos(angle), np.sin(angle)


def split(value):
    high = value.astype(jnp.bfloat16)
    return high, (value - high.astype(jnp.float32)).astype(jnp.bfloat16)


def dot(left, right):
    return jnp.dot(left, right, preferred_element_type=jnp.float32)


def dot_stacked(table, value):
    high, low = split(value)
    both = dot(table, jnp.concatenate([high, low], axis=0))
    rows = table.shape[0] // 2
    return both[:rows] + both[rows:]


def dot_parts(table, value):
    rows = table.shape[0] // 2
    high, low = table[:rows], table[rows:]
    left = [jnp.concatenate(pair, axis=1) for pair in ((high, high), (low, jnp.zeros_like(low)))]
    return dot_stacked(jnp.concatenate(left, axis=0), value)


def thirds(a, b, c, sign):
    scale = sign * math.sqrt(3.0) / 2.0
    tr, ti = b[0] + c[0], b[1] + c[1]
    vr, vi = (b[0] - c[0]) * scale, (b[1] - c[1]) * scale
    ur, ui = a[0] - 0.5 * tr, a[1] - 0.5 * ti
    return (a[0] + tr, a[1] + ti), (ur - vi, ui + vr), (ur + vi, ui - vr)


def dot_table_right(value, table):
    rows = table.shape[0] // 2
    high_table, low_table = table[:rows], table[rows:]
    high, low = split(value)
    return dot(
        jnp.concatenate([high, low, high], axis=1),
        jnp.concatenate([high_table, high_table, low_table], axis=0),
    )


def stacked(table):
    high, low = high_low(table)
    return np.block([[high, high], [low, np.zeros_like(low)]])


def range_tables(length, order, halves):
    inner = LANES
    outer = length // inner
    part = outer // 3
    k1 = np.arange(outer)
    q = np.arange(inner)
    inside = np.arange(part)
    per_tile = outer // len(order)
    blocks = per_tile // halves
    a1, a4 = [], []
    for p0 in range(3):
        c, s = trig(np.outer(inside, 3 * inside + p0), outer)
        a1.append(stacked(np.block([[c, s], [-s, c]])))
        c, s = trig(np.outer(3 * inside + p0, inside), outer)
        rows = [
            cc * part + (t * per_tile + half * blocks) // 3 + b
            for cc in range(2)
            for half in range(halves)
            for t in order
            for b in range(blocks // 3)
        ]
        a4.append(stacked(np.block([[c, -s], [s, c]])[np.array(rows)] / length))
    c2, s2 = trig(np.outer(q, q), inner)
    b2 = np.block([[c2, -s2], [s2, c2]])
    ct, st = trig(np.outer(k1, q), length)
    twiddle = np.stack([ct, st]).astype(np.float32)
    b2 = np.concatenate(high_low(b2))
    return np.stack(a1), b2, np.stack(a4), twiddle


def spot(tile, low):
    return lax.rem(tile, low) * FAR + lax.div(tile, low)


def range_kernel(outer, early, x_ref, slant_ref, a1_ref, b2_ref, a4_ref, t_ref, *rest):
    outs, (rows_ref, h_ref), held = rest[: 1 + early], rest[1 + early : 3 + early], rest[3 + early :]
    part = outer // 3

    def arrange():
        for c in range(2):
            for k2 in range(LANES):
                rows_ref[c, k2 : k2 + 1, :outer] = slant_ref[c, :, k2 * outer : (k2 + 1) * outer]
            h_ref[c] = rows_ref[c].T[:outer]

    if not early:
        pl.when(pl.program_id(0) == 0)(arrange)

    rows = outs[0].shape[1] * outs[0].shape[3]
    turned = held[0] if early else outs[0].reshape(outs[0].shape[0] * rows, LANES)
    ct, st = t_ref[0], t_ref[1]

    def batch(first):
        lines = range(first, first + BATCH)
        y = []
        for p0 in range(3):
            x = [
                jnp.concatenate(
                    [x_ref[c, 0, pl.ds(p0 * SUB + l, part, stride=3 * SUB), :] for c in range(2)], axis=0
                )
                for l in lines
            ]
            value = dot_stacked(a1_ref[p0], jnp.concatenate(x, axis=1))
            y.append((value[:part], value[part:]))
        yield
        y = thirds(*y, -1.0)
        z = []
        for b in range(BATCH):
            yr, yi = [
                jnp.concatenate([v[c][:, b * LANES : (b + 1) * LANES] for v in y], axis=0) for c in range(2)
            ]
            z.append(jnp.concatenate([yr * ct + yi * st, yi * ct - yr * st], axis=1))
        y = dot_table_right(jnp.concatenate(z, axis=0), b2_ref[...])
        yield
        hr, hi = h_ref[0], h_ref[1]
        z = []
        for b in range(BATCH):
            yr = y[b * outer : (b + 1) * outer, :LANES]
            yi = y[b * outer : (b + 1) * outer, LANES:]
            z.append(jnp.concatenate([yr * hr - yi * hi, -yr * hi - yi * hr], axis=1))
        y = dot_table_right(jnp.concatenate(z, axis=0), b2_ref[...])
        yield
        z = []
        for b in range(BATCH):
            yr = y[b * outer : (b + 1) * outer, :LANES]
            yi = y[b * outer : (b + 1) * outer, LANES:]
            zr, zi = yr * ct + yi * st, yr * st - yi * ct
            z.append(thirds(*[(zr[k * part : (k + 1) * part], zi[k * part : (k + 1) * part]) for k in range(3)], 1.0))
        y = []
        for p0 in range(3):
            value = jnp.concatenate([jnp.concatenate(z[b][p0], axis=0) for b in range(BATCH)], axis=1)
            y.append(dot_stacked(a4_ref[p0], value))
        yield
        for p0 in range(3):
            for b, l in enumerate(lines):
                for c in range(2):
                    turned[pl.ds((2 * p0 + c) * SUB + l, part, stride=6 * SUB), :] = y[p0][
                        c * part : (c + 1) * part, b * LANES : (b + 1) * LANES
                    ]
        yield

    batches = [batch(first) for first in range(0, SUB, BATCH)]
    for stage in range(5):
        for work in batches:
            next(work)
        if early and stage == 0:
            arrange()
    if not early:
        return
    near = outs[0].shape[0] // 2
    acq = lax.axis_index("acq")
    place = lax.axis_index("high") * (2 * near // FAR) + lax.axis_index("low")
    for k, out in enumerate(outs):
        for s in range(2 * near):
            tile = jnp.bitwise_xor(place, s % near + k * near)
            dest = jnp.bitwise_xor(acq, s // near) * 2 * near + spot(tile, 2 * near // FAR)
            value = turned[pl.ds(pl.multiple_of(dest * rows, SUB), rows), :]
            out[s, :, 0] = value.reshape(out.shape[1], out.shape[3], LANES)


def range_call(echo, slant, first, steps, order, halves, early=False):
    length = echo.shape[3]
    outer = length // LANES
    view = echo.reshape(2, -1, SUB, outer, LANES).transpose(0, 1, 3, 2, 4).reshape(2, -1, outer * SUB, LANES)
    tables = [slant, *range_tables(length, order, halves)]
    dests = len(order) * halves
    blocks = outer // dests
    rows = 2 * blocks * SUB
    whole = lambda shape: pl.BlockSpec(shape, lambda s: (0,) * len(shape))
    macs = steps * SUB * length * 2 * (2 * outer + 2 * LANES) * 2 * 3
    outs = 1 + early
    return pl.pallas_call(
        functools.partial(range_kernel, outer, early),
        grid=(steps,),
        in_specs=[pl.BlockSpec((2, 1, outer * SUB, LANES), lambda s: (0, first + s, 0, 0))]
        + [whole(t.shape) for t in tables],
        out_specs=[pl.BlockSpec((dests // outs, blocks, 1, 2 * SUB, LANES), lambda s: (0, 0, s, 0, 0))] * outs,
        scratch_shapes=[
            pltpu.VMEM((2, LANES, LANES), jnp.float32),
            pltpu.VMEM((2, outer, LANES), jnp.float32),
        ]
        + [pltpu.VMEM((dests * rows, LANES), jnp.float32)] * early,
        out_shape=[jax.ShapeDtypeStruct((dests // outs, blocks, steps, 2 * SUB, LANES), jnp.float32)] * outs,
        compiler_params=pltpu.CompilerParams(vmem_limit_bytes=VMEM_LIMIT),
        cost_estimate=pl.CostEstimate(
            flops=2 * macs, bytes_accessed=16 * steps * SUB * length, transcendentals=0
        ),
        name=f"range_compress_{first}",
    )(view, *[jnp.asarray(t) for t in tables])


def pair_kernel(kept_ref, came_ref, *outs):
    for s, out in enumerate(outs):
        out[0] = kept_ref[s, :, 0]
        out[1] = came_ref[s, :, 0]


def pair_call(kept, came):
    count, blocks, _, rows, _ = kept.shape
    vmem = pl.BlockSpec(memory_space=pltpu.VMEM)
    return pl.pallas_call(
        pair_kernel,
        in_specs=[vmem] * 2,
        out_specs=[vmem] * count,
        out_shape=[jax.ShapeDtypeStruct((2, blocks, rows, LANES), jnp.float32)] * count,
        compiler_params=pltpu.CompilerParams(vmem_limit_bytes=VMEM_LIMIT),
        cost_estimate=pl.CostEstimate(flops=10**12, bytes_accessed=4 * kept.size, transcendentals=0),
        name="pair_halves",
    )(kept, came)


def azimuth_tables(length):
    part = length // CLASSES
    f1 = np.arange(part)
    ahead, back = [], []
    first = (length - AOI) // 2
    u, s = np.arange(part // LOOK_AZ), np.arange(LOOK_AZ)
    lines = (first + u[None, :] * LOOK_AZ + s[:, None]).reshape(-1)
    for f0 in range(CLASSES):
        c, s = trig(np.outer(CLASSES * f1 + f0, np.arange(part)), length)
        ahead.append(np.concatenate(high_low(np.block([[c, s], [-s, c]]))))
        c, s = trig(np.outer(lines, CLASSES * f1 + f0), length)
        back.append(np.concatenate(high_low(np.block([[c, -s], [s, c]]) / length)))
    return [np.stack(ahead), np.stack(back)]


def cos_sin(angle):
    y = 0.5 * angle
    z = y * y
    sine = [1.0, -1 / 6, 1 / 120, -1 / 5040, 1 / 362880, -1 / 39916800]
    cosine = [1.0, -1 / 2, 1 / 24, -1 / 720, 1 / 40320, -1 / 3628800, 1 / 479001600]
    s, c = sine[-1], cosine[-1]
    for k in sine[-2::-1]:
        s = s * z + k
    for k in cosine[-2::-1]:
        c = c * z + k
    s = s * y
    return 1.0 - 2.0 * (s * s), 2.0 * (s * c)


def fours(a, b, c, d):
    (ar, ai), (br, bi), (cr, ci), (dr, di) = a, b, c, d
    pr, pi, mr, mi = ar + cr, ai + ci, ar - cr, ai - ci
    qr, qi, nr, ni = br + dr, bi + di, br - dr, bi - di
    return (pr + qr, pi + qi), (mr + ni, mi - nr), (pr - qr, pi - qi), (mr - ni, mi + nr)


def class_of(e, g):
    return (4 * e + 9 * g) % CLASSES


def focus(xr, xi, phases, tables):
    fw, bw = tables
    part = xr.shape[0] // CLASSES
    x = [(xr[k * part : (k + 1) * part], xi[k * part : (k + 1) * part]) for k in range(CLASSES)]
    columns = [thirds(*[x[(4 * i + 3 * j) % CLASSES] for i in range(3)], -1.0) for j in range(4)]
    classes = [None] * CLASSES
    for e in range(3):
        for g, pair in enumerate(fours(*[columns[j][e] for j in range(4)])):
            classes[class_of(e, g)] = pair
    z, forward = [], []
    for f0 in range(CLASSES + 1):
        if f0 < CLASSES:
            forward.append(dot_parts(fw[f0], jnp.concatenate(classes[f0], axis=0)))
        if f0 > 0:
            y, k = forward[f0 - 1], f0 - 1
            dr, di = y[:part], y[part:]
            pc, ps = phases(k)
            e = jnp.concatenate([dr * pc - di * ps, dr * ps + di * pc], axis=0)
            y = dot_parts(bw[k], e)
            z.append((y[:part], y[part:]))
    sums = [fours(*[z[class_of(e, g)] for g in range(4)]) for e in range(3)]
    outs = []
    for h in range(AOI // part):
        terms = [sums[e][h] for e in range(3)]
        outs.append(thirds(*terms, 1.0)[h % 3])
    return [jnp.concatenate([pair[c] for pair in outs], axis=0) for c in range(2)]


def looked_at(field, look):
    lines = AOI // 4 // LOOK_AZ
    groups = [field[k * lines : (k + 1) * lines] for k in range(AOI // lines)]
    added = [groups[k] + groups[k + 1] for k in range(0, len(groups), LOOK_AZ)]
    high, low = split(jnp.concatenate(added, axis=0))
    return dot(high, look) + dot(low, look)


def joint_kernel(order, rounds, me_ref, same_ref, x_ref, early_ref, own_angle, other_angle, fw, bw, look_ref, out, stage, looked):
    acq = me_ref[0]
    tiles = len(order)
    near = tiles // 2
    firsts = [acq * tiles, (1 - acq) * tiles]
    for part in range(2):
        for k, first in enumerate(firsts):
            lanes = slice(k * LANES, (k + 1) * LANES)
            for place, t in enumerate(order):
                stage[part, t, 1:, :, lanes] = x_ref[first + place, 0, :, part * SUB : (part + 1) * SUB, :]
            for s in range(near):
                for side in range(2):
                    tile = jnp.bitwise_xor(me_ref[1], s + side * near)
                    stage[part, tile, 0, :, lanes] = early_ref[k * near + s, side, 0, part * SUB : (part + 1) * SUB, :]
    xr, xi = [stage[part].reshape(-1, 2 * LANES) for part in range(2)]
    rows_of = lambda k: pl.ds(k, own_angle.shape[0] // CLASSES, stride=CLASSES)
    phases = lambda k: cos_sin(jnp.concatenate([a[rows_of(k), :] for a in (own_angle, other_angle)], axis=1))
    fr, fi = focus(xr, xi, phases, [fw, bw])
    mr, mi, pr, pi = fr[:, :LANES], fi[:, :LANES], fr[:, LANES:], fi[:, LANES:]
    look = look_ref[0]
    cross_real = looked_at(mr * pr + mi * pi, look[0])
    cross_imag = looked_at(mi * pr - mr * pi, look[1])
    own_real = looked_at(mr * mr + mi * mi, look[0])
    own_imag = looked_at(mi * mr - mr * mi, look[1])
    other_real = looked_at(pr * pr + pi * pi, look[0])
    other_imag = looked_at(pi * pr - pr * pi, look[1])
    block = pl.program_id(0)

    @pl.when(block == 0)
    def _():
        looked[...] = jnp.zeros_like(looked)

    for r in range(rounds):
        same = same_ref[r] != 0
        looked[0, r] += jnp.where(same, own_real + own_imag, cross_real + cross_imag)
        looked[1, r] += jnp.where(same, other_real + other_imag, cross_real - cross_imag)

    @pl.when(block == pl.num_programs(0) - 1)
    def _():
        for k, first in enumerate(firsts):
            groups = pack(looked[k, 0], looked[k, 1])
            for place, t in enumerate(order):
                for j, (value, at) in enumerate(groups):
                    out[first + place, j] = value[t * SUB + at : t * SUB + at + SUB // 2]


def pack(even, odd):
    half = SUB // 2
    free = lax.broadcasted_iota(jnp.int32, even.shape, 1) >= USED
    rest = [pltpu.roll(odd, (USED - SPARE * j) % LANES, 1) for j in range(3)]
    up = lambda value: pltpu.roll(value, value.shape[0] - half, 0)
    return (
        (jnp.where(free, up(rest[0]), even), 0),
        (jnp.where(free, rest[1], even), half),
        (jnp.where(free, up(rest[2]), odd), 0),
    )


def unpack(parts):
    lane = lax.broadcasted_iota(jnp.int32, parts[0].shape, 1)
    rest = [pltpu.roll(part, (SPARE * j - USED) % LANES, 1) for j, part in enumerate(parts)]
    last = jnp.where(lane < SPARE, rest[0], jnp.where(lane < 2 * SPARE, rest[1], rest[2]))
    return jnp.concatenate([parts[0], parts[1], parts[2], last], axis=0)


def joint_call(me, same, array, early, angle, other_angle, tables, order):
    dests, blocks, steps = array.shape[:3]
    tiles = len(order)
    lines = angle.shape[0]
    rounds = same.shape[0]
    wide = blocks * LANES // LOOK_RG
    look = np.stack(
        [
            np.stack([look_table(LANES, c * wide + b * LANES // LOOK_RG) for c in range(2)])
            for b in range(blocks)
        ]
    )
    return pl.pallas_call(
        functools.partial(joint_kernel, order, rounds),
        grid_spec=pltpu.PrefetchScalarGridSpec(
            num_scalar_prefetch=2,
            grid=(blocks,),
            in_specs=[
                pl.BlockSpec((dests, 1) + array.shape[2:], lambda b, me, same: (0, b, 0, 0, 0)),
                pl.BlockSpec(early.shape[:2] + (1,) + early.shape[3:], lambda b, me, same: (0, 0, b, 0, 0)),
                pl.BlockSpec((lines, LANES), lambda b, me, same: (0, me[0] * blocks + b)),
                pl.BlockSpec((lines, LANES), lambda b, me, same: (0, b)),
                *[pl.BlockSpec(t.shape, lambda b, me, same: (0, 0, 0)) for t in tables],
                pl.BlockSpec((1,) + look.shape[1:], lambda b, me, same: (b, 0, 0, 0)),
            ],
            out_specs=pl.BlockSpec((dests, 3, SUB // 2, LANES), lambda b, me, same: (0, 0, 0, 0)),
            scratch_shapes=[
                pltpu.VMEM((2, tiles, steps + 1, SUB, 2 * LANES), jnp.float32),
                pltpu.VMEM((2, rounds, AOI // LOOK_AZ, LANES), jnp.float32),
            ],
        ),
        out_shape=jax.ShapeDtypeStruct((dests, 3, SUB // 2, LANES), jnp.float32),
        compiler_params=pltpu.CompilerParams(vmem_limit_bytes=VMEM_LIMIT),
        cost_estimate=pl.CostEstimate(
            flops=2 * 2 * 3 * 6 * 256 * 256 * 2 * LANES * blocks,
            bytes_accessed=20 * lines * 2 * LANES * blocks,
            transcendentals=0,
        ),
        name="azimuth_interferogram",
    )(me, same, array, early, angle, other_angle, *[jnp.asarray(t) for t in tables], jnp.asarray(look))


def single_kernel(tiles, x_ref, angle_ref, fw, bw, out):
    xr, xi = [x_ref[:, 0, :, part * SUB : (part + 1) * SUB, :].reshape(-1, LANES) for part in range(2)]
    fr, fi = focus(xr, xi, lambda k: cos_sin(angle_ref[pl.ds(k, angle_ref.shape[0] // CLASSES, stride=CLASSES), :]), [fw, bw])
    out[:AOI] = fr
    out[AOI:] = fi


def single_call(array, angle, tables):
    tiles = array.shape[0]
    lines, columns = angle.shape
    return pl.pallas_call(
        functools.partial(single_kernel, tiles),
        grid=(columns // LANES,),
        in_specs=[
            pl.BlockSpec((tiles, 1) + array.shape[2:], lambda b: (0, b, 0, 0, 0)),
            pl.BlockSpec((lines, LANES), lambda b: (0, b)),
        ]
        + [pl.BlockSpec(t.shape, lambda b: (0, 0, 0)) for t in tables],
        out_specs=pl.BlockSpec((2 * AOI, LANES), lambda b: (0, b)),
        out_shape=jax.ShapeDtypeStruct((2 * AOI, columns), jnp.float32),
        compiler_params=pltpu.CompilerParams(vmem_limit_bytes=VMEM_LIMIT),
        name="azimuth_focus",
    )(array, angle, *[jnp.asarray(t) for t in tables])


def look_table(width, offset):
    table = np.zeros((width, LANES), np.float64)
    table[np.arange(width), offset + np.arange(width) // LOOK_RG] = 1.0 / (LOOK_AZ * LOOK_RG)
    return table.astype(ml_dtypes.bfloat16)


def cross_kernel(rounds, tiles, mine_ref, *refs):
    partner_refs, look_ref, out = refs[:rounds], refs[-2], refs[-1]
    mr, mi = mine_ref[:AOI], mine_ref[AOI:]
    per = AOI // LOOK_AZ // tiles
    for r in range(rounds):
        pr, pi = partner_refs[r][:AOI], partner_refs[r][AOI:]
        for c, field in enumerate((mr * pr + mi * pi, mi * pr - mr * pi)):
            looked = looked_at(field, look_ref[...])
            at = (c * rounds + r) * per
            for t in range(tiles):
                out[t, at : at + per, :] = looked[t * per : (t + 1) * per]


def cross_call(mine, partners, tiles):
    rounds = len(partners)
    width = mine.shape[1]
    look = jnp.asarray(look_table(width, 0))
    shape = (tiles, 2 * rounds * (AOI // LOOK_AZ // tiles), LANES)
    vmem = lambda: pl.BlockSpec(memory_space=pltpu.VMEM)
    return pl.pallas_call(
        functools.partial(cross_kernel, rounds, tiles),
        in_specs=[vmem() for _ in range(rounds + 2)],
        out_specs=vmem(),
        out_shape=jax.ShapeDtypeStruct(shape, jnp.float32),
        compiler_params=pltpu.CompilerParams(vmem_limit_bytes=VMEM_LIMIT),
        name="interferogram",
    )(mine, *partners, look)


def place_kernel(sources, valid, parts, in_ref, out):
    if in_ref.shape[1:] == (3, SUB // 2, LANES):
        values = {k: unpack([in_ref[k, j] for j in range(3)]) for k in sources}
    else:
        values = {k: in_ref[k] for k in sources}
    rows = values[sources[0]].shape[0]
    lane = lax.broadcasted_iota(jnp.int32, (rows, LANES), 1)
    for c in range(parts):
        for o in range(len(sources) * valid // LANES):
            acc = None
            for place, source in enumerate(sources):
                shift = place * valid - o * LANES
                if shift + valid <= 0 or shift >= LANES:
                    continue
                value = values[source]
                turn_by = (shift - c * valid) % LANES
                if turn_by:
                    value = pltpu.roll(value, turn_by, 1)
                acc = value if acc is None else jnp.where(lane >= shift, value, acc)
            out[c * rows : (c + 1) * rows, o * LANES : (o + 1) * LANES] = acc


def place_call(received, rows, sources, valid, parts):
    return pl.pallas_call(
        functools.partial(place_kernel, sources, valid, parts),
        in_specs=[pl.BlockSpec(memory_space=pltpu.VMEM)],
        out_specs=pl.BlockSpec(memory_space=pltpu.VMEM),
        out_shape=jax.ShapeDtypeStruct((parts * rows, len(sources) * valid), jnp.float32),
        compiler_params=pltpu.CompilerParams(vmem_limit_bytes=VMEM_LIMIT),
        name="place_samples",
    )(received)


def turn(array, axes):
    return lax.all_to_all(array, axes, split_axis=0, concat_axis=0, tiled=True)


def joint(tiles, echo, slant, angle, pairs):
    steps = echo.shape[2] // SUB
    columns = angle.shape[1]
    rounds = pairs.shape[0]
    acq = lax.axis_index("acq")
    same = (lax.dynamic_index_in_dim(pairs, acq, 1, keepdims=False) == acq).astype(jnp.int32)
    theirs = lax.dynamic_slice_in_dim(angle, (1 - acq) * (columns // 2), columns // 2, 1)
    other_angle = lax.ppermute(theirs, "acq", [(0, 1), (1, 0)])
    low = lax.axis_size("low")
    order = [h * low + k for k in range(low) for h in range(tiles // low)]
    axes = ("acq", "low", "high")
    tile = lax.axis_index("high") * low + lax.axis_index("low")
    me = jnp.stack([acq, tile]).astype(jnp.int32)
    kept, given = range_call(echo, slant, 0, 1, order, 2, early=True)
    came = lax.ppermute(given, "high", [(h, h ^ (FAR // 2)) for h in range(FAR)])
    (sent,) = range_call(echo, slant, 1, steps - 1, order, 2)
    array = turn(sent, axes)
    early = list(pair_call(kept, came))
    near = tiles // 2
    for s in range(1, tiles):
        flip = s // near * tiles + s % near
        early[s] = lax.ppermute(early[s], ("acq", "high", "low"), [(i, i ^ flip) for i in range(2 * tiles)])
    early = jnp.stack(early)
    looked = joint_call(me, same, array, early, angle, other_angle, azimuth_tables(angle.shape[0]), order)
    sources = [half * tiles + order.index(t) for t in range(tiles) for half in range(2)]
    result = place_call(turn(looked, axes), rounds * SUB, sources, columns // 2 // LOOK_RG, 2)
    return result.reshape(2, rounds, 1, -1, result.shape[1])


def separate(tiles, echo, slant, angle, pairs):
    columns = angle.shape[1]
    rounds = pairs.shape[0]
    (sent,) = range_call(echo, slant, 0, echo.shape[2] // SUB, list(range(tiles)), 1)
    mine = single_call(turn(sent, ("high", "low")), angle, azimuth_tables(angle.shape[0]))
    every = lax.all_gather(mine, "acq", axis=0)
    partner = lax.dynamic_index_in_dim(pairs, lax.axis_index("acq"), 1, keepdims=False)
    partners = [lax.dynamic_index_in_dim(every, partner[r], 0, keepdims=False) for r in range(rounds)]
    looked = turn(cross_call(mine, partners, tiles), ("high", "low"))
    result = place_call(looked, looked.shape[1], list(range(tiles)), columns // LOOK_RG, 1)
    return result.reshape(2, rounds, 1, -1, result.shape[1])


def shards(tiles, acqs, echo, slant, angle, pairs):
    fits = echo.shape[2] > SUB and tiles == FAR * FAR and AOI // LOOK_AZ == tiles * SUB
    fits = fits and angle.shape[2] // LOOK_RG == USED and pairs.shape[0] == 2
    program = joint if acqs == 2 and fits else separate
    return program(tiles, echo, slant, angle[0], pairs)


def solution(mesh):
    acqs, tiles = mesh.shape["acq"], mesh.shape["tile"]
    low = 1 << (tiles.bit_length() // 2)
    low = low if tiles % low == 0 else 1
    split_mesh = jax.sharding.Mesh(mesh.devices.reshape(acqs, tiles // low, low), ("acq", "high", "low"))
    tile = ("high", "low")
    in_specs = (P(None, "acq", tile, None), P(None, "acq", None), P("acq", None, tile), P())
    out_specs = P(None, None, "acq", tile, None)
    body = functools.partial(shards, tiles, acqs)
    return jax.shard_map(body, mesh=split_mesh, in_specs=in_specs, out_specs=out_specs, check_vma=False)
```

```python
import functools
import math

import jax
import jax.numpy as jnp
import ml_dtypes
import numpy as np
from jax import lax
from jax.experimental import pallas as pl
from jax.experimental.pallas import tpu as pltpu
from jax.sharding import PartitionSpec as P

LOOK_AZ = 2
LOOK_RG = 8
AOI = 256
LANES = 128
SUB = 8
FAR = 4
SPARE = 32
USED = LANES - SPARE
CLASSES = 12
BATCH = 4
VMEM_LIMIT = 56 * 1024 * 1024


def high_low(table):
    high = table.astype(ml_dtypes.bfloat16)
    low = (table - high.astype(np.float64)).astype(ml_dtypes.bfloat16)
    return np.stack([high, low])


def trig(product, period):
    angle = (product % period) * (2.0 * math.pi / period)
    return np.cos(angle), np.sin(angle)


def split(value):
    high = value.astype(jnp.bfloat16)
    return high, (value - high.astype(jnp.float32)).astype(jnp.bfloat16)


def dot(left, right):
    return jnp.dot(left, right, preferred_element_type=jnp.float32)


def dot_stacked(table, value):
    high, low = split(value)
    both = dot(table, jnp.concatenate([high, low], axis=0))
    rows = table.shape[0] // 2
    return both[:rows] + both[rows:]


def dot_parts(table, value):
    rows = table.shape[0] // 2
    high, low = table[:rows], table[rows:]
    left = [jnp.concatenate(pair, axis=1) for pair in ((high, high), (low, jnp.zeros_like(low)))]
    return dot_stacked(jnp.concatenate(left, axis=0), value)


def thirds(a, b, c, sign):
    scale = sign * math.sqrt(3.0) / 2.0
    tr, ti = b[0] + c[0], b[1] + c[1]
    vr, vi = (b[0] - c[0]) * scale, (b[1] - c[1]) * scale
    ur, ui = a[0] - 0.5 * tr, a[1] - 0.5 * ti
    return (a[0] + tr, a[1] + ti), (ur - vi, ui + vr), (ur + vi, ui - vr)


def dot_table_right(value, table):
    rows = table.shape[0] // 2
    high_table, low_table = table[:rows], table[rows:]
    high, low = split(value)
    return dot(
        jnp.concatenate([high, low, high], axis=1),
        jnp.concatenate([high_table, high_table, low_table], axis=0),
    )


def stacked(table):
    high, low = high_low(table)
    return np.block([[high, high], [low, np.zeros_like(low)]])


def range_tables(length, order, halves):
    inner = LANES
    outer = length // inner
    part = outer // 3
    k1 = np.arange(outer)
    q = np.arange(inner)
    inside = np.arange(part)
    per_tile = outer // len(order)
    blocks = per_tile // halves
    a1, a4 = [], []
    for p0 in range(3):
        c, s = trig(np.outer(inside, 3 * inside + p0), outer)
        a1.append(stacked(np.block([[c, s], [-s, c]])))
        c, s = trig(np.outer(3 * inside + p0, inside), outer)
        rows = [
            cc * part + (t * per_tile + half * blocks) // 3 + b
            for cc in range(2)
            for half in range(halves)
            for t in order
            for b in range(blocks // 3)
        ]
        a4.append(stacked(np.block([[c, -s], [s, c]])[np.array(rows)] / length))
    c2, s2 = trig(np.outer(q, q), inner)
    b2 = np.block([[c2, -s2], [s2, c2]])
    ct, st = trig(np.outer(k1, q), length)
    twiddle = np.stack([ct, st]).astype(np.float32)
    b2 = np.concatenate(high_low(b2))
    return np.stack(a1), b2, np.stack(a4), twiddle


def range_kernel(outer, early, x_ref, slant_ref, a1_ref, b2_ref, a4_ref, t_ref, *rest):
    outs, (rows_ref, h_ref), held = rest[: 1 + early], rest[1 + early : 3 + early], rest[3 + early :]
    part = outer // 3

    @pl.when(pl.program_id(0) == 0)
    def _():
        for c in range(2):
            for k2 in range(LANES):
                rows_ref[c, k2 : k2 + 1, :outer] = slant_ref[c, :, k2 * outer : (k2 + 1) * outer]
            h_ref[c] = rows_ref[c].T[:outer]

    rows = outs[0].shape[1] * outs[0].shape[3]
    turned = held[0] if early else outs[0].reshape(outs[0].shape[0] * rows, LANES)
    ct, st = t_ref[0], t_ref[1]
    hr, hi = h_ref[0], h_ref[1]

    def batch(first):
        lines = range(first, first + BATCH)
        y = []
        for p0 in range(3):
            x = [
                jnp.concatenate(
                    [x_ref[c, 0, pl.ds(p0 * SUB + l, part, stride=3 * SUB), :] for c in range(2)], axis=0
                )
                for l in lines
            ]
            value = dot_stacked(a1_ref[p0], jnp.concatenate(x, axis=1))
            y.append((value[:part], value[part:]))
        yield
        y = thirds(*y, -1.0)
        z = []
        for b in range(BATCH):
            yr, yi = [
                jnp.concatenate([v[c][:, b * LANES : (b + 1) * LANES] for v in y], axis=0) for c in range(2)
            ]
            z.append(jnp.concatenate([yr * ct + yi * st, yi * ct - yr * st], axis=1))
        y = dot_table_right(jnp.concatenate(z, axis=0), b2_ref[...])
        yield
        z = []
        for b in range(BATCH):
            yr = y[b * outer : (b + 1) * outer, :LANES]
            yi = y[b * outer : (b + 1) * outer, LANES:]
            z.append(jnp.concatenate([yr * hr - yi * hi, -yr * hi - yi * hr], axis=1))
        y = dot_table_right(jnp.concatenate(z, axis=0), b2_ref[...])
        yield
        z = []
        for b in range(BATCH):
            yr = y[b * outer : (b + 1) * outer, :LANES]
            yi = y[b * outer : (b + 1) * outer, LANES:]
            zr, zi = yr * ct + yi * st, yr * st - yi * ct
            z.append(thirds(*[(zr[k * part : (k + 1) * part], zi[k * part : (k + 1) * part]) for k in range(3)], 1.0))
        y = []
        for p0 in range(3):
            value = jnp.concatenate([jnp.concatenate(z[b][p0], axis=0) for b in range(BATCH)], axis=1)
            y.append(dot_stacked(a4_ref[p0], value))
        yield
        for p0 in range(3):
            for b, l in enumerate(lines):
                for c in range(2):
                    turned[pl.ds((2 * p0 + c) * SUB + l, part, stride=6 * SUB), :] = y[p0][
                        c * part : (c + 1) * part, b * LANES : (b + 1) * LANES
                    ]
        yield

    batches = [batch(first) for first in range(0, SUB, BATCH)]
    for _ in range(5):
        for work in batches:
            next(work)
    if not early:
        return
    near = outs[0].shape[0] // 2
    acq = lax.axis_index("acq")
    place = lax.axis_index("high") * (2 * near // FAR) + lax.axis_index("low")
    for k, out in enumerate(outs):
        for s in range(2 * near):
            tile = jnp.bitwise_xor(place, s % near + k * near)
            dest = jnp.bitwise_xor(acq, s // near) * 2 * near + tile
            value = turned[pl.ds(pl.multiple_of(dest * rows, SUB), rows), :]
            out[s, :, 0] = value.reshape(out.shape[1], out.shape[3], LANES)


def range_call(echo, slant, first, steps, order, halves, early=False):
    length = echo.shape[3]
    outer = length // LANES
    view = echo.reshape(2, -1, SUB, outer, LANES).transpose(0, 1, 3, 2, 4).reshape(2, -1, outer * SUB, LANES)
    tables = [slant, *range_tables(length, order, halves)]
    dests = len(order) * halves
    blocks = outer // dests
    rows = 2 * blocks * SUB
    whole = lambda shape: pl.BlockSpec(shape, lambda s: (0,) * len(shape))
    macs = steps * SUB * length * 2 * (2 * outer + 2 * LANES) * 2 * 3
    outs = 1 + early
    return pl.pallas_call(
        functools.partial(range_kernel, outer, early),
        grid=(steps,),
        in_specs=[pl.BlockSpec((2, 1, outer * SUB, LANES), lambda s: (0, first + s, 0, 0))]
        + [whole(t.shape) for t in tables],
        out_specs=[pl.BlockSpec((dests // outs, blocks, 1, 2 * SUB, LANES), lambda s: (0, 0, s, 0, 0))] * outs,
        scratch_shapes=[
            pltpu.VMEM((2, LANES, LANES), jnp.float32),
            pltpu.VMEM((2, outer, LANES), jnp.float32),
        ]
        + [pltpu.VMEM((dests * rows, LANES), jnp.float32)] * early,
        out_shape=[jax.ShapeDtypeStruct((dests // outs, blocks, steps, 2 * SUB, LANES), jnp.float32)] * outs,
        compiler_params=pltpu.CompilerParams(vmem_limit_bytes=VMEM_LIMIT),
        cost_estimate=pl.CostEstimate(
            flops=2 * macs, bytes_accessed=16 * steps * SUB * length, transcendentals=0
        ),
        name=f"range_compress_{first}",
    )(view, *[jnp.asarray(t) for t in tables])


def pair_kernel(kept_ref, came_ref, *outs):
    for s, out in enumerate(outs):
        out[0] = kept_ref[s, :, 0]
        out[1] = came_ref[s, :, 0]


def pair_call(kept, came):
    count, blocks, _, rows, _ = kept.shape
    vmem = pl.BlockSpec(memory_space=pltpu.VMEM)
    return pl.pallas_call(
        pair_kernel,
        in_specs=[vmem] * 2,
        out_specs=[vmem] * count,
        out_shape=[jax.ShapeDtypeStruct((2, blocks, rows, LANES), jnp.float32)] * count,
        compiler_params=pltpu.CompilerParams(vmem_limit_bytes=VMEM_LIMIT),
        cost_estimate=pl.CostEstimate(flops=10**12, bytes_accessed=4 * kept.size, transcendentals=0),
        name="pair_halves",
    )(kept, came)


def azimuth_tables(length):
    part = length // CLASSES
    f1 = np.arange(part)
    ahead, back = [], []
    first = (length - AOI) // 2
    u, s = np.arange(part // LOOK_AZ), np.arange(LOOK_AZ)
    lines = (first + u[None, :] * LOOK_AZ + s[:, None]).reshape(-1)
    for f0 in range(CLASSES):
        c, s = trig(np.outer(CLASSES * f1 + f0, np.arange(part)), length)
        ahead.append(np.concatenate(high_low(np.block([[c, s], [-s, c]]))))
        c, s = trig(np.outer(lines, CLASSES * f1 + f0), length)
        back.append(np.concatenate(high_low(np.block([[c, -s], [s, c]]) / length)))
    return [np.stack(ahead), np.stack(back)]


def cos_sin(angle):
    y = 0.5 * angle
    z = y * y
    sine = [1.0, -1 / 6, 1 / 120, -1 / 5040, 1 / 362880, -1 / 39916800]
    cosine = [1.0, -1 / 2, 1 / 24, -1 / 720, 1 / 40320, -1 / 3628800, 1 / 479001600]
    s, c = sine[-1], cosine[-1]
    for k in sine[-2::-1]:
        s = s * z + k
    for k in cosine[-2::-1]:
        c = c * z + k
    s = s * y
    return 1.0 - 2.0 * (s * s), 2.0 * (s * c)


def fours(a, b, c, d):
    (ar, ai), (br, bi), (cr, ci), (dr, di) = a, b, c, d
    pr, pi, mr, mi = ar + cr, ai + ci, ar - cr, ai - ci
    qr, qi, nr, ni = br + dr, bi + di, br - dr, bi - di
    return (pr + qr, pi + qi), (mr + ni, mi - nr), (pr - qr, pi - qi), (mr - ni, mi + nr)


def class_of(e, g):
    return (4 * e + 9 * g) % CLASSES


def focus(xr, xi, phases, tables):
    fw, bw = tables
    part = xr.shape[0] // CLASSES
    x = [(xr[k * part : (k + 1) * part], xi[k * part : (k + 1) * part]) for k in range(CLASSES)]
    columns = [thirds(*[x[(4 * i + 3 * j) % CLASSES] for i in range(3)], -1.0) for j in range(4)]
    classes = [None] * CLASSES
    for e in range(3):
        for g, pair in enumerate(fours(*[columns[j][e] for j in range(4)])):
            classes[class_of(e, g)] = pair
    z, forward = [], []
    for f0 in range(CLASSES + 1):
        if f0 < CLASSES:
            forward.append(dot_parts(fw[f0], jnp.concatenate(classes[f0], axis=0)))
        if f0 > 0:
            y, k = forward[f0 - 1], f0 - 1
            dr, di = y[:part], y[part:]
            pc, ps = phases(k)
            e = jnp.concatenate([dr * pc - di * ps, dr * ps + di * pc], axis=0)
            y = dot_parts(bw[k], e)
            z.append((y[:part], y[part:]))
    sums = [fours(*[z[class_of(e, g)] for g in range(4)]) for e in range(3)]
    outs = []
    for h in range(AOI // part):
        terms = [sums[e][h] for e in range(3)]
        outs.append(thirds(*terms, 1.0)[h % 3])
    return [jnp.concatenate([pair[c] for pair in outs], axis=0) for c in range(2)]


def looked_at(field, look):
    lines = AOI // 4 // LOOK_AZ
    groups = [field[k * lines : (k + 1) * lines] for k in range(AOI // lines)]
    added = [groups[k] + groups[k + 1] for k in range(0, len(groups), LOOK_AZ)]
    high, low = split(jnp.concatenate(added, axis=0))
    return dot(high, look) + dot(low, look)


def joint_kernel(order, rounds, me_ref, same_ref, x_ref, early_ref, own_angle, other_angle, fw, bw, look_ref, out, stage, looked):
    acq = me_ref[0]
    tiles = len(order)
    near = tiles // 2
    firsts = [acq * tiles, (1 - acq) * tiles]
    for part in range(2):
        for k, first in enumerate(firsts):
            lanes = slice(k * LANES, (k + 1) * LANES)
            for place, t in enumerate(order):
                stage[part, t, 1:, :, lanes] = x_ref[first + place, 0, :, part * SUB : (part + 1) * SUB, :]
            for s in range(near):
                for side in range(2):
                    tile = jnp.bitwise_xor(me_ref[1], s + side * near)
                    stage[part, tile, 0, :, lanes] = early_ref[k * near + s, side, 0, part * SUB : (part + 1) * SUB, :]
    xr, xi = [stage[part].reshape(-1, 2 * LANES) for part in range(2)]
    rows_of = lambda k: pl.ds(k, own_angle.shape[0] // CLASSES, stride=CLASSES)
    phases = lambda k: cos_sin(jnp.concatenate([a[rows_of(k), :] for a in (own_angle, other_angle)], axis=1))
    fr, fi = focus(xr, xi, phases, [fw, bw])
    mr, mi, pr, pi = fr[:, :LANES], fi[:, :LANES], fr[:, LANES:], fi[:, LANES:]
    look = look_ref[0]
    cross_real = looked_at(mr * pr + mi * pi, look[0])
    cross_imag = looked_at(mi * pr - mr * pi, look[1])
    own_real = looked_at(mr * mr + mi * mi, look[0])
    own_imag = looked_at(mi * mr - mr * mi, look[1])
    other_real = looked_at(pr * pr + pi * pi, look[0])
    other_imag = looked_at(pi * pr - pr * pi, look[1])
    block = pl.program_id(0)

    @pl.when(block == 0)
    def _():
        looked[...] = jnp.zeros_like(looked)

    for r in range(rounds):
        same = same_ref[r] != 0
        looked[0, r] += jnp.where(same, own_real + own_imag, cross_real + cross_imag)
        looked[1, r] += jnp.where(same, other_real + other_imag, cross_real - cross_imag)

    @pl.when(block == pl.num_programs(0) - 1)
    def _():
        for k, first in enumerate(firsts):
            groups = pack(looked[k, 0], looked[k, 1])
            for place, t in enumerate(order):
                for j, (value, at) in enumerate(groups):
                    out[first + place, j] = value[t * SUB + at : t * SUB + at + SUB // 2]


def pack(even, odd):
    half = SUB // 2
    free = lax.broadcasted_iota(jnp.int32, even.shape, 1) >= USED
    rest = [pltpu.roll(odd, (USED - SPARE * j) % LANES, 1) for j in range(3)]
    up = lambda value: pltpu.roll(value, value.shape[0] - half, 0)
    return (
        (jnp.where(free, up(rest[0]), even), 0),
        (jnp.where(free, rest[1], even), half),
        (jnp.where(free, up(rest[2]), odd), 0),
    )


def unpack(parts):
    lane = lax.broadcasted_iota(jnp.int32, parts[0].shape, 1)
    rest = [pltpu.roll(part, (SPARE * j - USED) % LANES, 1) for j, part in enumerate(parts)]
    last = jnp.where(lane < SPARE, rest[0], jnp.where(lane < 2 * SPARE, rest[1], rest[2]))
    return jnp.concatenate([parts[0], parts[1], parts[2], last], axis=0)


def joint_call(me, same, array, early, angle, other_angle, tables, order):
    dests, blocks, steps = array.shape[:3]
    tiles = len(order)
    lines = angle.shape[0]
    rounds = same.shape[0]
    wide = blocks * LANES // LOOK_RG
    look = np.stack(
        [
            np.stack([look_table(LANES, c * wide + b * LANES // LOOK_RG) for c in range(2)])
            for b in range(blocks)
        ]
    )
    return pl.pallas_call(
        functools.partial(joint_kernel, order, rounds),
        grid_spec=pltpu.PrefetchScalarGridSpec(
            num_scalar_prefetch=2,
            grid=(blocks,),
            in_specs=[
                pl.BlockSpec((dests, 1) + array.shape[2:], lambda b, me, same: (0, b, 0, 0, 0)),
                pl.BlockSpec(early.shape[:2] + (1,) + early.shape[3:], lambda b, me, same: (0, 0, b, 0, 0)),
                pl.BlockSpec((lines, LANES), lambda b, me, same: (0, me[0] * blocks + b)),
                pl.BlockSpec((lines, LANES), lambda b, me, same: (0, b)),
                *[pl.BlockSpec(t.shape, lambda b, me, same: (0, 0, 0)) for t in tables],
                pl.BlockSpec((1,) + look.shape[1:], lambda b, me, same: (b, 0, 0, 0)),
            ],
            out_specs=pl.BlockSpec((dests, 3, SUB // 2, LANES), lambda b, me, same: (0, 0, 0, 0)),
            scratch_shapes=[
                pltpu.VMEM((2, tiles, steps + 1, SUB, 2 * LANES), jnp.float32),
                pltpu.VMEM((2, rounds, AOI // LOOK_AZ, LANES), jnp.float32),
            ],
        ),
        out_shape=jax.ShapeDtypeStruct((dests, 3, SUB // 2, LANES), jnp.float32),
        compiler_params=pltpu.CompilerParams(vmem_limit_bytes=VMEM_LIMIT),
        cost_estimate=pl.CostEstimate(
            flops=2 * 2 * 3 * 6 * 256 * 256 * 2 * LANES * blocks,
            bytes_accessed=20 * lines * 2 * LANES * blocks,
            transcendentals=0,
        ),
        name="azimuth_interferogram",
    )(me, same, array, early, angle, other_angle, *[jnp.asarray(t) for t in tables], jnp.asarray(look))


def single_kernel(tiles, x_ref, angle_ref, fw, bw, out):
    xr, xi = [x_ref[:, 0, :, part * SUB : (part + 1) * SUB, :].reshape(-1, LANES) for part in range(2)]
    fr, fi = focus(xr, xi, lambda k: cos_sin(angle_ref[pl.ds(k, angle_ref.shape[0] // CLASSES, stride=CLASSES), :]), [fw, bw])
    out[:AOI] = fr
    out[AOI:] = fi


def single_call(array, angle, tables):
    tiles = array.shape[0]
    lines, columns = angle.shape
    return pl.pallas_call(
        functools.partial(single_kernel, tiles),
        grid=(columns // LANES,),
        in_specs=[
            pl.BlockSpec((tiles, 1) + array.shape[2:], lambda b: (0, b, 0, 0, 0)),
            pl.BlockSpec((lines, LANES), lambda b: (0, b)),
        ]
        + [pl.BlockSpec(t.shape, lambda b: (0, 0, 0)) for t in tables],
        out_specs=pl.BlockSpec((2 * AOI, LANES), lambda b: (0, b)),
        out_shape=jax.ShapeDtypeStruct((2 * AOI, columns), jnp.float32),
        compiler_params=pltpu.CompilerParams(vmem_limit_bytes=VMEM_LIMIT),
        name="azimuth_focus",
    )(array, angle, *[jnp.asarray(t) for t in tables])


def look_table(width, offset):
    table = np.zeros((width, LANES), np.float64)
    table[np.arange(width), offset + np.arange(width) // LOOK_RG] = 1.0 / (LOOK_AZ * LOOK_RG)
    return table.astype(ml_dtypes.bfloat16)


def cross_kernel(rounds, tiles, mine_ref, *refs):
    partner_refs, look_ref, out = refs[:rounds], refs[-2], refs[-1]
    mr, mi = mine_ref[:AOI], mine_ref[AOI:]
    per = AOI // LOOK_AZ // tiles
    for r in range(rounds):
        pr, pi = partner_refs[r][:AOI], partner_refs[r][AOI:]
        for c, field in enumerate((mr * pr + mi * pi, mi * pr - mr * pi)):
            looked = looked_at(field, look_ref[...])
            at = (c * rounds + r) * per
            for t in range(tiles):
                out[t, at : at + per, :] = looked[t * per : (t + 1) * per]


def cross_call(mine, partners, tiles):
    rounds = len(partners)
    width = mine.shape[1]
    look = jnp.asarray(look_table(width, 0))
    shape = (tiles, 2 * rounds * (AOI // LOOK_AZ // tiles), LANES)
    vmem = lambda: pl.BlockSpec(memory_space=pltpu.VMEM)
    return pl.pallas_call(
        functools.partial(cross_kernel, rounds, tiles),
        in_specs=[vmem() for _ in range(rounds + 2)],
        out_specs=vmem(),
        out_shape=jax.ShapeDtypeStruct(shape, jnp.float32),
        compiler_params=pltpu.CompilerParams(vmem_limit_bytes=VMEM_LIMIT),
        name="interferogram",
    )(mine, *partners, look)


def place_kernel(sources, valid, parts, in_ref, out):
    if in_ref.shape[1:] == (3, SUB // 2, LANES):
        values = {k: unpack([in_ref[k, j] for j in range(3)]) for k in sources}
    else:
        values = {k: in_ref[k] for k in sources}
    rows = values[sources[0]].shape[0]
    lane = lax.broadcasted_iota(jnp.int32, (rows, LANES), 1)
    for c in range(parts):
        for o in range(len(sources) * valid // LANES):
            acc = None
            for place, source in enumerate(sources):
                shift = place * valid - o * LANES
                if shift + valid <= 0 or shift >= LANES:
                    continue
                value = values[source]
                turn_by = (shift - c * valid) % LANES
                if turn_by:
                    value = pltpu.roll(value, turn_by, 1)
                acc = value if acc is None else jnp.where(lane >= shift, value, acc)
            out[c * rows : (c + 1) * rows, o * LANES : (o + 1) * LANES] = acc


def place_call(received, rows, sources, valid, parts):
    return pl.pallas_call(
        functools.partial(place_kernel, sources, valid, parts),
        in_specs=[pl.BlockSpec(memory_space=pltpu.VMEM)],
        out_specs=pl.BlockSpec(memory_space=pltpu.VMEM),
        out_shape=jax.ShapeDtypeStruct((parts * rows, len(sources) * valid), jnp.float32),
        compiler_params=pltpu.CompilerParams(vmem_limit_bytes=VMEM_LIMIT),
        name="place_samples",
    )(received)


def turn(array, axes):
    return lax.all_to_all(array, axes, split_axis=0, concat_axis=0, tiled=True)


def joint(tiles, echo, slant, angle, pairs):
    steps = echo.shape[2] // SUB
    columns = angle.shape[1]
    rounds = pairs.shape[0]
    acq = lax.axis_index("acq")
    same = (lax.dynamic_index_in_dim(pairs, acq, 1, keepdims=False) == acq).astype(jnp.int32)
    theirs = lax.dynamic_slice_in_dim(angle, (1 - acq) * (columns // 2), columns // 2, 1)
    other_angle = lax.ppermute(theirs, "acq", [(0, 1), (1, 0)])
    low = lax.axis_size("low")
    order = list(range(tiles))
    axes = ("acq", "high", "low")
    tile = lax.axis_index("high") * low + lax.axis_index("low")
    me = jnp.stack([acq, tile]).astype(jnp.int32)
    kept, given = range_call(echo, slant, 0, 1, order, 2, early=True)
    came = lax.ppermute(given, "high", [(h, h ^ (FAR // 2)) for h in range(FAR)])
    (sent,) = range_call(echo, slant, 1, steps - 1, order, 2)
    array = turn(sent, axes)
    early = list(pair_call(kept, came))
    near = tiles // 2
    for s in range(1, tiles):
        flip = s // near * tiles + s % near
        early[s] = lax.ppermute(early[s], ("acq", "high", "low"), [(i, i ^ flip) for i in range(2 * tiles)])
    early = jnp.stack(early)
    looked = joint_call(me, same, array, early, angle, other_angle, azimuth_tables(angle.shape[0]), order)
    sources = [half * tiles + order.index(t) for t in range(tiles) for half in range(2)]
    result = place_call(turn(looked, axes), rounds * SUB, sources, columns // 2 // LOOK_RG, 2)
    return result.reshape(2, rounds, 1, -1, result.shape[1])


def separate(tiles, echo, slant, angle, pairs):
    columns = angle.shape[1]
    rounds = pairs.shape[0]
    (sent,) = range_call(echo, slant, 0, echo.shape[2] // SUB, list(range(tiles)), 1)
    mine = single_call(turn(sent, ("high", "low")), angle, azimuth_tables(angle.shape[0]))
    every = lax.all_gather(mine, "acq", axis=0)
    partner = lax.dynamic_index_in_dim(pairs, lax.axis_index("acq"), 1, keepdims=False)
    partners = [lax.dynamic_index_in_dim(every, partner[r], 0, keepdims=False) for r in range(rounds)]
    looked = turn(cross_call(mine, partners, tiles), ("high", "low"))
    result = place_call(looked, looked.shape[1], list(range(tiles)), columns // LOOK_RG, 1)
    return result.reshape(2, rounds, 1, -1, result.shape[1])


def shards(tiles, acqs, echo, slant, angle, pairs):
    fits = echo.shape[2] > SUB and tiles == FAR * FAR and AOI // LOOK_AZ == tiles * SUB
    fits = fits and angle.shape[2] // LOOK_RG == USED and pairs.shape[0] == 2
    program = joint if acqs == 2 and fits else separate
    return program(tiles, echo, slant, angle[0], pairs)


def solution(mesh):
    acqs, tiles = mesh.shape["acq"], mesh.shape["tile"]
    low = 1 << (tiles.bit_length() // 2)
    low = low if tiles % low == 0 else 1
    split_mesh = jax.sharding.Mesh(mesh.devices.reshape(acqs, tiles // low, low), ("acq", "high", "low"))
    tile = ("high", "low")
    in_specs = (P(None, "acq", tile, None), P(None, "acq", None), P("acq", None, tile), P())
    out_specs = P(None, None, "acq", tile, None)
    body = functools.partial(shards, tiles, acqs)
    return jax.shard_map(body, mesh=split_mesh, in_specs=in_specs, out_specs=out_specs, check_vma=False)
```

```python
import functools
import math

import jax
import jax.numpy as jnp
import ml_dtypes
import numpy as np
from jax import lax
from jax.experimental import pallas as pl
from jax.experimental.pallas import tpu as pltpu
from jax.sharding import PartitionSpec as P

LOOK_AZ = 2
LOOK_RG = 8
AOI = 256
LANES = 128
SUB = 8
FAR = 4
SPARE = 32
USED = LANES - SPARE
CLASSES = 12
BATCH = 4
VMEM_LIMIT = 56 * 1024 * 1024


def high_low(table):
    high = table.astype(ml_dtypes.bfloat16)
    low = (table - high.astype(np.float64)).astype(ml_dtypes.bfloat16)
    return np.stack([high, low])


def trig(product, period):
    angle = (product % period) * (2.0 * math.pi / period)
    return np.cos(angle), np.sin(angle)


def split(value):
    high = value.astype(jnp.bfloat16)
    return high, (value - high.astype(jnp.float32)).astype(jnp.bfloat16)


def dot(left, right):
    return jnp.dot(left, right, preferred_element_type=jnp.float32)


def dot_stacked(table, value):
    high, low = split(value)
    both = dot(table, jnp.concatenate([high, low], axis=0))
    rows = table.shape[0] // 2
    return both[:rows] + both[rows:]


def dot_parts(table, value):
    rows = table.shape[0] // 2
    high, low = table[:rows], table[rows:]
    left = [jnp.concatenate(pair, axis=1) for pair in ((high, high), (low, jnp.zeros_like(low)))]
    return dot_stacked(jnp.concatenate(left, axis=0), value)


def thirds(a, b, c, sign):
    scale = sign * math.sqrt(3.0) / 2.0
    tr, ti = b[0] + c[0], b[1] + c[1]
    vr, vi = (b[0] - c[0]) * scale, (b[1] - c[1]) * scale
    ur, ui = a[0] - 0.5 * tr, a[1] - 0.5 * ti
    return (a[0] + tr, a[1] + ti), (ur - vi, ui + vr), (ur + vi, ui - vr)


def dot_table_right(value, table):
    rows = table.shape[0] // 2
    high_table, low_table = table[:rows], table[rows:]
    high, low = split(value)
    return dot(
        jnp.concatenate([high, low, high], axis=1),
        jnp.concatenate([high_table, high_table, low_table], axis=0),
    )


def stacked(table):
    high, low = high_low(table)
    return np.block([[high, high], [low, np.zeros_like(low)]])


def range_tables(length, order, halves):
    inner = LANES
    outer = length // inner
    part = outer // 3
    k1 = np.arange(outer)
    q = np.arange(inner)
    inside = np.arange(part)
    per_tile = outer // len(order)
    blocks = per_tile // halves
    a1, a4 = [], []
    for p0 in range(3):
        c, s = trig(np.outer(inside, 3 * inside + p0), outer)
        a1.append(stacked(np.block([[c, s], [-s, c]])))
        c, s = trig(np.outer(3 * inside + p0, inside), outer)
        rows = [
            cc * part + (t * per_tile + half * blocks) // 3 + b
            for cc in range(2)
            for half in range(halves)
            for t in order
            for b in range(blocks // 3)
        ]
        a4.append(stacked(np.block([[c, -s], [s, c]])[np.array(rows)] / length))
    c2, s2 = trig(np.outer(q, q), inner)
    b2 = np.block([[c2, -s2], [s2, c2]])
    ct, st = trig(np.outer(k1, q), length)
    twiddle = np.stack([ct, st]).astype(np.float32)
    b2 = np.concatenate(high_low(b2))
    return np.stack(a1), b2, np.stack(a4), twiddle


def range_kernel(outer, early, x_ref, slant_ref, a1_ref, b2_ref, a4_ref, t_ref, *rest):
    outs, (rows_ref, h_ref), held = rest[: 1 + early], rest[1 + early : 3 + early], rest[3 + early :]
    part = outer // 3

    @pl.when(pl.program_id(0) == 0)
    def _():
        for c in range(2):
            for k2 in range(LANES):
                rows_ref[c, k2 : k2 + 1, :outer] = slant_ref[c, :, k2 * outer : (k2 + 1) * outer]
            h_ref[c] = rows_ref[c].T[:outer]

    rows = outs[0].shape[1] * outs[0].shape[3]
    turned = held[0] if early else outs[0].reshape(outs[0].shape[0] * rows, LANES)
    ct, st = t_ref[0], t_ref[1]
    hr, hi = h_ref[0], h_ref[1]

    def batch(first):
        lines = range(first, first + BATCH)
        y = []
        for p0 in range(3):
            x = [
                jnp.concatenate(
                    [x_ref[c, 0, pl.ds(p0 * SUB + l, part, stride=3 * SUB), :] for c in range(2)], axis=0
                )
                for l in lines
            ]
            value = dot_stacked(a1_ref[p0], jnp.concatenate(x, axis=1))
            y.append((value[:part], value[part:]))
        yield
        y = thirds(*y, -1.0)
        z = []
        for b in range(BATCH):
            yr, yi = [
                jnp.concatenate([v[c][:, b * LANES : (b + 1) * LANES] for v in y], axis=0) for c in range(2)
            ]
            z.append(jnp.concatenate([yr * ct + yi * st, yi * ct - yr * st], axis=1))
        y = dot_table_right(jnp.concatenate(z, axis=0), b2_ref[...])
        yield
        z = []
        for b in range(BATCH):
            yr = y[b * outer : (b + 1) * outer, :LANES]
            yi = y[b * outer : (b + 1) * outer, LANES:]
            z.append(jnp.concatenate([yr * hr - yi * hi, -yr * hi - yi * hr], axis=1))
        y = dot_table_right(jnp.concatenate(z, axis=0), b2_ref[...])
        yield
        z = []
        for b in range(BATCH):
            yr = y[b * outer : (b + 1) * outer, :LANES]
            yi = y[b * outer : (b + 1) * outer, LANES:]
            zr, zi = yr * ct + yi * st, yr * st - yi * ct
            z.append(thirds(*[(zr[k * part : (k + 1) * part], zi[k * part : (k + 1) * part]) for k in range(3)], 1.0))
        y = []
        for p0 in range(3):
            value = jnp.concatenate([jnp.concatenate(z[b][p0], axis=0) for b in range(BATCH)], axis=1)
            y.append(dot_stacked(a4_ref[p0], value))
        yield
        for p0 in range(3):
            for b, l in enumerate(lines):
                for c in range(2):
                    turned[pl.ds((2 * p0 + c) * SUB + l, part, stride=6 * SUB), :] = y[p0][
                        c * part : (c + 1) * part, b * LANES : (b + 1) * LANES
                    ]
        yield

    batches = [batch(first) for first in range(0, SUB, BATCH)]
    for _ in range(5):
        for work in batches:
            next(work)
    if not early:
        return
    near = outs[0].shape[0] // 2
    acq = lax.axis_index("acq")
    place = lax.axis_index("high") * (2 * near // FAR) + lax.axis_index("low")
    for k, out in enumerate(outs):
        for s in range(2 * near):
            tile = jnp.bitwise_xor(place, s % near + k * near)
            dest = jnp.bitwise_xor(acq, s // near) * 2 * near + tile
            value = turned[pl.ds(pl.multiple_of(dest * rows, SUB), rows), :]
            out[s, :, 0] = value.reshape(out.shape[1], out.shape[3], LANES)


def range_call(echo, slant, first, steps, order, halves, early=False):
    length = echo.shape[3]
    outer = length // LANES
    view = echo.reshape(2, -1, SUB, outer, LANES).transpose(0, 1, 3, 2, 4).reshape(2, -1, outer * SUB, LANES)
    tables = [slant, *range_tables(length, order, halves)]
    dests = len(order) * halves
    blocks = outer // dests
    rows = 2 * blocks * SUB
    whole = lambda shape: pl.BlockSpec(shape, lambda s: (0,) * len(shape))
    macs = steps * SUB * length * 2 * (2 * outer + 2 * LANES) * 2 * 3
    outs = 1 + early
    return pl.pallas_call(
        functools.partial(range_kernel, outer, early),
        grid=(steps,),
        in_specs=[pl.BlockSpec((2, 1, outer * SUB, LANES), lambda s: (0, first + s, 0, 0))]
        + [whole(t.shape) for t in tables],
        out_specs=[pl.BlockSpec((dests // outs, blocks, 1, 2 * SUB, LANES), lambda s: (0, 0, s, 0, 0))] * outs,
        scratch_shapes=[
            pltpu.VMEM((2, LANES, LANES), jnp.float32),
            pltpu.VMEM((2, outer, LANES), jnp.float32),
        ]
        + [pltpu.VMEM((dests * rows, LANES), jnp.float32)] * early,
        out_shape=[jax.ShapeDtypeStruct((dests // outs, blocks, steps, 2 * SUB, LANES), jnp.float32)] * outs,
        compiler_params=pltpu.CompilerParams(vmem_limit_bytes=VMEM_LIMIT),
        cost_estimate=pl.CostEstimate(
            flops=2 * macs, bytes_accessed=16 * steps * SUB * length, transcendentals=0
        ),
        name=f"range_compress_{first}",
    )(view, *[jnp.asarray(t) for t in tables])


def pair_kernel(kept_ref, came_ref, *outs):
    for s, out in enumerate(outs):
        out[0] = kept_ref[s, :, 0]
        out[1] = came_ref[s, :, 0]


def pair_call(kept, came):
    count, blocks, _, rows, _ = kept.shape
    vmem = pl.BlockSpec(memory_space=pltpu.VMEM)
    return pl.pallas_call(
        pair_kernel,
        in_specs=[vmem] * 2,
        out_specs=[vmem] * count,
        out_shape=[jax.ShapeDtypeStruct((2, blocks, rows, LANES), jnp.float32)] * count,
        compiler_params=pltpu.CompilerParams(vmem_limit_bytes=VMEM_LIMIT),
        cost_estimate=pl.CostEstimate(flops=10**12, bytes_accessed=4 * kept.size, transcendentals=0),
        name="pair_halves",
    )(kept, came)


def azimuth_tables(length):
    part = length // CLASSES
    f1 = np.arange(part)
    ahead, back = [], []
    first = (length - AOI) // 2
    u, s = np.arange(part // LOOK_AZ), np.arange(LOOK_AZ)
    lines = (first + u[None, :] * LOOK_AZ + s[:, None]).reshape(-1)
    for f0 in range(CLASSES):
        c, s = trig(np.outer(CLASSES * f1 + f0, np.arange(part)), length)
        ahead.append(np.concatenate(high_low(np.block([[c, s], [-s, c]]))))
        c, s = trig(np.outer(lines, CLASSES * f1 + f0), length)
        back.append(np.concatenate(high_low(np.block([[c, -s], [s, c]]) / length)))
    return [np.stack(ahead), np.stack(back)]


def cos_sin(angle):
    y = 0.5 * angle
    z = y * y
    sine = [1.0, -1 / 6, 1 / 120, -1 / 5040, 1 / 362880, -1 / 39916800]
    cosine = [1.0, -1 / 2, 1 / 24, -1 / 720, 1 / 40320, -1 / 3628800, 1 / 479001600]
    s, c = sine[-1], cosine[-1]
    for k in sine[-2::-1]:
        s = s * z + k
    for k in cosine[-2::-1]:
        c = c * z + k
    s = s * y
    return 1.0 - 2.0 * (s * s), 2.0 * (s * c)


def fours(a, b, c, d):
    (ar, ai), (br, bi), (cr, ci), (dr, di) = a, b, c, d
    pr, pi, mr, mi = ar + cr, ai + ci, ar - cr, ai - ci
    qr, qi, nr, ni = br + dr, bi + di, br - dr, bi - di
    return (pr + qr, pi + qi), (mr + ni, mi - nr), (pr - qr, pi - qi), (mr - ni, mi + nr)


def class_of(e, g):
    return (4 * e + 9 * g) % CLASSES


def focus(xr, xi, phases, tables):
    fw, bw = tables
    part = xr.shape[0] // CLASSES
    x = [(xr[k * part : (k + 1) * part], xi[k * part : (k + 1) * part]) for k in range(CLASSES)]
    columns = [thirds(*[x[(4 * i + 3 * j) % CLASSES] for i in range(3)], -1.0) for j in range(4)]
    classes = [None] * CLASSES
    for e in range(3):
        for g, pair in enumerate(fours(*[columns[j][e] for j in range(4)])):
            classes[class_of(e, g)] = pair
    z, forward = [], []
    for f0 in range(CLASSES + 1):
        if f0 < CLASSES:
            forward.append(dot_parts(fw[f0], jnp.concatenate(classes[f0], axis=0)))
        if f0 > 0:
            y, k = forward[f0 - 1], f0 - 1
            dr, di = y[:part], y[part:]
            pc, ps = phases(k)
            e = jnp.concatenate([dr * pc - di * ps, dr * ps + di * pc], axis=0)
            y = dot_parts(bw[k], e)
            z.append((y[:part], y[part:]))
    sums = [fours(*[z[class_of(e, g)] for g in range(4)]) for e in range(3)]
    outs = []
    for h in range(AOI // part):
        terms = [sums[e][h] for e in range(3)]
        outs.append(thirds(*terms, 1.0)[h % 3])
    return [jnp.concatenate([pair[c] for pair in outs], axis=0) for c in range(2)]


def looked_at(field, look):
    lines = AOI // 4 // LOOK_AZ
    groups = [field[k * lines : (k + 1) * lines] for k in range(AOI // lines)]
    added = [groups[k] + groups[k + 1] for k in range(0, len(groups), LOOK_AZ)]
    high, low = split(jnp.concatenate(added, axis=0))
    return dot(high, look) + dot(low, look)


def joint_kernel(order, rounds, me_ref, same_ref, x_ref, early_ref, own_angle, other_angle, fw, bw, look_ref, out, stage, looked):
    acq = me_ref[0]
    tiles = len(order)
    near = tiles // 2
    firsts = [acq * tiles, (1 - acq) * tiles]
    for part in range(2):
        for k, first in enumerate(firsts):
            lanes = slice(k * LANES, (k + 1) * LANES)
            for place, t in enumerate(order):
                stage[part, t, 1:, :, lanes] = x_ref[first + place, 0, :, part * SUB : (part + 1) * SUB, :]
            for s in range(near):
                for side in range(2):
                    tile = jnp.bitwise_xor(me_ref[1], s + side * near)
                    stage[part, tile, 0, :, lanes] = early_ref[k * near + s, side, 0, part * SUB : (part + 1) * SUB, :]
    xr, xi = [stage[part].reshape(-1, 2 * LANES) for part in range(2)]
    rows_of = lambda k: pl.ds(k, own_angle.shape[0] // CLASSES, stride=CLASSES)
    phases = lambda k: cos_sin(jnp.concatenate([a[rows_of(k), :] for a in (own_angle, other_angle)], axis=1))
    fr, fi = focus(xr, xi, phases, [fw, bw])
    mr, mi, pr, pi = fr[:, :LANES], fi[:, :LANES], fr[:, LANES:], fi[:, LANES:]
    look = look_ref[0]
    cross_real = looked_at(mr * pr + mi * pi, look[0])
    cross_imag = looked_at(mi * pr - mr * pi, look[1])
    own_real = looked_at(mr * mr + mi * mi, look[0])
    own_imag = looked_at(mi * mr - mr * mi, look[1])
    other_real = looked_at(pr * pr + pi * pi, look[0])
    other_imag = looked_at(pi * pr - pr * pi, look[1])
    block = pl.program_id(0)

    @pl.when(block == 0)
    def _():
        looked[...] = jnp.zeros_like(looked)

    for r in range(rounds):
        same = same_ref[r] != 0
        looked[0, r] += jnp.where(same, own_real + own_imag, cross_real + cross_imag)
        looked[1, r] += jnp.where(same, other_real + other_imag, cross_real - cross_imag)

    @pl.when(block == pl.num_programs(0) - 1)
    def _():
        for k, first in enumerate(firsts):
            groups = pack(looked[k, 0], looked[k, 1])
            for place, t in enumerate(order):
                for j, (value, at) in enumerate(groups):
                    out[first + place, j] = value[t * SUB + at : t * SUB + at + SUB // 2]


def pack(even, odd):
    half = SUB // 2
    free = lax.broadcasted_iota(jnp.int32, even.shape, 1) >= USED
    rest = [pltpu.roll(odd, (USED - SPARE * j) % LANES, 1) for j in range(3)]
    up = lambda value: pltpu.roll(value, value.shape[0] - half, 0)
    return (
        (jnp.where(free, up(rest[0]), even), 0),
        (jnp.where(free, rest[1], even), half),
        (jnp.where(free, up(rest[2]), odd), 0),
    )


def unpack(parts):
    lane = lax.broadcasted_iota(jnp.int32, parts[0].shape, 1)
    rest = [pltpu.roll(part, (SPARE * j - USED) % LANES, 1) for j, part in enumerate(parts)]
    last = jnp.where(lane < SPARE, rest[0], jnp.where(lane < 2 * SPARE, rest[1], rest[2]))
    return jnp.concatenate([parts[0], parts[1], parts[2], last], axis=0)


def joint_call(me, same, array, early, angle, other_angle, tables, order):
    dests, blocks, steps = array.shape[:3]
    tiles = len(order)
    lines = angle.shape[0]
    rounds = same.shape[0]
    wide = blocks * LANES // LOOK_RG
    look = np.stack(
        [
            np.stack([look_table(LANES, c * wide + b * LANES // LOOK_RG) for c in range(2)])
            for b in range(blocks)
        ]
    )
    return pl.pallas_call(
        functools.partial(joint_kernel, order, rounds),
        grid_spec=pltpu.PrefetchScalarGridSpec(
            num_scalar_prefetch=2,
            grid=(blocks,),
            in_specs=[
                pl.BlockSpec((dests, 1) + array.shape[2:], lambda b, me, same: (0, b, 0, 0, 0)),
                pl.BlockSpec(early.shape[:2] + (1,) + early.shape[3:], lambda b, me, same: (0, 0, b, 0, 0)),
                pl.BlockSpec((lines, LANES), lambda b, me, same: (0, me[0] * blocks + b)),
                pl.BlockSpec((lines, LANES), lambda b, me, same: (0, b)),
                *[pl.BlockSpec(t.shape, lambda b, me, same: (0, 0, 0)) for t in tables],
                pl.BlockSpec((1,) + look.shape[1:], lambda b, me, same: (b, 0, 0, 0)),
            ],
            out_specs=pl.BlockSpec((dests, 3, SUB // 2, LANES), lambda b, me, same: (0, 0, 0, 0)),
            scratch_shapes=[
                pltpu.VMEM((2, tiles, steps + 1, SUB, 2 * LANES), jnp.float32),
                pltpu.VMEM((2, rounds, AOI // LOOK_AZ, LANES), jnp.float32),
            ],
        ),
        out_shape=jax.ShapeDtypeStruct((dests, 3, SUB // 2, LANES), jnp.float32),
        compiler_params=pltpu.CompilerParams(vmem_limit_bytes=VMEM_LIMIT),
        cost_estimate=pl.CostEstimate(
            flops=2 * 2 * 3 * 6 * 256 * 256 * 2 * LANES * blocks,
            bytes_accessed=20 * lines * 2 * LANES * blocks,
            transcendentals=0,
        ),
        name="azimuth_interferogram",
    )(me, same, array, early, angle, other_angle, *[jnp.asarray(t) for t in tables], jnp.asarray(look))


def single_kernel(tiles, x_ref, angle_ref, fw, bw, out):
    xr, xi = [x_ref[:, 0, :, part * SUB : (part + 1) * SUB, :].reshape(-1, LANES) for part in range(2)]
    fr, fi = focus(xr, xi, lambda k: cos_sin(angle_ref[pl.ds(k, angle_ref.shape[0] // CLASSES, stride=CLASSES), :]), [fw, bw])
    out[:AOI] = fr
    out[AOI:] = fi


def single_call(array, angle, tables):
    tiles = array.shape[0]
    lines, columns = angle.shape
    return pl.pallas_call(
        functools.partial(single_kernel, tiles),
        grid=(columns // LANES,),
        in_specs=[
            pl.BlockSpec((tiles, 1) + array.shape[2:], lambda b: (0, b, 0, 0, 0)),
            pl.BlockSpec((lines, LANES), lambda b: (0, b)),
        ]
        + [pl.BlockSpec(t.shape, lambda b: (0, 0, 0)) for t in tables],
        out_specs=pl.BlockSpec((2 * AOI, LANES), lambda b: (0, b)),
        out_shape=jax.ShapeDtypeStruct((2 * AOI, columns), jnp.float32),
        compiler_params=pltpu.CompilerParams(vmem_limit_bytes=VMEM_LIMIT),
        name="azimuth_focus",
    )(array, angle, *[jnp.asarray(t) for t in tables])


def look_table(width, offset):
    table = np.zeros((width, LANES), np.float64)
    table[np.arange(width), offset + np.arange(width) // LOOK_RG] = 1.0 / (LOOK_AZ * LOOK_RG)
    return table.astype(ml_dtypes.bfloat16)


def cross_kernel(rounds, tiles, mine_ref, *refs):
    partner_refs, look_ref, out = refs[:rounds], refs[-2], refs[-1]
    mr, mi = mine_ref[:AOI], mine_ref[AOI:]
    per = AOI // LOOK_AZ // tiles
    for r in range(rounds):
        pr, pi = partner_refs[r][:AOI], partner_refs[r][AOI:]
        for c, field in enumerate((mr * pr + mi * pi, mi * pr - mr * pi)):
            looked = looked_at(field, look_ref[...])
            at = (c * rounds + r) * per
            for t in range(tiles):
                out[t, at : at + per, :] = looked[t * per : (t + 1) * per]


def cross_call(mine, partners, tiles):
    rounds = len(partners)
    width = mine.shape[1]
    look = jnp.asarray(look_table(width, 0))
    shape = (tiles, 2 * rounds * (AOI // LOOK_AZ // tiles), LANES)
    vmem = lambda: pl.BlockSpec(memory_space=pltpu.VMEM)
    return pl.pallas_call(
        functools.partial(cross_kernel, rounds, tiles),
        in_specs=[vmem() for _ in range(rounds + 2)],
        out_specs=vmem(),
        out_shape=jax.ShapeDtypeStruct(shape, jnp.float32),
        compiler_params=pltpu.CompilerParams(vmem_limit_bytes=VMEM_LIMIT),
        name="interferogram",
    )(mine, *partners, look)


def place_kernel(sources, valid, parts, in_ref, out):
    if in_ref.shape[1:] == (3, SUB // 2, LANES):
        values = {k: unpack([in_ref[k, j] for j in range(3)]) for k in sources}
    else:
        values = {k: in_ref[k] for k in sources}
    rows = values[sources[0]].shape[0]
    lane = lax.broadcasted_iota(jnp.int32, (rows, LANES), 1)
    for c in range(parts):
        for o in range(len(sources) * valid // LANES):
            acc = None
            for place, source in enumerate(sources):
                shift = place * valid - o * LANES
                if shift + valid <= 0 or shift >= LANES:
                    continue
                value = values[source]
                turn_by = (shift - c * valid) % LANES
                if turn_by:
                    value = pltpu.roll(value, turn_by, 1)
                acc = value if acc is None else jnp.where(lane >= shift, value, acc)
            out[c * rows : (c + 1) * rows, o * LANES : (o + 1) * LANES] = acc


def place_call(received, rows, sources, valid, parts):
    return pl.pallas_call(
        functools.partial(place_kernel, sources, valid, parts),
        in_specs=[pl.BlockSpec(memory_space=pltpu.VMEM)],
        out_specs=pl.BlockSpec(memory_space=pltpu.VMEM),
        out_shape=jax.ShapeDtypeStruct((parts * rows, len(sources) * valid), jnp.float32),
        compiler_params=pltpu.CompilerParams(vmem_limit_bytes=VMEM_LIMIT),
        name="place_samples",
    )(received)


def turn(array, axes):
    return lax.all_to_all(array, axes, split_axis=0, concat_axis=0, tiled=True)


def joint(tiles, echo, slant, angle, pairs):
    steps = echo.shape[2] // SUB
    columns = angle.shape[1]
    rounds = pairs.shape[0]
    acq = lax.axis_index("acq")
    same = (lax.dynamic_index_in_dim(pairs, acq, 1, keepdims=False) == acq).astype(jnp.int32)
    theirs = lax.dynamic_slice_in_dim(angle, (1 - acq) * (columns // 2), columns // 2, 1)
    other_angle = lax.ppermute(theirs, "acq", [(0, 1), (1, 0)])
    low = lax.axis_size("low")
    order = list(range(tiles))
    axes = ("acq", "high", "low")
    tile = lax.axis_index("high") * low + lax.axis_index("low")
    me = jnp.stack([acq, tile]).astype(jnp.int32)
    kept, given = range_call(echo, slant, 0, 1, order, 2, early=True)
    came = lax.ppermute(given, "high", [(h, h ^ (FAR // 2)) for h in range(FAR)])
    (sent,) = range_call(echo, slant, 1, steps - 1, order, 2)
    array = turn(sent, axes)
    early = list(pair_call(kept, came))
    near = tiles // 2
    for s in sorted(range(1, tiles), key=lambda s: (s % near) // FAR):
        flip = s // near * tiles + s % near
        early[s] = lax.ppermute(early[s], ("acq", "high", "low"), [(i, i ^ flip) for i in range(2 * tiles)])
    early = jnp.stack(early)
    looked = joint_call(me, same, array, early, angle, other_angle, azimuth_tables(angle.shape[0]), order)
    sources = [half * tiles + order.index(t) for t in range(tiles) for half in range(2)]
    result = place_call(turn(looked, axes), rounds * SUB, sources, columns // 2 // LOOK_RG, 2)
    return result.reshape(2, rounds, 1, -1, result.shape[1])


def separate(tiles, echo, slant, angle, pairs):
    columns = angle.shape[1]
    rounds = pairs.shape[0]
    (sent,) = range_call(echo, slant, 0, echo.shape[2] // SUB, list(range(tiles)), 1)
    mine = single_call(turn(sent, ("high", "low")), angle, azimuth_tables(angle.shape[0]))
    every = lax.all_gather(mine, "acq", axis=0)
    partner = lax.dynamic_index_in_dim(pairs, lax.axis_index("acq"), 1, keepdims=False)
    partners = [lax.dynamic_index_in_dim(every, partner[r], 0, keepdims=False) for r in range(rounds)]
    looked = turn(cross_call(mine, partners, tiles), ("high", "low"))
    result = place_call(looked, looked.shape[1], list(range(tiles)), columns // LOOK_RG, 1)
    return result.reshape(2, rounds, 1, -1, result.shape[1])


def shards(tiles, acqs, echo, slant, angle, pairs):
    fits = echo.shape[2] > SUB and tiles == FAR * FAR and AOI // LOOK_AZ == tiles * SUB
    fits = fits and angle.shape[2] // LOOK_RG == USED and pairs.shape[0] == 2
    program = joint if acqs == 2 and fits else separate
    return program(tiles, echo, slant, angle[0], pairs)


def solution(mesh):
    acqs, tiles = mesh.shape["acq"], mesh.shape["tile"]
    low = 1 << (tiles.bit_length() // 2)
    low = low if tiles % low == 0 else 1
    split_mesh = jax.sharding.Mesh(mesh.devices.reshape(acqs, tiles // low, low), ("acq", "high", "low"))
    tile = ("high", "low")
    in_specs = (P(None, "acq", tile, None), P(None, "acq", None), P("acq", None, tile), P())
    out_specs = P(None, None, "acq", tile, None)
    body = functools.partial(shards, tiles, acqs)
    return jax.shard_map(body, mesh=split_mesh, in_specs=in_specs, out_specs=out_specs, check_vma=False)
```
